32 devices in a mesh: img: 8 (over z, y), band: 4 (over x, core).
Axes of the slice: x: 2, y: 2, z: 4, core: 2. Of those that a mesh axis runs over, the one named last changes fastest.
Arguments:
- inputs: bfloat16 [256, 400, 432], P('img', 'band'), may hold values from -6 to 6
- cotangent: bfloat16 [256, 400, 432], P('img', 'band'), may hold values from -6 to 6
- grid_sizes: int32 [256], P('img'), may hold values from 10 to 18, as said below
- w_qkv: float32 [432, 1296], replicated, may hold values from -0.21875 to 0.21875
- w_out: float32 [432, 432], replicated, may hold values from -0.875 to 0.875
- w_fc1: float32 [432, 1728], replicated, may hold values from -0.3125 to 0.3125
- w_fc2: float32 [1728, 432], replicated, may hold values from -0.15625 to 0.15625
- norm_gains: float32 [2, 432], replicated, may hold values from 0.7 to 6.5
- biases: float32 [4, 432], replicated, may hold values from -1.75 to 1.75
- fc1_bias: float32 [1728], replicated, may hold values from -1.75 to 1.75
- head_params: float32 [4, 9], replicated, may hold values from -2 to 2, as said below
- rows_qkv: float32 [432], replicated, may hold values from 8.467612e-08 to 3.3424783e-07
- cols_qkv: float32 [1296], replicated, may hold values from 8.467612e-08 to 3.3424783e-07
- rows_out: float32 [432], replicated, may hold values from 8.484082e-09 to 3.3489798e-08
- cols_out: float32 [432], replicated, may hold values from 8.484082e-09 to 3.3489798e-08
- rows_fc1: float32 [432], replicated, may hold values from 1.8307755e-08 to 7.3677555e-08
- cols_fc1: float32 [1728], replicated, may hold values from 1.8307755e-08 to 7.3677555e-08
- rows_fc2: float32 [1728], replicated, may hold values from 8.467612e-08 to 3.3424783e-07
- cols_fc2: float32 [432], replicated, may hold values from 8.467612e-08 to 3.3424783e-07
- gain_moment: float32 [2, 432], replicated, may hold values from 5.8048983e-08 to 2.3219593e-07
- bias_moment: float32 [4, 432], replicated, may hold values from 3.3424783e-07 to 1.3369913e-06
- fc1_bias_moment: float32 [1728], replicated, may hold values from 1.2502857e-08 to 4.911837e-08
- head_moment: float32 [4, 9], replicated, may hold values from 3.3424783e-07 to 1.3369913e-06
Outputs:
- output: bfloat16 [256, 400, 432], P('img', 'band')
- input_grad: float32 [256, 400, 432], P('img', 'band')
- grad_norm: float32 [1], replicated
- grad_qkv: float32 [432, 1296], replicated
- grad_out: float32 [432, 432], replicated
- grad_fc1: float32 [432, 1728], replicated
- grad_fc2: float32 [1728, 432], replicated
- grad_gains: float32 [2, 432], replicated
- grad_biases: float32 [4, 432], replicated
- grad_fc1_bias: float32 [1728], replicated
- grad_head: float32 [4, 9], replicated
- new_qkv: float32 [432, 1296], replicated
- new_out: float32 [432, 432], replicated
- new_fc1: float32 [432, 1728], replicated
- new_fc2: float32 [1728, 432], replicated
- new_gains: float32 [2, 432], replicated
- new_biases: float32 [4, 432], replicated
- new_fc1_bias: float32 [1728], replicated
- new_head: float32 [4, 9], replicated
- new_rows_qkv: float32 [432], replicated
- new_cols_qkv: float32 [1296], replicated
- new_rows_out: float32 [432], replicated
- new_cols_out: float32 [432], replicated
- new_rows_fc1: float32 [432], replicated
- new_cols_fc1: float32 [1728], replicated
- new_rows_fc2: float32 [1728], replicated
- new_cols_fc2: float32 [432], replicated
- new_gain_moment: float32 [2, 432], replicated
- new_bias_moment: float32 [4, 432], replicated
- new_fc1_bias_moment: float32 [1728], replicated
- new_head_moment: float32 [4, 9], replicated
The draws below stay inside these ranges and needn't reach their ends.
Inputs may be any that keep to these rules, and one draw needn't show every extreme that they name: `grid_sizes`: each value is 10, 14 or 18; every aligned block of 32 images holds a grid of 18 and a grid of 10. `head_params`: row 2 is negative.
All inputs are finite; a program needn't handle non-finite values.
Results may differ from the reference program's by a relative error of at most 0.02.
The reference program's roundings to bfloat16 on the way count: a program that leaves them out, or rounds other values in their place, can miss the bound.
Values may be sent and summed in bfloat16 or wider, within the bound.
A program may use at most 256 MiB of HBM per device.

```python
import math
import jax
import jax.numpy as jnp
from jax import lax

D = 432
HEADS = 9
FF = 1728
GRID = 20
STEP = 10
IMG_DEV = 32
IMAGES = 256


def draw_grid_sizes(key, part):
    key = jax.random.fold_in(key, 5)
    size_key, slot_key = jax.random.split(key)
    groups = IMAGES // IMG_DEV
    drawn_size = jax.random.randint(size_key, (groups, IMG_DEV), 0, 3)
    forced = jax.random.randint(slot_key, (groups, 1), 0, IMG_DEV)
    within = jnp.arange(IMG_DEV, dtype=jnp.int32)[None, :]
    drawn_size = jnp.where(within == forced, 2, drawn_size)
    drawn_size = jnp.where(within == (forced + 1) % IMG_DEV, 0, drawn_size)
    return (10 + 4 * drawn_size).reshape(IMAGES).astype(jnp.int32)


def draw_norm_gains(key, part):
    key = jax.random.fold_in(key, 11)
    position = jnp.arange(D, dtype=jnp.float32) / (D - 1)
    rising = jnp.exp(jnp.log(3.0) * position)
    noise = jax.random.uniform(key, (2, D), jnp.float32, 0.8, 1.2)
    return (rising[None, :] * noise).astype(jnp.float32)


def draw_head_params(key, part):
    key = jax.random.fold_in(key, 17)
    strength_key, offset_key, gate_key = jax.random.split(key, 3)
    strength = jnp.exp(jax.random.uniform(strength_key, (HEADS,), jnp.float32, math.log(0.05), math.log(0.5)))
    offsets = jax.random.uniform(offset_key, (2, HEADS), jnp.float32, -2.0, 2.0)
    gate_param = jax.random.uniform(gate_key, (1, HEADS), jnp.float32, -2.0, 2.0)
    return jnp.concatenate([2.0 * strength[None, :] * offsets, -strength[None, :], gate_param], axis=0).astype(jnp.float32)


def block_levels(own_key, dims, cuts, least, high):
    def one(dim, parts):
        steps = jax.random.uniform(jax.random.fold_in(jax.random.fold_in(own_key, 6), dim), (parts,), jnp.float32, least / len(cuts), high / len(cuts))
        return jnp.repeat(jnp.exp(steps), dims[dim] // parts).reshape((-1,) + (1,) * (len(dims) - dim - 1))

    level = one(*cuts[0])
    for cut in cuts[1:]:
        level = level * one(*cut)
    return level


def gaussian(key, shape, scale, limit, pieces=(), kind=jnp.bfloat16):
    entries = jax.random.normal(key, shape, jnp.float32) * scale
    if len(pieces) > 0:
        entries = block_levels(key, shape, pieces, -0.22, 0.18) * entries
    return jnp.clip(entries, min=-limit, max=limit).astype(kind)


def setup_inputs(seed: int = 0) -> dict:
    key_list = jax.random.split(jax.random.key(seed), 24)
    return {
        "inputs": gaussian(key_list[0], (IMAGES, GRID * GRID, D), 1.0, 6.0, ((0, 8), (1, 4))),
        "cotangent": gaussian(key_list[1], (IMAGES, GRID * GRID, D), 1.0, 6.0, ((0, 8), (1, 4))),
        "grid_sizes": draw_grid_sizes(jax.random.fold_in(key_list[23], 71), 0),
        "w_qkv": gaussian(key_list[3], (D, 3 * D), (2 * D) ** -0.5, 0.21875, (), jnp.float32),
        "w_out": gaussian(key_list[4], (D, D), (D // 8) ** -0.5, 0.875, (), jnp.float32),
        "w_fc1": gaussian(key_list[5], (D, FF), D ** -0.5, 0.3125, (), jnp.float32),
        "w_fc2": gaussian(key_list[6], (FF, D), FF ** -0.5, 0.15625, (), jnp.float32),
        "norm_gains": draw_norm_gains(jax.random.fold_in(key_list[23], 71), 0),
        "biases": gaussian(key_list[8], (4, D), 0.3, 1.75, (), jnp.float32),
        "fc1_bias": gaussian(key_list[9], (FF,), 0.3, 1.75, (), jnp.float32),
        "head_params": draw_head_params(jax.random.fold_in(key_list[23], 71), 0),
        "rows_qkv": jnp.clip(jnp.exp(jax.random.uniform(key_list[11], (D,), jnp.float32, math.log(8.467611678497633e-08), math.log(3.3424782941438025e-07))), 8.467611678497633e-08, 3.3424782941438025e-07),
        "cols_qkv": jnp.clip(jnp.exp(jax.random.uniform(key_list[12], (3 * D,), jnp.float32, math.log(8.467611678497633e-08), math.log(3.3424782941438025e-07))), 8.467611678497633e-08, 3.3424782941438025e-07),
        "rows_out": jnp.clip(jnp.exp(jax.random.uniform(key_list[13], (D,), jnp.float32, math.log(8.484081881476868e-09), math.log(3.3489797601760074e-08))), 8.484081881476868e-09, 3.3489797601760074e-08),
        "cols_out": jnp.clip(jnp.exp(jax.random.uniform(key_list[14], (D,), jnp.float32, math.log(8.484081881476868e-09), math.log(3.3489797601760074e-08))), 8.484081881476868e-09, 3.3489797601760074e-08),
        "rows_fc1": jnp.clip(jnp.exp(jax.random.uniform(key_list[15], (D,), jnp.float32, math.log(1.830775531175277e-08), math.log(7.367755472387216e-08))), 1.830775531175277e-08, 7.367755472387216e-08),
        "cols_fc1": jnp.clip(jnp.exp(jax.random.uniform(key_list[16], (FF,), jnp.float32, math.log(1.830775531175277e-08), math.log(7.367755472387216e-08))), 1.830775531175277e-08, 7.367755472387216e-08),
        "rows_fc2": jnp.clip(jnp.exp(jax.random.uniform(key_list[17], (FF,), jnp.float32, math.log(8.467611678497633e-08), math.log(3.3424782941438025e-07))), 8.467611678497633e-08, 3.3424782941438025e-07),
        "cols_fc2": jnp.clip(jnp.exp(jax.random.uniform(key_list[18], (D,), jnp.float32, math.log(8.467611678497633e-08), math.log(3.3424782941438025e-07))), 8.467611678497633e-08, 3.3424782941438025e-07),
        "gain_moment": jnp.clip(jnp.exp(jax.random.uniform(key_list[19], (2, D), jnp.float32, math.log(5.804898250971746e-08), math.log(2.3219593003886985e-07))), 5.804898250971746e-08, 2.3219593003886985e-07),
        "bias_moment": jnp.clip(jnp.exp(jax.random.uniform(key_list[20], (4, D), jnp.float32, math.log(3.3424782941438025e-07), math.log(1.336991317657521e-06))), 3.3424782941438025e-07, 1.336991317657521e-06),
        "fc1_bias_moment": jnp.clip(jnp.exp(jax.random.uniform(key_list[21], (FF,), jnp.float32, math.log(1.2502857416052393e-08), math.log(4.9118369815914775e-08))), 1.2502857416052393e-08, 4.9118369815914775e-08),
        "head_moment": jnp.clip(jnp.exp(jax.random.uniform(key_list[22], (4, HEADS), jnp.float32, math.log(3.3424782941438025e-07), math.log(1.336991317657521e-06))), 3.3424782941438025e-07, 1.336991317657521e-06),
    }


@jax.custom_vjp
def low(v):
    return lax.optimization_barrier(v.astype(jnp.bfloat16)).astype(jnp.float32)

@jax.custom_vjp
def low_back(v):
    return v

def low_keep(v):
    return (low(v), None)

def low_pass(kept, grad):
    return (grad,)

def back_keep(v):
    return (v, None)

def back_low(kept, grad):
    return (low(grad),)
low.defvjp(low_keep, low_pass)
low_back.defvjp(back_keep, back_low)
PRECISE = lax.Precision.HIGHEST
NORM_FLOOR = 1e-06
FLOOR_ONE = 1e-30
FLOOR_TWO = 0.001
STEP_RATE = 0.6
CLIP_RMS = 1.0
MASKED = -1e+30

def layer_norm(values, gain_row, shift_row):
    averaged = lax.optimization_barrier(jnp.mean(values, axis=-1, keepdims=True))
    centered = values - averaged
    variance = lax.optimization_barrier(jnp.mean(centered * centered, axis=-1, keepdims=True))
    return centered * lax.rsqrt(variance + NORM_FLOOR) * gain_row + shift_row

def attend_image(queries, keys_in, values_in, grid_size, head_params):
    total_slots = queries.shape[0]
    head_count = head_params.shape[1]
    head_size = queries.shape[1] // head_count
    slot_ids = jnp.arange(total_slots, dtype=jnp.int32)
    rows_at = slot_ids // GRID
    cols_at = slot_ids % GRID
    live_slot = (rows_at < grid_size) & (cols_at < grid_size)
    delta_x = (cols_at[None, :] - cols_at[:, None]).astype(jnp.float32)
    delta_y = (rows_at[None, :] - rows_at[:, None]).astype(jnp.float32)
    distance = delta_x * delta_x + delta_y * delta_y
    query_heads = queries.reshape(total_slots, head_count, head_size)
    key_heads = keys_in.reshape(total_slots, head_count, head_size)
    value_heads = values_in.reshape(total_slots, head_count, head_size)
    raw_scores = jnp.einsum('qhd,khd->hqk', query_heads, key_heads, precision=PRECISE) * head_size ** (-0.5)
    scores = jnp.where(live_slot[None, None, :], low_back(raw_scores), MASKED)
    content = jax.nn.softmax(scores, axis=-1)
    positional = head_params[0][:, None, None] * delta_x[None] + head_params[1][:, None, None] * delta_y[None] + head_params[2][:, None, None] * distance[None]
    placed = jax.nn.softmax(jnp.where(live_slot[None, None, :], positional, MASKED), axis=-1)
    gate_open = jax.nn.sigmoid(head_params[3])[:, None, None]
    mixed_probs = low((1.0 - gate_open) * content + gate_open * placed)
    attended = jnp.einsum('hqk,khd->qhd', mixed_probs, value_heads, precision=PRECISE)
    return attended.reshape(total_slots, head_count * head_size)

def forward(values, w_qkv, w_out, w_fc1, w_fc2, norm_gains, biases, fc1_bias, head_params, grid_sizes):
    columns = values.shape[2]
    normed = low(layer_norm(values, norm_gains[0], biases[0]))
    projected = jnp.einsum('nsd,de->nse', normed, low(w_qkv), precision=PRECISE)
    projected = low(low_back(projected))
    queries = projected[:, :, :columns]
    keys_in = projected[:, :, columns:2 * columns]
    values_in = projected[:, :, 2 * columns:]

    def image_attention(member):
        return attend_image(member[0], member[1], member[2], member[3], head_params)
    attended = lax.map(jax.checkpoint(image_attention), (queries, keys_in, values_in, grid_sizes))
    attended = low(low_back(attended))
    branch = low_back(jnp.einsum('nsd,de->nse', attended, low(w_out), precision=PRECISE) + biases[2])
    hidden = values + branch
    normed_two = low(layer_norm(hidden, norm_gains[1], biases[1]))
    before = low_back(jnp.einsum('nsd,df->nsf', normed_two, low(w_fc1), precision=PRECISE) + fc1_bias)
    activated = low(jax.nn.gelu(before))
    result = hidden + jnp.einsum('nsf,fd->nsd', activated, low(w_fc2), precision=PRECISE) + biases[3]
    slot_ids = jnp.arange(values.shape[1], dtype=jnp.int32)
    rows_at = slot_ids // GRID
    cols_at = slot_ids % GRID
    live_slot = (rows_at[None, :] < grid_sizes[:, None]) & (cols_at[None, :] < grid_sizes[:, None])
    return jnp.where(live_slot[:, :, None], result, 0.0)

def matrix_update(grad_in, weight, rows_old, cols_old, decay_rate):
    squares = grad_in * grad_in
    rows_new = decay_rate * rows_old + (1.0 - decay_rate) * (lax.optimization_barrier(jnp.mean(squares, axis=1)) + FLOOR_ONE)
    cols_new = decay_rate * cols_old + (1.0 - decay_rate) * (lax.optimization_barrier(jnp.mean(squares, axis=0)) + FLOOR_ONE)
    update = grad_in * lax.rsqrt(rows_new[:, None] * cols_new[None, :] / jnp.mean(rows_new))
    update = update / jnp.maximum(1.0, jnp.sqrt(jnp.mean(update * update)) / CLIP_RMS)
    weight_new = weight - STEP_RATE * jnp.maximum(FLOOR_TWO, jnp.sqrt(jnp.mean(weight * weight))) * update
    return (weight_new, rows_new, cols_new)

def vector_update(grad_in, weight, moment, decay_rate):
    moment_new = decay_rate * moment + (1.0 - decay_rate) * (grad_in * grad_in + FLOOR_ONE)
    update = grad_in * lax.rsqrt(moment_new)
    update = update / jnp.maximum(1.0, jnp.sqrt(jnp.mean(update * update)) / CLIP_RMS)
    weight_new = weight - STEP_RATE * jnp.maximum(FLOOR_TWO, jnp.sqrt(jnp.mean(weight * weight))) * update
    return (weight_new, moment_new)

def reference(inputs, cotangent, grid_sizes, w_qkv, w_out, w_fc1, w_fc2, norm_gains, biases, fc1_bias, head_params, rows_qkv, cols_qkv, rows_out, cols_out, rows_fc1, cols_fc1, rows_fc2, cols_fc2, gain_moment, bias_moment, fc1_bias_moment, head_moment):

    def apply_block(values, w_one, w_two, w_three, w_four, gains_in, biases_in, fc1_in, head_in):
        return forward(values, w_one, w_two, w_three, w_four, gains_in, biases_in, fc1_in, head_in, grid_sizes)
    result, pullback = jax.vjp(apply_block, inputs.astype(jnp.float32), w_qkv, w_out, w_fc1, w_fc2, norm_gains, biases, fc1_bias, head_params)
    all_grads = pullback(cotangent.astype(jnp.float32))
    input_grad = all_grads[0]
    weight_grads = all_grads[1:]
    square_total = sum((jnp.sum(member * member) for member in weight_grads))
    grad_norm = jnp.sqrt(square_total)
    factor = 1.0 / jnp.maximum(grad_norm, 1.0)
    clipped = [member * factor for member in weight_grads]
    decay_rate = 1.0 - STEP ** (-0.8)
    new_qkv, new_rows_qkv, new_cols_qkv = matrix_update(clipped[0], w_qkv, rows_qkv, cols_qkv, decay_rate)
    new_out, new_rows_out, new_cols_out = matrix_update(clipped[1], w_out, rows_out, cols_out, decay_rate)
    new_fc1, new_rows_fc1, new_cols_fc1 = matrix_update(clipped[2], w_fc1, rows_fc1, cols_fc1, decay_rate)
    new_fc2, new_rows_fc2, new_cols_fc2 = matrix_update(clipped[3], w_fc2, rows_fc2, cols_fc2, decay_rate)
    new_gains, new_gain_moment = vector_update(clipped[4], norm_gains, gain_moment, decay_rate)
    new_biases, new_bias_moment = vector_update(clipped[5], biases, bias_moment, decay_rate)
    new_fc1_bias, new_fc1_bias_moment = vector_update(clipped[6], fc1_bias, fc1_bias_moment, decay_rate)
    new_head, new_head_moment = vector_update(clipped[7], head_params, head_moment, decay_rate)
    return (result.astype(jnp.bfloat16), input_grad, grad_norm.reshape(1), clipped[0], clipped[1], clipped[2], clipped[3], clipped[4], clipped[5], clipped[6], clipped[7], new_qkv, new_out, new_fc1, new_fc2, new_gains, new_biases, new_fc1_bias, new_head, new_rows_qkv, new_cols_qkv, new_rows_out, new_cols_out, new_rows_fc1, new_cols_fc1, new_rows_fc2, new_cols_fc2, new_gain_moment, new_bias_moment, new_fc1_bias_moment, new_head_moment)
```

```python
import functools
import math

import jax
import jax.numpy as jnp
import numpy as np
from jax import lax
from jax.experimental import pallas as pl
from jax.experimental.pallas import tpu as pltpu
from jax.sharding import PartitionSpec as P

GRID = 20
STEP = 10
SIDES = (18, 14, 10)

NORM_FLOOR = 1e-06
FLOOR_ONE = 1e-30
FLOOR_TWO = 0.001
STEP_RATE = 0.6
CLIP_RMS = 1.0
MASKED = -1e30

BF16 = jnp.bfloat16
F32 = jnp.float32
VMEM_LIMIT = 60 * 1024 * 1024
SUB = 16
LANE = 128


def round_up(value, unit):
    return (value + unit - 1) // unit * unit


def side_sizes(side):
    live = side * side
    return live, round_up(live, SUB), round_up(live, LANE)


def dot_nn(left, right):
    return lax.dot_general(left, right, (((1,), (0,)), ((), ())), preferred_element_type=F32)


def dot_nt(left, right):
    return lax.dot_general(left, right, (((1,), (1,)), ((), ())), preferred_element_type=F32)


def select_matrix(side):
    live, rows, _ = side_sizes(side)
    made = np.zeros((rows, GRID * GRID), np.float32)
    for row in range(side):
        for col in range(side):
            made[row * side + col, row * GRID + col] = 1.0
    return made


def place_table(side, head_params, gate_value):
    live, rows, lanes = side_sizes(side)
    key_ids = np.arange(rows)
    query_ids = np.arange(lanes)
    delta_x = (key_ids % side)[:, None] - (query_ids % side)[None, :]
    delta_y = (key_ids // side)[:, None] - (query_ids // side)[None, :]
    distance = (delta_x * delta_x + delta_y * delta_y).astype(np.float32)
    inside = (key_ids < live)[:, None] & (query_ids < live)[None, :]
    scores = (
        head_params[0][:, None, None] * delta_x.astype(np.float32)[None]
        + head_params[1][:, None, None] * delta_y.astype(np.float32)[None]
        + head_params[2][:, None, None] * distance[None]
    )
    scores = jnp.where((key_ids < live)[None, :, None], scores, MASKED)
    table = jax.nn.softmax(scores, axis=1) * gate_value[:, None, None]
    return jnp.where(inside[None], table, 0.0)


def fold_rows(values):
    rows, columns = values.shape
    return jnp.sum(values.reshape(rows // 8, 8, columns), axis=0)


def image_kernel(
    columns,
    heads,
    hidden_units,
    unroll_heads,
    sizes_ref,
    gate_ref,
    x_ref,
    ct_ref,
    sel_refs,
    selt_refs,
    place_refs,
    wqkv_ref,
    wout_ref,
    w1_ref,
    w2_ref,
    gains_ref,
    biases_ref,
    fc1b_ref,
    out_ref,
    ig_ref,
    gqkv_ref,
    gout_ref,
    g1_ref,
    g2t_ref,
    vec_ref,
    fc1g_ref,
    headq_ref,
    proj_s,
    projt_s,
    da_s,
    dat_s,
    cont_s,
    mix_s,
    attt_s,
    gt_s,
    act_s,
    gb_s,
    vec_s,
    fc1g_s,
    racc_s,
    gsum_refs,
):
    step = pl.program_id(0)
    steps = pl.num_programs(0)
    head_size = columns // heads
    width = wqkv_ref.shape[1] // 3
    window = 256
    score_scale = head_size ** (-0.5)
    chunk = 256
    chunks = w1_ref.shape[1] // chunk

    @pl.when(step == 0)
    def _():
        gqkv_ref[...] = jnp.zeros_like(gqkv_ref)
        gout_ref[...] = jnp.zeros_like(gout_ref)
        g1_ref[...] = jnp.zeros_like(g1_ref)
        g2t_ref[...] = jnp.zeros_like(g2t_ref)
        vec_s[...] = jnp.zeros_like(vec_s)
        fc1g_s[...] = jnp.zeros_like(fc1g_s)
        racc_s[...] = jnp.zeros_like(racc_s)
        for ref in gsum_refs:
            ref[...] = jnp.zeros_like(ref)

    def head_place(head):
        first_lane = head * head_size
        start = jnp.minimum((first_lane // LANE) * LANE, width - window)
        start = pl.multiple_of(start, LANE)
        lanes = lax.broadcasted_iota(jnp.int32, (1, window), 1) + start
        mask = (lanes >= first_lane) & (lanes < first_lane + head_size)
        return start, mask, pl.multiple_of(first_lane, SUB)

    def loop_heads(body):
        def group(index, carry):
            for inner in range(unroll_heads):
                body(index * unroll_heads + inner)
            return carry

        lax.fori_loop(0, heads // unroll_heads, group, 0)

    def image(side, sel_ref, selt_ref, place_ref, gsum_ref):
        live, rows, lanes = side_sizes(side)
        edge = live // 8 * 8

        def norm(values):
            averaged = jnp.mean(values, axis=-1, keepdims=True)
            centered = values - averaged
            variance = jnp.mean(centered * centered, axis=-1, keepdims=True)
            inverse = lax.rsqrt(variance + NORM_FLOOR)
            return centered * inverse, inverse

        def norm_back(grad, unit, inverse, gain):
            scaled = grad * gain
            first_mean = jnp.mean(scaled, axis=-1, keepdims=True)
            second_mean = jnp.mean(scaled * unit, axis=-1, keepdims=True)
            return inverse * (scaled - first_mean - unit * second_mean)

        x = dot_nn(sel_ref[...], x_ref[0])
        unit_one, inverse_one = norm(x)
        first_b = (unit_one * gains_ref[0:1, :] + biases_ref[0:1, :]).astype(BF16)
        proj_s[:rows, :] = dot_nn(first_b, wqkv_ref[...]).astype(BF16)
        if lanes > rows:
            proj_s[rows:lanes, :] = jnp.zeros((lanes - rows, 3 * width), BF16)
        for part in range(3):
            piece = proj_s[:lanes, part * width : (part + 1) * width]
            projt_s[part, :, :lanes] = piece.T

        def forward_head(head):
            start, mask, row = head_place(head)
            query = jnp.where(mask, proj_s[:lanes, pl.ds(start, window)], 0)
            key = proj_s[:rows, pl.ds(width + start, window)]
            score = dot_nt(key, query) * (score_scale * math.log2(math.e))
            tail = lax.broadcasted_iota(jnp.int32, (rows - edge, lanes), 0) < live - edge
            score = jnp.concatenate(
                [score[:edge], jnp.where(tail, score[edge:], MASKED)], axis=0
            )
            top = jnp.max(score, axis=0, keepdims=True)
            raised = jnp.exp2(score - top)
            total = jnp.sum(raised, axis=0, keepdims=True)
            content = raised * (gate_ref[head] / total)
            cont_s[head, :rows, :lanes] = content
            mixed = (content + place_ref[head]).astype(BF16)
            mix_s[head, :rows, :lanes] = mixed
            value_t = projt_s[2, pl.ds(row, head_size), :rows]
            attt_s[pl.ds(row, head_size), :lanes] = dot_nn(value_t, mixed).astype(BF16)

        loop_heads(forward_head)

        attended = attt_s[:, :lanes].T[:rows]
        hidden = x + (dot_nn(attended, wout_ref[:columns, :]) + biases_ref[2:3, :])
        unit_two, inverse_two = norm(hidden)
        second_b = (unit_two * gains_ref[1:2, :] + biases_ref[1:2, :]).astype(BF16)
        ct_b = dot_nn(sel_ref[...], ct_ref[0]).astype(BF16)

        for index in range(chunks):
            at = slice(index * chunk, (index + 1) * chunk)
            before = dot_nn(second_b, w1_ref[:, at]) + fc1b_ref[:, at]
            grad_act = dot_nt(ct_b, w2_ref[at, :])
            square = before * before
            inner = before * (
                math.sqrt(2.0 / math.pi) + (math.sqrt(2.0 / math.pi) * 0.044715) * square
            )
            half = 0.5 * jnp.tanh(inner) + 0.5
            activated = before * half
            slope = half + activated * (1.0 - half) * (
                2.0 * math.sqrt(2.0 / math.pi)
                + (6.0 * math.sqrt(2.0 / math.pi) * 0.044715) * square
            )
            act_s[:rows, at] = activated.astype(BF16)
            grad_b = (grad_act * slope).astype(BF16)
            gb_s[:rows, at] = grad_b
            fc1g_s[:, at] += fold_rows(grad_b.astype(F32))

        result = (
            hidden + dot_nn(act_s[:rows, :], w2_ref[...]) + biases_ref[3:4, :]
        )
        out_ref[0] = dot_nn(selt_ref[...], result.astype(BF16)).astype(BF16)

        ct_t = ct_b.T
        second_t = second_b.T
        units = g1_ref.shape[1]
        for index in range(chunks):
            low, high = index * chunk, min((index + 1) * chunk, units)
            g1_ref[:, low:high] += dot_nn(second_t, gb_s[:rows, low:high])
            g2t_ref[:, low:high] += dot_nn(ct_t, act_s[:rows, low:high])

        ct_f = ct_b.astype(F32)
        grad_second = dot_nt(gb_s[:rows, :], w1_ref[...])
        grad_hidden = ct_f + norm_back(grad_second, unit_two, inverse_two, gains_ref[1:2, :])
        branch_b = grad_hidden.astype(BF16)
        vec_s[1] += fold_rows(grad_second * unit_two)
        vec_s[3] += fold_rows(grad_second)
        vec_s[4] += fold_rows(branch_b.astype(F32))
        vec_s[5] += fold_rows(ct_f)
        gout_ref[...] += dot_nn(attt_s[:, :rows], branch_b)
        da_s[:rows, :] = dot_nt(branch_b, wout_ref[...]).astype(BF16)
        if lanes > rows:
            da_s[rows:lanes, :] = jnp.zeros((lanes - rows, width), BF16)
        dat_s[:, :lanes] = da_s[:lanes, :].T

        def backward_head(head):
            start, mask, row = head_place(head)
            grad_att = jnp.where(mask, da_s[:lanes, pl.ds(start, window)], 0)
            value = proj_s[:rows, pl.ds(2 * width + start, window)]
            grad_mixed = dot_nt(value, grad_att)
            gsum_ref[head] += grad_mixed
            content = cont_s[head, :rows, :lanes]
            product = grad_mixed * content
            total = jnp.sum(product, axis=0, keepdims=True) / gate_ref[head]
            racc_s[head, :, :lanes] += total
            grad_content = (product - content * total).astype(BF16)
            mixed = mix_s[head, :rows, :lanes]
            at = pl.ds(row, head_size)
            gt_s[2, at, :rows] = dot_nt(dat_s[at, :lanes], mixed).astype(BF16)
            gt_s[1, at, :rows] = (
                dot_nt(projt_s[0, at, :lanes], grad_content) * score_scale
            ).astype(BF16)
            gt_s[0, at, :lanes] = (
                dot_nn(projt_s[1, at, :rows], grad_content) * score_scale
            ).astype(BF16)

        loop_heads(backward_head)

        first_t = first_b.T
        grad_first = jnp.zeros((rows, columns), F32)
        for part in range(3):
            piece = gt_s[part, :, :lanes].T[:rows]
            gqkv_ref[part] += dot_nn(first_t, piece)
            grad_first += dot_nt(piece, wqkv_ref[:, part * width : part * width + columns])
        vec_s[0] += fold_rows(grad_first * unit_one)
        vec_s[2] += fold_rows(grad_first)
        input_grad = grad_hidden + norm_back(grad_first, unit_one, inverse_one, gains_ref[0:1, :])
        ig_ref[0] = dot_nn(selt_ref[...], input_grad.astype(BF16)).astype(BF16)

    for index, side in enumerate(SIDES):

        @pl.when(sizes_ref[step] == side)
        def _(index=index, side=side):
            image(side, sel_refs[index], selt_refs[index], place_refs[index], gsum_refs[index])

    @pl.when(step == steps - 1)
    def _():
        for row in range(6):
            vec_ref[row : row + 1, :] = jnp.sum(vec_s[row], axis=0, keepdims=True)
        fc1g_ref[...] = jnp.sum(fc1g_s[...], axis=0, keepdims=True)[:, : fc1g_ref.shape[1]]

        def head_sums(head, carry):
            pieces = [jnp.zeros((1, headq_ref.shape[2]), F32) for _ in range(4)]
            gate_open = 1.0 - gate_ref[head]
            for index, side in enumerate(SIDES):
                live, rows, lanes = side_sizes(side)
                middle = 0.5 * (side - 1)
                place = place_refs[index][head]
                weighted = gsum_refs[index][head] * place
                key_ids = lax.broadcasted_iota(jnp.int32, (rows, 1), 0)
                query_ids = lax.broadcasted_iota(jnp.int32, (1, lanes), 1)
                key_x = (key_ids % side).astype(F32) - middle
                key_y = (key_ids // side).astype(F32) - middle
                query_x = (query_ids % side).astype(F32) - middle
                query_y = (query_ids // side).astype(F32) - middle

                def moment(values, factor):
                    return jnp.sum(values * factor, axis=0, keepdims=True)

                base = jnp.sum(weighted, axis=0, keepdims=True)
                scaled = base / gate_open
                radius = key_x * key_x + key_y * key_y
                part_x = moment(weighted, key_x) - moment(place, key_x) * scaled
                part_y = moment(weighted, key_y) - moment(place, key_y) * scaled
                part_r = moment(weighted, radius) - moment(place, radius) * scaled
                part_r = part_r - 2.0 * (query_x * part_x + query_y * part_y)
                full = [part_x, part_y, part_r, gate_ref[head] * base]
                for row in range(4):
                    if lanes < headq_ref.shape[2]:
                        full[row] = jnp.concatenate(
                            [full[row], jnp.zeros((1, headq_ref.shape[2] - lanes), F32)], axis=1
                        )
                    pieces[row] = pieces[row] + full[row]
            pieces[3] = pieces[3] - gate_open * gate_ref[head] * racc_s[head]
            for row in range(4):
                headq_ref[head, row : row + 1, :] = pieces[row]
            return carry

        lax.fori_loop(0, heads, head_sums, 0)


def run_images(x, ct, sizes, wqkv, wout, w1, w2, gains, biases, fc1b, head_params, unroll_heads=3):
    images, slots, columns = x.shape
    heads = head_params.shape[1]
    width = wqkv.shape[1] // 3
    units = w2.shape[0]
    padded = w1.shape[1]
    hidden_units = fc1b.shape[1]
    gate_value = jax.nn.sigmoid(head_params[3])
    sels = [jnp.asarray(select_matrix(side), BF16) for side in SIDES]
    selts = [jnp.asarray(select_matrix(side).T, BF16) for side in SIDES]
    places = [place_table(side, head_params, gate_value) for side in SIDES]
    sizes_all = [side_sizes(side) for side in SIDES]
    most_rows = max(size[1] for size in sizes_all)
    most_lanes = max(size[2] for size in sizes_all)

    def whole(array):
        rank = len(array.shape)
        return pl.BlockSpec(
            array.shape, lambda i, *_: (0,) * rank, pipeline_mode=pl.Buffered(1)
        )

    def image_spec():
        return pl.BlockSpec((1, slots, columns), lambda i, *_: (i, 0, 0))

    real_units = 4 * columns
    out_shapes = [
        jax.ShapeDtypeStruct((images, slots, columns), BF16),
        jax.ShapeDtypeStruct((images, slots, columns), BF16),
        jax.ShapeDtypeStruct((3, columns, columns), F32),
        jax.ShapeDtypeStruct((columns, columns), F32),
        jax.ShapeDtypeStruct((columns, real_units), F32),
        jax.ShapeDtypeStruct((columns, real_units), F32),
        jax.ShapeDtypeStruct((6, columns), F32),
        jax.ShapeDtypeStruct((1, real_units), F32),
        jax.ShapeDtypeStruct((heads, 4, most_lanes), F32),
    ]
    scratch = [
        pltpu.VMEM((most_lanes, 3 * width), BF16),
        pltpu.VMEM((3, width, most_lanes), BF16),
        pltpu.VMEM((most_lanes, width), BF16),
        pltpu.VMEM((width, most_lanes), BF16),
        pltpu.VMEM((heads, most_rows, most_lanes), F32),
        pltpu.VMEM((heads, most_rows, most_lanes), BF16),
        pltpu.VMEM((columns, most_lanes), BF16),
        pltpu.VMEM((3, columns, most_lanes), BF16),
        pltpu.VMEM((most_rows, padded), BF16),
        pltpu.VMEM((most_rows, padded), BF16),
        pltpu.VMEM((6, 8, columns), F32),
        pltpu.VMEM((8, padded), F32),
        pltpu.VMEM((heads, 1, most_lanes), F32),
        [pltpu.VMEM((heads, size[1], size[2]), F32) for size in sizes_all],
    ]
    smalls = [sels, selts, places, wqkv, wout, w1, w2, gains, biases, fc1b]
    specs = jax.tree.map(whole, smalls)
    body = functools.partial(image_kernel, columns, heads, real_units, unroll_heads)
    return pl.pallas_call(
        body,
        grid_spec=pltpu.PrefetchScalarGridSpec(
            num_scalar_prefetch=2,
            grid=(images,),
            in_specs=[image_spec(), image_spec()] + specs,
            out_specs=[image_spec(), image_spec()] + [whole(s) for s in out_shapes[2:]],
            scratch_shapes=scratch,
        ),
        out_shape=out_shapes,
        compiler_params=pltpu.CompilerParams(vmem_limit_bytes=VMEM_LIMIT),
        cost_estimate=pl.CostEstimate(flops=40_000_000_000, bytes_accessed=40_000_000, transcendentals=0),
    )(sizes, 1.0 - gate_value, x, ct, *smalls)


def pad_weights(w_qkv, w_out, w_fc1, w_fc2, fc1_bias):
    columns = w_qkv.shape[0]
    width = round_up(columns, LANE)
    units = round_up(w_fc1.shape[1], 256)
    extra = units - w_fc1.shape[1]
    wqkv = jnp.pad(
        w_qkv.astype(BF16).reshape(columns, 3, columns), ((0, 0), (0, 0), (0, width - columns))
    ).reshape(columns, 3 * width)
    wout = jnp.pad(w_out.astype(BF16), ((0, width - columns), (0, 0)))
    w1 = jnp.pad(w_fc1.astype(BF16), ((0, 0), (0, extra)))
    w2 = jnp.pad(w_fc2.astype(BF16), ((0, extra), (0, 0)))
    fc1b = jnp.pad(fc1_bias[None, :], ((0, 0), (0, extra)))
    return wqkv, wout, w1, w2, fc1b


def apply_update(update, weight, update_mean):
    update = update / jnp.maximum(1.0, jnp.sqrt(update_mean) / CLIP_RMS)
    return weight - STEP_RATE * jnp.maximum(FLOOR_TWO, jnp.sqrt(jnp.mean(weight * weight))) * update


def matrix_update(grad_in, weight, rows_old, cols_old, decay_rate):
    squares = grad_in * grad_in
    rows_new = decay_rate * rows_old + (1.0 - decay_rate) * (jnp.mean(squares, axis=1) + FLOOR_ONE)
    cols_new = decay_rate * cols_old + (1.0 - decay_rate) * (jnp.mean(squares, axis=0) + FLOOR_ONE)
    update = grad_in * lax.rsqrt(rows_new[:, None] * cols_new[None, :] / jnp.mean(rows_new))
    return (apply_update(update, weight, jnp.mean(update * update)), rows_new, cols_new)


def vector_update(grad_in, weight, moment, decay_rate):
    moment_new = decay_rate * moment + (1.0 - decay_rate) * (grad_in * grad_in + FLOOR_ONE)
    update = grad_in * lax.rsqrt(moment_new)
    return (apply_update(update, weight, jnp.mean(update * update)), moment_new)


def deal_images(grid_sizes, devices):
    count = grid_sizes.shape[0]
    ids = jnp.arange(count, dtype=jnp.int32)
    ahead = (grid_sizes[None, :] > grid_sizes[:, None]) | (
        (grid_sizes[None, :] == grid_sizes[:, None]) & (ids[None, :] < ids[:, None])
    )
    rank = jnp.sum(ahead.astype(jnp.int32), axis=1)
    turn = rank // devices
    seat = rank % devices
    seat = jnp.where(turn % 2 == 0, seat, devices - 1 - seat)
    place = seat * (count // devices) + turn
    order = jnp.sum(jnp.where(place[None, :] == ids[:, None], ids[None, :], 0), axis=1)
    return order, place


def per_device(
    inputs,
    cotangent,
    grid_sizes,
    w_qkv,
    w_out,
    w_fc1,
    w_fc2,
    norm_gains,
    biases,
    fc1_bias,
    head_params,
    rows_qkv,
    cols_qkv,
    rows_out,
    cols_out,
    rows_fc1,
    cols_fc1,
    rows_fc2,
    cols_fc2,
    gain_moment,
    bias_moment,
    fc1_bias_moment,
    head_moment,
):
    band_count = lax.axis_size("band")
    band_index = lax.axis_index("band")
    columns = inputs.shape[2]
    per_band = inputs.shape[0] // band_count
    order, place = deal_images(grid_sizes, band_count)
    sizes_used = lax.dynamic_slice_in_dim(grid_sizes[order], band_index * per_band, per_band)
    inputs_used = lax.all_to_all(inputs[order], "band", split_axis=0, concat_axis=1, tiled=True)
    cotangent_used = lax.all_to_all(
        cotangent[order], "band", split_axis=0, concat_axis=1, tiled=True
    )
    wqkv, wout, w1, w2, fc1b = pad_weights(w_qkv, w_out, w_fc1, w_fc2, fc1_bias)
    output, input_grad, gqkv, gout, g1, g2t, vec, fc1g, headq = run_images(
        inputs_used, cotangent_used, sizes_used, wqkv, wout, w1, w2, norm_gains, biases, fc1b,
        head_params,
    )
    output_back = lax.all_to_all(output, "band", split_axis=1, concat_axis=0, tiled=True)
    input_back = lax.all_to_all(input_grad, "band", split_axis=1, concat_axis=0, tiled=True)
    output = output_back[place]
    input_grad = input_back[place].astype(F32)
    head_part = jnp.sum(headq, axis=2).T
    decay_rate = 1.0 - STEP ** (-0.8)
    weights = (w_qkv, w_out, w_fc1, w_fc2)
    row_moments = (rows_qkv, rows_out, rows_fc1, rows_fc2)
    col_moments = (cols_qkv, cols_out, cols_fc1, cols_fc2)
    summed = lax.psum((gqkv, gout, g1, g2t, vec, fc1g[0], head_part), ("img", "band"))
    summed = (
        jnp.transpose(summed[0], (1, 0, 2)).reshape(columns, 3 * columns),
        summed[1],
        summed[2],
        summed[3].T,
        summed[4][:2],
        summed[4][2:],
        summed[5],
        summed[6],
    )
    square_total = sum((jnp.sum(member * member) for member in summed))
    factor = 1.0 / jnp.maximum(jnp.sqrt(square_total), 1.0)
    clipped = [member * factor for member in summed]
    updated = [
        matrix_update(clipped[i], weights[i], row_moments[i], col_moments[i], decay_rate)
        for i in range(4)
    ]
    olds = (norm_gains, biases, fc1_bias, head_params)
    moments = (gain_moment, bias_moment, fc1_bias_moment, head_moment)
    vectors = [vector_update(clipped[4 + i], olds[i], moments[i], decay_rate) for i in range(4)]
    return (
        output,
        input_grad,
        jnp.sqrt(square_total).reshape(1),
        *clipped,
        *[member[0] for member in updated],
        *[member[0] for member in vectors],
        *[part for member in updated for part in member[1:]],
        *[member[1] for member in vectors],
    )


def solution(mesh):
    split = P("img", "band", None)
    return jax.shard_map(
        per_device,
        mesh=mesh,
        in_specs=(split, split, P("img")) + (P(),) * 20,
        out_specs=(split, split) + (P(),) * 29,
        check_vma=False,
    )
```

```python
import functools
import math

import jax
import jax.numpy as jnp
import numpy as np
from jax import lax
from jax.experimental import pallas as pl
from jax.experimental.pallas import tpu as pltpu
from jax.sharding import PartitionSpec as P

GRID = 20
STEP = 10
SIDES = (18, 14, 10)

NORM_FLOOR = 1e-06
FLOOR_ONE = 1e-30
FLOOR_TWO = 0.001
STEP_RATE = 0.6
CLIP_RMS = 1.0
MASKED = -1e30

BF16 = jnp.bfloat16
F32 = jnp.float32
VMEM_LIMIT = 60 * 1024 * 1024
SUB = 16
SMALL_ROWS = 16
WAVES = 2
LANE = 128


def round_up(value, unit):
    return (value + unit - 1) // unit * unit


def side_sizes(side):
    live = side * side
    return live, round_up(live, SUB), round_up(live, LANE)


def dot_nn(left, right):
    return lax.dot_general(left, right, (((1,), (0,)), ((), ())), preferred_element_type=F32)


def dot_nt(left, right):
    return lax.dot_general(left, right, (((1,), (1,)), ((), ())), preferred_element_type=F32)


def select_matrix(side):
    live, rows, _ = side_sizes(side)
    made = np.zeros((rows, GRID * GRID), np.float32)
    for row in range(side):
        for col in range(side):
            made[row * side + col, row * GRID + col] = 1.0
    return made


def place_table(side, head_params, gate_value):
    live, rows, lanes = side_sizes(side)
    key_ids = np.arange(rows)
    query_ids = np.arange(lanes)
    delta_x = (key_ids % side)[:, None] - (query_ids % side)[None, :]
    delta_y = (key_ids // side)[:, None] - (query_ids // side)[None, :]
    distance = (delta_x * delta_x + delta_y * delta_y).astype(np.float32)
    inside = (key_ids < live)[:, None] & (query_ids < live)[None, :]
    scores = (
        head_params[0][:, None, None] * delta_x.astype(np.float32)[None]
        + head_params[1][:, None, None] * delta_y.astype(np.float32)[None]
        + head_params[2][:, None, None] * distance[None]
    )
    scores = jnp.where((key_ids < live)[None, :, None], scores, MASKED)
    table = jax.nn.softmax(scores, axis=1) * gate_value[:, None, None]
    return jnp.where(inside[None], table, 0.0)


def fold_rows(values):
    rows, columns = values.shape
    return jnp.sum(values.reshape(rows // 8, 8, columns), axis=0)


def image_kernel(
    columns,
    heads,
    hidden_units,
    unroll_heads,
    sizes_ref,
    gate_ref,
    x_ref,
    ct_ref,
    sel_refs,
    selt_refs,
    place_refs,
    wqkv_ref,
    wback_ref,
    wout_ref,
    w1_ref,
    w2_ref,
    gains_ref,
    biases_ref,
    fc1b_ref,
    out_ref,
    ig_ref,
    tiles_ref,
    small_ref,
    proj_s,
    projt_s,
    da_s,
    dat_s,
    cont_s,
    mix_s,
    attt_s,
    gt_s,
    act_s,
    gb_s,
    vec_s,
    fc1g_s,
    racc_s,
    gqkv_ref,
    gout_ref,
    g1_ref,
    g2t_ref,
    gsum_refs,
):
    step = pl.program_id(0)
    steps = pl.num_programs(0)
    head_size = columns // heads
    width = wqkv_ref.shape[1] // 3
    window = 256
    score_scale = head_size ** (-0.5)
    chunk = 256
    chunks = w1_ref.shape[1] // chunk

    @pl.when(step == 0)
    def _():
        gqkv_ref[...] = jnp.zeros_like(gqkv_ref)
        gout_ref[...] = jnp.zeros_like(gout_ref)
        g1_ref[...] = jnp.zeros_like(g1_ref)
        g2t_ref[...] = jnp.zeros_like(g2t_ref)
        vec_s[...] = jnp.zeros_like(vec_s)
        fc1g_s[...] = jnp.zeros_like(fc1g_s)
        racc_s[...] = jnp.zeros_like(racc_s)
        for ref in gsum_refs:
            ref[...] = jnp.zeros_like(ref)

    def head_place(head):
        first_lane = head * head_size
        start = jnp.minimum((first_lane // LANE) * LANE, width - window)
        start = pl.multiple_of(start, LANE)
        lanes = lax.broadcasted_iota(jnp.int32, (1, window), 1) + start
        mask = (lanes >= first_lane) & (lanes < first_lane + head_size)
        return start, mask, pl.multiple_of(first_lane, SUB)

    def loop_heads(body):
        def group(index, carry):
            for inner in range(unroll_heads):
                body(index * unroll_heads + inner)
            return carry

        lax.fori_loop(0, heads // unroll_heads, group, 0)

    def image(side, sel_ref, selt_ref, place_ref, gsum_ref):
        live, rows, lanes = side_sizes(side)
        edge = live // 8 * 8

        def norm(values):
            averaged = jnp.mean(values, axis=-1, keepdims=True)
            centered = values - averaged
            variance = jnp.mean(centered * centered, axis=-1, keepdims=True)
            inverse = lax.rsqrt(variance + NORM_FLOOR)
            return centered * inverse, inverse

        def norm_back(grad, unit, inverse, gain):
            scaled = grad * gain
            first_mean = jnp.mean(scaled, axis=-1, keepdims=True)
            second_mean = jnp.mean(scaled * unit, axis=-1, keepdims=True)
            return inverse * (scaled - first_mean - unit * second_mean)

        x = dot_nn(sel_ref[...], x_ref[0])
        unit_one, inverse_one = norm(x)
        first_b = (unit_one * gains_ref[0:1, :] + biases_ref[0:1, :]).astype(BF16)
        proj_s[:rows, :] = dot_nn(first_b, wqkv_ref[...]).astype(BF16)
        if lanes > rows:
            proj_s[rows:lanes, :] = jnp.zeros((lanes - rows, 3 * width), BF16)
        for part in range(3):
            piece = proj_s[:lanes, part * width : (part + 1) * width]
            projt_s[part, :, :lanes] = piece.T

        def forward_head(head):
            start, mask, row = head_place(head)
            query = jnp.where(mask, proj_s[:lanes, pl.ds(start, window)], 0)
            key = proj_s[:rows, pl.ds(width + start, window)]
            score = dot_nt(key, query) * (score_scale * math.log2(math.e))
            tail = lax.broadcasted_iota(jnp.int32, (rows - edge, lanes), 0) < live - edge
            score = jnp.concatenate(
                [score[:edge], jnp.where(tail, score[edge:], MASKED)], axis=0
            )
            top = jnp.max(score, axis=0, keepdims=True)
            raised = jnp.exp2(score - top)
            total = jnp.sum(raised, axis=0, keepdims=True)
            content = raised * (gate_ref[head] / total)
            cont_s[head, :rows, :lanes] = content
            mixed = (content + place_ref[head]).astype(BF16)
            mix_s[head, :rows, :lanes] = mixed
            value_t = projt_s[2, pl.ds(row, head_size), :rows]
            attt_s[pl.ds(row, head_size), :lanes] = dot_nn(value_t, mixed).astype(BF16)

        loop_heads(forward_head)

        attended = attt_s[:, :lanes].T[:rows]
        hidden = x + (dot_nn(attended, wout_ref[:columns, :]) + biases_ref[2:3, :])
        unit_two, inverse_two = norm(hidden)
        second_b = (unit_two * gains_ref[1:2, :] + biases_ref[1:2, :]).astype(BF16)
        ct_b = dot_nn(sel_ref[...], ct_ref[0]).astype(BF16)

        for index in range(chunks):
            at = slice(index * chunk, (index + 1) * chunk)
            before = dot_nn(second_b, w1_ref[:, at]) + fc1b_ref[:, at]
            grad_act = dot_nt(ct_b, w2_ref[at, :])
            square = before * before
            inner = before * (
                math.sqrt(2.0 / math.pi) + (math.sqrt(2.0 / math.pi) * 0.044715) * square
            )
            half = 0.5 * jnp.tanh(inner) + 0.5
            activated = before * half
            slope = half + activated * (1.0 - half) * (
                2.0 * math.sqrt(2.0 / math.pi)
                + (6.0 * math.sqrt(2.0 / math.pi) * 0.044715) * square
            )
            act_s[:rows, at] = activated.astype(BF16)
            grad_b = (grad_act * slope).astype(BF16)
            gb_s[:rows, at] = grad_b
            fc1g_s[:, at] += fold_rows(grad_b.astype(F32))

        result = (
            hidden + dot_nn(act_s[:rows, :], w2_ref[...]) + biases_ref[3:4, :]
        )
        out_ref[0] = dot_nn(selt_ref[...], result.astype(BF16)).astype(BF16)

        ct_t = ct_b.T
        second_t = second_b.T
        units = hidden_units
        for index in range(chunks):
            low, high = index * chunk, min((index + 1) * chunk, units)
            g1_ref[:, low:high] += dot_nn(second_t, gb_s[:rows, low:high])
            g2t_ref[:, low:high] += dot_nn(ct_t, act_s[:rows, low:high])

        ct_f = ct_b.astype(F32)
        grad_second = dot_nt(gb_s[:rows, :], w1_ref[...])
        grad_hidden = ct_f + norm_back(grad_second, unit_two, inverse_two, gains_ref[1:2, :])
        branch_b = grad_hidden.astype(BF16)
        vec_s[1] += fold_rows(grad_second * unit_two)
        vec_s[3] += fold_rows(grad_second)
        vec_s[4] += fold_rows(branch_b.astype(F32))
        vec_s[5] += fold_rows(ct_f)
        gout_ref[:, :columns] += dot_nn(attt_s[:, :rows], branch_b)
        da_s[:rows, :] = dot_nt(branch_b, wout_ref[...]).astype(BF16)
        if lanes > rows:
            da_s[rows:lanes, :] = jnp.zeros((lanes - rows, width), BF16)
        dat_s[:, :lanes] = da_s[:lanes, :].T

        def backward_head(head):
            start, mask, row = head_place(head)
            grad_att = jnp.where(mask, da_s[:lanes, pl.ds(start, window)], 0)
            value = proj_s[:rows, pl.ds(2 * width + start, window)]
            grad_mixed = dot_nt(value, grad_att)
            gsum_ref[head] += grad_mixed
            content = cont_s[head, :rows, :lanes]
            product = grad_mixed * content
            total = jnp.sum(product, axis=0, keepdims=True) / gate_ref[head]
            racc_s[head, :, :lanes] += total
            grad_content = (product - content * total).astype(BF16)
            mixed = mix_s[head, :rows, :lanes]
            at = pl.ds(row, head_size)
            gt_s[pl.ds(pl.multiple_of(2 * columns + row, SUB), head_size), :rows] = dot_nt(
                dat_s[at, :lanes], mixed
            ).astype(BF16)
            gt_s[pl.ds(pl.multiple_of(columns + row, SUB), head_size), :rows] = (
                dot_nt(projt_s[0, at, :lanes], grad_content) * score_scale
            ).astype(BF16)
            gt_s[at, :lanes] = (
                dot_nn(projt_s[1, at, :rows], grad_content) * score_scale
            ).astype(BF16)

        loop_heads(backward_head)

        first_t = first_b.T
        grad_proj = gt_s[:, :lanes].T[:rows]
        gqkv_ref[:, : 3 * columns] += dot_nn(first_t, grad_proj)
        grad_first = dot_nt(grad_proj, wback_ref[...])
        vec_s[0] += fold_rows(grad_first * unit_one)
        vec_s[2] += fold_rows(grad_first)
        input_grad = grad_hidden + norm_back(grad_first, unit_one, inverse_one, gains_ref[0:1, :])
        ig_ref[0] = dot_nn(selt_ref[...], input_grad.astype(BF16)).astype(BF16)

    for index, side in enumerate(SIDES):

        @pl.when(sizes_ref[step] == side)
        def _(index=index, side=side):
            image(side, sel_refs[index], selt_refs[index], place_refs[index], gsum_refs[index])

    @pl.when(step == steps - 1)
    def _():
        table = (gqkv_ref, gout_ref, g1_ref, g2t_ref)
        across = sum(ref.shape[1] // LANE for ref in table)
        row_tiles = columns // SUB

        def emit(index, carry):
            at = pl.ds(pl.multiple_of(index * SUB, SUB), SUB)
            place = index * across
            for ref in table:
                for col in range(ref.shape[1] // LANE):
                    tiles_ref[place] = ref[at, col * LANE : (col + 1) * LANE].astype(BF16)
                    place = place + 1
            return carry

        lax.fori_loop(0, row_tiles, emit, 0)
        for spare in range(row_tiles * across, tiles_ref.shape[0]):
            tiles_ref[spare] = jnp.zeros((SUB, LANE), BF16)

        small_ref[...] = jnp.zeros_like(small_ref)
        for row in range(6):
            small_ref[row : row + 1, :columns] = jnp.sum(vec_s[row], axis=0, keepdims=True)
        fc1_row = jnp.sum(fc1g_s[...], axis=0, keepdims=True)
        parts = hidden_units // columns
        for part in range(parts):
            small_ref[6 + part : 7 + part, :columns] = fc1_row[
                :, part * columns : (part + 1) * columns
            ]

        tile_rows = lax.broadcasted_iota(jnp.int32, (8, LANE), 0)
        tile_lanes = lax.broadcasted_iota(jnp.int32, (8, LANE), 1)

        def head_sums(head, carry):
            pieces = [jnp.zeros((1, 1), F32) for _ in range(4)]
            gate_open = 1.0 - gate_ref[head]
            for index, side in enumerate(SIDES):
                live, rows, lanes = side_sizes(side)
                middle = 0.5 * (side - 1)
                place = place_refs[index][head]
                weighted = gsum_refs[index][head] * place
                key_ids = lax.broadcasted_iota(jnp.int32, (rows, 1), 0)
                query_ids = lax.broadcasted_iota(jnp.int32, (1, lanes), 1)
                key_x = (key_ids % side).astype(F32) - middle
                key_y = (key_ids // side).astype(F32) - middle
                query_x = (query_ids % side).astype(F32) - middle
                query_y = (query_ids // side).astype(F32) - middle

                def moment(values, factor):
                    return jnp.sum(values * factor, axis=0, keepdims=True)

                base = jnp.sum(weighted, axis=0, keepdims=True)
                scaled = base / gate_open
                radius = key_x * key_x + key_y * key_y
                part_x = moment(weighted, key_x) - moment(place, key_x) * scaled
                part_y = moment(weighted, key_y) - moment(place, key_y) * scaled
                part_r = moment(weighted, radius) - moment(place, radius) * scaled
                part_r = part_r - 2.0 * (query_x * part_x + query_y * part_y)
                full = [part_x, part_y, part_r, gate_ref[head] * base]
                for row in range(4):
                    pieces[row] += jnp.sum(full[row], axis=1, keepdims=True)
            pieces[3] -= gate_open * gate_ref[head] * jnp.sum(racc_s[head], axis=1, keepdims=True)
            for row in range(4):
                carry = carry + jnp.where(
                    (tile_rows == row) & (tile_lanes == head), pieces[row], 0.0
                )
            return carry

        head_tile = lax.fori_loop(0, heads, head_sums, jnp.zeros((8, LANE), F32))
        first_row = 6 + parts
        small_ref[first_row : first_row + 4, :LANE] = head_tile[:4]


def run_images(
    x, ct, sizes, wqkv, wback, wout, w1, w2, gains, biases, fc1b, head_params, units, tiles, unroll_heads=3
):
    images, slots, columns = x.shape
    heads = head_params.shape[1]
    width = wqkv.shape[1] // 3
    padded = w1.shape[1]
    gate_value = jax.nn.sigmoid(head_params[3])
    sels = [jnp.asarray(select_matrix(side), BF16) for side in SIDES]
    selts = [jnp.asarray(select_matrix(side).T, BF16) for side in SIDES]
    places = [place_table(side, head_params, gate_value) for side in SIDES]
    sizes_all = [side_sizes(side) for side in SIDES]
    most_rows = max(size[1] for size in sizes_all)
    most_lanes = max(size[2] for size in sizes_all)

    def whole(array):
        rank = len(array.shape)
        return pl.BlockSpec(
            array.shape, lambda i, *_: (0,) * rank, pipeline_mode=pl.Buffered(1)
        )

    def image_spec():
        return pl.BlockSpec((1, slots, columns), lambda i, *_: (i, 0, 0))

    out_shapes = [
        jax.ShapeDtypeStruct((images, slots, columns), BF16),
        jax.ShapeDtypeStruct((images, slots, columns), BF16),
        jax.ShapeDtypeStruct((tiles, SUB, LANE), BF16),
        jax.ShapeDtypeStruct((SMALL_ROWS, width), F32),
    ]
    scratch = [
        pltpu.VMEM((most_lanes, 3 * width), BF16),
        pltpu.VMEM((3, width, most_lanes), BF16),
        pltpu.VMEM((most_lanes, width), BF16),
        pltpu.VMEM((width, most_lanes), BF16),
        pltpu.VMEM((heads, most_rows, most_lanes), F32),
        pltpu.VMEM((heads, most_rows, most_lanes), BF16),
        pltpu.VMEM((columns, most_lanes), BF16),
        pltpu.VMEM((3 * columns, most_lanes), BF16),
        pltpu.VMEM((most_rows, padded), BF16),
        pltpu.VMEM((most_rows, padded), BF16),
        pltpu.VMEM((6, 8, columns), F32),
        pltpu.VMEM((8, padded), F32),
        pltpu.VMEM((heads, 1, most_lanes), F32),
        pltpu.VMEM((columns, round_up(3 * columns, LANE)), F32),
        pltpu.VMEM((columns, width), F32),
        pltpu.VMEM((columns, padded), F32),
        pltpu.VMEM((columns, padded), F32),
        [pltpu.VMEM((heads, size[1], size[2]), F32) for size in sizes_all],
    ]
    hidden_units = units
    smalls = [sels, selts, places, wqkv, wback, wout, w1, w2, gains, biases, fc1b]
    specs = jax.tree.map(whole, smalls)
    body = functools.partial(image_kernel, columns, heads, hidden_units, unroll_heads)
    return pl.pallas_call(
        body,
        grid_spec=pltpu.PrefetchScalarGridSpec(
            num_scalar_prefetch=2,
            grid=(images,),
            in_specs=[image_spec(), image_spec()] + specs,
            out_specs=[image_spec(), image_spec()] + [whole(s) for s in out_shapes[2:]],
            scratch_shapes=scratch,
        ),
        out_shape=out_shapes,
        compiler_params=pltpu.CompilerParams(vmem_limit_bytes=VMEM_LIMIT),
        cost_estimate=pl.CostEstimate(flops=40_000_000_000, bytes_accessed=40_000_000, transcendentals=0),
    )(sizes, 1.0 - gate_value, x, ct, *smalls)


def pad_weights(w_qkv, w_out, w_fc1, w_fc2, fc1_bias):
    columns = w_qkv.shape[0]
    width = round_up(columns, LANE)
    units = round_up(w_fc1.shape[1], 256)
    extra = units - w_fc1.shape[1]
    wqkv = jnp.pad(
        w_qkv.astype(BF16).reshape(columns, 3, columns), ((0, 0), (0, 0), (0, width - columns))
    ).reshape(columns, 3 * width)
    wout = jnp.pad(w_out.astype(BF16), ((0, width - columns), (0, 0)))
    w1 = jnp.pad(w_fc1.astype(BF16), ((0, 0), (0, extra)))
    w2 = jnp.pad(w_fc2.astype(BF16), ((0, extra), (0, 0)))
    fc1b = jnp.pad(fc1_bias[None, :], ((0, 0), (0, extra)))
    return wqkv, w_qkv.astype(BF16), wout, w1, w2, fc1b
def reduce_plan(tile_total, devices):
    each = -(-tile_total // devices)
    waves = []
    base = 0
    for wave in range(WAVES):
        share = each // WAVES + (1 if wave < each % WAVES else 0)
        if share:
            first = -(-share // 2)
            waves.append((base, first, share - first))
            base += devices * share
    return waves, each * devices


def reduce_kernel(
    waves,
    rank_z,
    own_ref,
    small_ref,
    full_out,
    small_out,
    own,
    full,
    recv0,
    recv1,
    recv2,
    recv3,
    small_own,
    small_recv,
    send_sem,
    recv_sem,
    small_send,
    small_got,
    copy_sem,
):
    img = lax.axis_index("img")
    band = lax.axis_index("band")
    z, y = img // 2, img % 2
    x, c = band // 2, band % 2
    half_ranks = 4 * rank_z
    near = (img, x * 2 + 1 - c)
    near_x = (img, (1 - x) * 2 + c)
    near_y = (z * 2 + 1 - y, band)
    far_z = [(lax.rem(z + k, rank_z) * 2 + y, band) for k in range(1, rank_z)]
    partners = [near, near_x, near_y] + far_z
    mesh_ids = pl.DeviceIdType.MESH

    load = pltpu.make_async_copy(own_ref, own, copy_sem.at[0])
    load.start()
    small_own[...] = small_ref[...]

    barrier = pltpu.get_barrier_semaphore()
    for partner in partners:
        pl.semaphore_signal(barrier, inc=1, device_id=partner, device_id_type=mesh_ids)
    pl.semaphore_wait(barrier, len(partners))
    load.wait()

    counters = [0] * len(waves)

    def send(wave, src, dst, target):
        slot = counters[wave]
        counters[wave] += 1
        copy = pltpu.make_async_remote_copy(
            src_ref=src,
            dst_ref=dst,
            send_sem=send_sem.at[wave, slot],
            recv_sem=recv_sem.at[wave, slot],
            device_id=target,
            device_id_type=mesh_ids,
        )
        copy.start()
        return copy

    def send_small(slot, src, dst, target):
        copy = pltpu.make_async_remote_copy(
            src_ref=src,
            dst_ref=dst,
            send_sem=small_send.at[slot],
            recv_sem=small_got.at[slot],
            device_id=target,
            device_id_type=mesh_ids,
        )
        copy.start()
        return copy

    def add_tiles(dst, dst_at, parts, count, out=None, out_at=None):
        out = dst if out is None else out
        out_at = dst_at if out_at is None else out_at
        block = 8

        def one(offset, size):
            total = dst[pl.ds(dst_at + offset, size)].astype(F32)
            for ref, at in parts:
                total += ref[pl.ds(at + offset, size)].astype(F32)
            out[pl.ds(out_at + offset, size)] = total.astype(BF16)

        if count >= block:

            def step(index, carry):
                one(index * block, block)
                return carry

            lax.fori_loop(0, count // block, step, 0)
        rest = count % block
        if rest:
            one(count - rest, rest)

    geometry = []
    at1 = at2 = at3 = 0
    for base, first, second in waves:
        half = half_ranks * (first + second)
        mine = base + c * half
        geometry.append(
            dict(
                base=base,
                half=half,
                mine=mine,
                a=first,
                b=second,
                base_a=mine,
                base_b=mine + half_ranks * first,
                at0=base // 2,
                at1a=at1,
                at1b=at1 + 2 * rank_z * first,
                at2a=at2,
                at2b=at2 + rank_z * first,
                at3a=at3,
                at3b=at3 + (rank_z - 1) * first,
            )
        )
        at1 += 2 * rank_z * (first + second)
        at2 += rank_z * (first + second)
        at3 += (rank_z - 1) * (first + second)

    wave_ids = range(len(waves))
    pending = {}
    small_copy = send_small(0, small_own, small_recv.at[0], near)
    for w in wave_ids:
        g = geometry[w]
        pending[w] = [
            send(
                w,
                own.at[pl.ds(g["base"] + (1 - c) * g["half"], g["half"])],
                recv0.at[pl.ds(g["at0"], g["half"])],
                near,
            )
        ]

    for w in wave_ids:
        g = geometry[w]
        for copy in pending[w]:
            copy.wait()
        add_tiles(own, g["mine"], [(recv0, g["at0"])], g["half"])
        size_a, size_b = 2 * rank_z * g["a"], 2 * rank_z * g["b"]
        pending[w] = [
            send(
                w,
                own.at[pl.ds(g["base_a"] + (1 - x) * size_a, size_a)],
                recv1.at[pl.ds(g["at1a"], size_a)],
                near_x,
            )
        ]
        if size_b:
            pending[w].append(
                send(
                    w,
                    own.at[pl.ds(g["base_b"] + (1 - y) * size_b, size_b)],
                    recv1.at[pl.ds(g["at1b"], size_b)],
                    near_y,
                )
            )

    small_copy.wait()
    small_own[...] = small_own[...] + small_recv[0]
    small_copy = send_small(1, small_own, small_recv.at[1], near_x)

    for w in wave_ids:
        g = geometry[w]
        for copy in pending[w]:
            copy.wait()
        size_a, size_b = 2 * rank_z * g["a"], 2 * rank_z * g["b"]
        at_a, at_b = g["base_a"] + x * size_a, g["base_b"] + y * size_b
        add_tiles(own, at_a, [(recv1, g["at1a"])], size_a)
        add_tiles(own, at_b, [(recv1, g["at1b"])], size_b)
        size_a, size_b = size_a // 2, size_b // 2
        pending[w] = [
            send(
                w,
                own.at[pl.ds(at_a + (1 - y) * size_a, size_a)],
                recv2.at[pl.ds(g["at2a"], size_a)],
                near_y,
            )
        ]
        if size_b:
            pending[w].append(
                send(
                    w,
                    own.at[pl.ds(at_b + (1 - x) * size_b, size_b)],
                    recv2.at[pl.ds(g["at2b"], size_b)],
                    near_x,
                )
            )
        g["line_a"] = at_a + y * size_a
        g["line_b"] = at_b + x * size_b

    small_copy.wait()
    small_own[...] = small_own[...] + small_recv[1]
    small_copy = send_small(2, small_own, small_recv.at[2], near_y)

    for w in wave_ids:
        g = geometry[w]
        for copy in pending[w]:
            copy.wait()
        add_tiles(own, g["line_a"], [(recv2, g["at2a"])], rank_z * g["a"])
        add_tiles(own, g["line_b"], [(recv2, g["at2b"])], rank_z * g["b"])
        pending[w] = []
        for k in range(1, rank_z):
            other = lax.rem(z + k, rank_z)
            for name, size in (("a", g["a"]), ("b", g["b"])):
                if size:
                    pending[w].append(
                        send(
                            w,
                            own.at[pl.ds(g["line_" + name] + other * size, size)],
                            recv3.at[pl.ds(g["at3" + name] + (k - 1) * size, size)],
                            far_z[k - 1],
                        )
                    )

    small_copy.wait()
    small_own[...] = small_own[...] + small_recv[2]
    small_recv[3] = small_own[...]
    small_copies = [
        send_small(2 + k, small_own, small_recv.at[3 + k], far_z[k - 1]) for k in range(1, rank_z)
    ]

    for w in wave_ids:
        g = geometry[w]
        for copy in pending[w]:
            copy.wait()
        pending[w] = []
        for name, size in (("a", g["a"]), ("b", g["b"])):
            if not size:
                continue
            at = g["line_" + name] + z * size
            parts = [(recv3, g["at3" + name] + k * size) for k in range(rank_z - 1)]
            add_tiles(own, at, parts, size, full, at)
            for k in range(1, rank_z):
                piece = full.at[pl.ds(at, size)]
                pending[w].append(send(w, piece, piece, far_z[k - 1]))

    for copy in small_copies:
        copy.wait()

    def add_line(index, total):
        return total + small_recv[3 + lax.rem(index - z + rank_z, rank_z)]

    small_out[...] = lax.fori_loop(
        1, rank_z, add_line, small_recv[3 + lax.rem(rank_z - z, rank_z)]
    )

    for w in wave_ids:
        g = geometry[w]
        for copy in pending[w]:
            copy.wait()
        piece = full.at[pl.ds(g["line_a"], rank_z * g["a"])]
        pending[w] = [send(w, piece, piece, near_y)]
        if g["b"]:
            piece = full.at[pl.ds(g["line_b"], rank_z * g["b"])]
            pending[w].append(send(w, piece, piece, near_x))

    for w in wave_ids:
        g = geometry[w]
        for copy in pending[w]:
            copy.wait()
        size_a, size_b = 2 * rank_z * g["a"], 2 * rank_z * g["b"]
        piece = full.at[pl.ds(g["base_a"] + x * size_a, size_a)]
        pending[w] = [send(w, piece, piece, near_x)]
        if size_b:
            piece = full.at[pl.ds(g["base_b"] + y * size_b, size_b)]
            pending[w].append(send(w, piece, piece, near_y))

    for w in wave_ids:
        g = geometry[w]
        for copy in pending[w]:
            copy.wait()
        piece = full.at[pl.ds(g["mine"], g["half"])]
        pending[w] = [send(w, piece, piece, near)]

    for w in wave_ids:
        for copy in pending[w]:
            copy.wait()
    store = pltpu.make_async_copy(full, full_out, copy_sem.at[1])
    store.start()
    store.wait()


def reduce_all(tiles, small, waves, img_count):
    total = tiles.shape[0]
    rank_z = img_count // 2
    per = sum(first + second for _, first, second in waves)
    copies = 2 * (5 + 2 * (rank_z - 1))
    return pl.pallas_call(
        functools.partial(reduce_kernel, waves, rank_z),
        out_shape=[
            jax.ShapeDtypeStruct(tiles.shape, BF16),
            jax.ShapeDtypeStruct(small.shape, F32),
        ],
        in_specs=[pl.BlockSpec(memory_space=pl.ANY), pl.BlockSpec(memory_space=pltpu.VMEM)],
        out_specs=[pl.BlockSpec(memory_space=pl.ANY), pl.BlockSpec(memory_space=pltpu.VMEM)],
        scratch_shapes=[
            pltpu.VMEM(tiles.shape, BF16),
            pltpu.VMEM(tiles.shape, BF16),
            pltpu.VMEM((total // 2, SUB, LANE), BF16),
            pltpu.VMEM((2 * rank_z * per, SUB, LANE), BF16),
            pltpu.VMEM((rank_z * per, SUB, LANE), BF16),
            pltpu.VMEM((max(rank_z - 1, 1) * per, SUB, LANE), BF16),
            pltpu.VMEM(small.shape, F32),
            pltpu.VMEM((3 + rank_z,) + small.shape, F32),
            pltpu.SemaphoreType.DMA((len(waves), copies)),
            pltpu.SemaphoreType.DMA((len(waves), copies)),
            pltpu.SemaphoreType.DMA((2 + rank_z,)),
            pltpu.SemaphoreType.DMA((2 + rank_z,)),
            pltpu.SemaphoreType.DMA((2,)),
        ],
        compiler_params=pltpu.CompilerParams(
            collective_id=1, has_side_effects=True, vmem_limit_bytes=VMEM_LIMIT
        ),
    )(tiles, small)


def update_kernel(
    decay_rate,
    head_count,
    tiles_ref,
    small_ref,
    weight_refs,
    row_refs,
    col_refs,
    vector_refs,
    moment_refs,
    norm_out,
    grad_outs,
    vgrad_outs,
    new_outs,
    vnew_outs,
    row_outs,
    col_outs,
    moment_outs,
    natural,
    flipped,
    rowsq,
):
    columns = weight_refs[1].shape[0]
    across = sum(ref.shape[1] // LANE for ref in natural)
    block = 48

    def gather(index, carry):
        at = pl.ds(pl.multiple_of(index * SUB, SUB), SUB)
        place = index * across
        for ref in natural:
            for col in range(ref.shape[1] // LANE):
                ref[at, col * LANE : (col + 1) * LANE] = tiles_ref[place]
                place = place + 1
        return carry

    lax.fori_loop(0, columns // SUB, gather, 0)
    flipped[...] = natural[3][...].T
    grads = (natural[0], natural[1], natural[2], flipped)
    shapes = [ref.shape for ref in weight_refs]

    col_squares = []
    total = jnp.zeros((1, 1), F32)
    for index in range(4):
        count, wide = shapes[index]

        def measure(step, carry, index=index, wide=wide):
            at = pl.ds(pl.multiple_of(step * block, SUB), block)
            grad = grads[index][at, :wide].astype(F32)
            square = grad * grad
            rowsq[index][at, :] = jnp.sum(square, axis=1, keepdims=True)
            return carry + fold_rows(square)

        folded = lax.fori_loop(0, count // block, measure, jnp.zeros((8, wide), F32))
        col_square = jnp.sum(folded, axis=0, keepdims=True)
        col_squares.append(col_square)
        total += jnp.sum(col_square, axis=1, keepdims=True)

    parts = vector_refs[2].shape[0]
    places = (
        (slice(0, 2), columns),
        (slice(2, 6), columns),
        (slice(6, 6 + parts), columns),
        (slice(6 + parts, 10 + parts), head_count),
    )
    vectors = [small_ref[rows, :wide] for rows, wide in places]
    for grad in vectors:
        total += jnp.sum(jnp.sum(grad * grad, axis=0, keepdims=True), axis=1, keepdims=True)
    norm = jnp.sqrt(total)
    norm_out[...] = norm
    factor = 1.0 / jnp.maximum(norm, 1.0)

    for index in range(4):
        grad = vectors[index] * factor
        weight = vector_refs[index][...]
        moment = decay_rate * moment_refs[index][...] + (1.0 - decay_rate) * (
            grad * grad + FLOOR_ONE
        )
        update = grad * lax.rsqrt(moment)
        size = weight.shape[0] * weight.shape[1]

        def average(values, size=size):
            return jnp.sum(jnp.sum(values, axis=0, keepdims=True), axis=1, keepdims=True) / size

        update = update / jnp.maximum(1.0, jnp.sqrt(average(update * update)) / CLIP_RMS)
        scale = STEP_RATE * jnp.maximum(FLOOR_TWO, jnp.sqrt(average(weight * weight)))
        vgrad_outs[index][...] = grad
        vnew_outs[index][...] = weight - scale * update
        moment_outs[index][...] = moment

    for index in range(4):
        count, wide = shapes[index]
        row_old = jnp.broadcast_to(row_refs[index][...], (LANE, count)).T
        rows_new = decay_rate * row_old + (1.0 - decay_rate) * (
            rowsq[index][...] * (factor * factor) / wide + FLOOR_ONE
        )
        cols_new = decay_rate * col_refs[index][...] + (1.0 - decay_rate) * (
            col_squares[index] * (factor * factor) / count + FLOOR_ONE
        )
        row_outs[index][...] = rows_new.T[:1, :]
        col_outs[index][...] = cols_new
        row_mean = jnp.sum(rows_new[:, :1], axis=0, keepdims=True) / count
        rowsq[index][...] = lax.rsqrt(rows_new[:, :1] / row_mean) * factor
        col_factor = lax.rsqrt(cols_new)

        def scan(step, carry, index=index, wide=wide, col_factor=col_factor):
            at = pl.ds(pl.multiple_of(step * block, SUB), block)
            update = grads[index][at, :wide].astype(F32) * col_factor * rowsq[index][at, :]
            weight = weight_refs[index][at, :]
            return (
                carry[0] + fold_rows(update * update),
                carry[1] + fold_rows(weight * weight),
            )

        zero = jnp.zeros((8, wide), F32)
        sums = lax.fori_loop(0, count // block, scan, (zero, zero))
        means = [
            jnp.sum(jnp.sum(s, axis=0, keepdims=True), axis=1, keepdims=True) / (count * wide)
            for s in sums
        ]
        scale = STEP_RATE * jnp.maximum(FLOOR_TWO, jnp.sqrt(means[1]))
        scale = scale / jnp.maximum(1.0, jnp.sqrt(means[0]) / CLIP_RMS)

        def write(step, carry, index=index, wide=wide, col_factor=col_factor, scale=scale):
            at = pl.ds(pl.multiple_of(step * block, SUB), block)
            grad = grads[index][at, :wide].astype(F32)
            grad_outs[index][at, :] = grad * factor
            update = grad * col_factor * (rowsq[index][at, :] * scale)
            new_outs[index][at, :] = weight_refs[index][at, :] - update
            return carry

        lax.fori_loop(0, count // block, write, 0)


def update_all(tiles, small, weights, rows, cols, vectors, moments, decay_rate):
    columns = weights[1].shape[0]
    head_count = vectors[3].shape[1]
    units = weights[2].shape[1]
    parts = units // columns
    flat = lambda v: v.reshape(1, -1)
    rows = [flat(v) for v in rows]
    cols = [flat(v) for v in cols]
    vectors = [v.reshape(parts, columns) if v.ndim == 1 else v for v in vectors]
    moments = [v.reshape(parts, columns) if v.ndim == 1 else v for v in moments]
    like = lambda group: [jax.ShapeDtypeStruct(v.shape, F32) for v in group]
    outs = [
        jax.ShapeDtypeStruct((1, 1), F32),
        like(weights),
        like(vectors),
        like(weights),
        like(vectors),
        like(rows),
        like(cols),
        like(vectors),
    ]
    vmem = pl.BlockSpec(memory_space=pltpu.VMEM)
    args = (tiles, small, list(weights), rows, cols, vectors, moments)
    padded = round_up(units, 256)
    scratch = [
        [
            pltpu.VMEM((columns, round_up(3 * columns, LANE)), BF16),
            pltpu.VMEM((columns, round_up(columns, LANE)), BF16),
            pltpu.VMEM((columns, padded), BF16),
            pltpu.VMEM((columns, padded), BF16),
        ],
        pltpu.VMEM((padded, columns), BF16),
        [pltpu.VMEM((weight.shape[0], 1), F32) for weight in weights],
    ]
    made = pl.pallas_call(
        functools.partial(update_kernel, decay_rate, head_count),
        out_shape=outs,
        in_specs=jax.tree.map(lambda _: vmem, args),
        out_specs=jax.tree.map(lambda _: vmem, outs),
        scratch_shapes=scratch,
        compiler_params=pltpu.CompilerParams(vmem_limit_bytes=VMEM_LIMIT),
    )(*args)
    norm, grads, vgrads, news, vnews, row_new, col_new, moment_new = made
    spread = lambda group: [v.reshape(-1) if i == 2 else v for i, v in enumerate(group)]
    moved = []
    for index in range(4):
        moved += [row_new[index].reshape(-1), col_new[index].reshape(-1)]
    return (
        norm.reshape(1),
        *grads,
        *spread(vgrads),
        *news,
        *spread(vnews),
        *moved,
        *spread(moment_new),
    )


def deal_images(grid_sizes, devices):
    count = grid_sizes.shape[0]
    ids = jnp.arange(count, dtype=jnp.int32)
    ahead = (grid_sizes[None, :] > grid_sizes[:, None]) | (
        (grid_sizes[None, :] == grid_sizes[:, None]) & (ids[None, :] < ids[:, None])
    )
    rank = jnp.sum(ahead.astype(jnp.int32), axis=1)
    turn = rank // devices
    seat = rank % devices
    seat = jnp.where(turn % 2 == 0, seat, devices - 1 - seat)
    place = seat * (count // devices) + turn
    order = jnp.sum(jnp.where(place[None, :] == ids[:, None], ids[None, :], 0), axis=1)
    return order, place


def per_device(
    inputs,
    cotangent,
    grid_sizes,
    w_qkv,
    w_out,
    w_fc1,
    w_fc2,
    norm_gains,
    biases,
    fc1_bias,
    head_params,
    rows_qkv,
    cols_qkv,
    rows_out,
    cols_out,
    rows_fc1,
    cols_fc1,
    rows_fc2,
    cols_fc2,
    gain_moment,
    bias_moment,
    fc1_bias_moment,
    head_moment,
):
    band_count = lax.axis_size("band")
    img_count = lax.axis_size("img")
    band_index = lax.axis_index("band")
    columns = inputs.shape[2]
    units = w_fc1.shape[1]
    per_band = inputs.shape[0] // band_count
    order, place = deal_images(grid_sizes, band_count)
    sizes_used = lax.dynamic_slice_in_dim(grid_sizes[order], band_index * per_band, per_band)
    inputs_used = lax.all_to_all(inputs[order], "band", split_axis=0, concat_axis=1, tiled=True)
    cotangent_used = lax.all_to_all(
        cotangent[order], "band", split_axis=0, concat_axis=1, tiled=True
    )
    tile_total = (columns // SUB) * (
        round_up(3 * columns, LANE) + round_up(columns, LANE) + 2 * round_up(units, 256)
    ) // LANE
    waves, tile_count = reduce_plan(tile_total, band_count * img_count)
    wqkv, wback, wout, w1, w2, fc1b = pad_weights(w_qkv, w_out, w_fc1, w_fc2, fc1_bias)
    output, input_grad, tiles, small = run_images(
        inputs_used, cotangent_used, sizes_used, wqkv, wback, wout, w1, w2, norm_gains, biases,
        fc1b, head_params, units, tile_count,
    )
    output_back = lax.all_to_all(output, "band", split_axis=1, concat_axis=0, tiled=True)
    input_back = lax.all_to_all(input_grad, "band", split_axis=1, concat_axis=0, tiled=True)
    output = output_back[place]
    input_grad = input_back[place].astype(F32)
    full, small = reduce_all(tiles, small, waves, img_count)
    updated = update_all(
        full,
        small,
        (w_qkv, w_out, w_fc1, w_fc2),
        (rows_qkv, rows_out, rows_fc1, rows_fc2),
        (cols_qkv, cols_out, cols_fc1, cols_fc2),
        (norm_gains, biases, fc1_bias, head_params),
        (gain_moment, bias_moment, fc1_bias_moment, head_moment),
        1.0 - STEP ** (-0.8),
    )
    return (output, input_grad, *updated)


def solution(mesh):
    split = P("img", "band", None)
    return jax.shard_map(
        per_device,
        mesh=mesh,
        in_specs=(split, split, P("img")) + (P(),) * 20,
        out_specs=(split, split) + (P(),) * 29,
        check_vma=False,
    )
```

```python
import functools
import math

import jax
import jax.numpy as jnp
import numpy as np
from jax import lax
from jax.experimental import pallas as pl
from jax.experimental.pallas import tpu as pltpu
from jax.sharding import PartitionSpec as P

GRID = 20
STEP = 10
SIDES = (18, 14, 10)

NORM_FLOOR = 1e-06
FLOOR_ONE = 1e-30
FLOOR_TWO = 0.001
STEP_RATE = 0.6
CLIP_RMS = 1.0
MASKED = -1e30

BF16 = jnp.bfloat16
F32 = jnp.float32
VMEM_LIMIT = 60 * 1024 * 1024
SUB = 16
SMALL_ROWS = 16
WAVES = 4
AXIS_ORDER = "cylhx"
LANE = 128


def round_up(value, unit):
    return (value + unit - 1) // unit * unit


def side_sizes(side):
    live = side * side
    return live, round_up(live, SUB), round_up(live, LANE)


def dot_nn(left, right):
    return lax.dot_general(left, right, (((1,), (0,)), ((), ())), preferred_element_type=F32)


def dot_nt(left, right):
    return lax.dot_general(left, right, (((1,), (1,)), ((), ())), preferred_element_type=F32)


def piece_rows(bands):
    return round_up(GRID // bands * max(SIDES), SUB)


def select_matrix(side, bands):
    live, rows, _ = side_sizes(side)
    tall, piece = GRID // bands, piece_rows(bands)
    made = np.zeros((rows, bands * piece), np.float32)
    for row in range(side):
        for col in range(side):
            at = row // tall * piece + (row % tall) * side + col
            made[row * side + col, at] = 1.0
    return made


def pack_matrix(bands):
    tall, piece = GRID // bands, piece_rows(bands)
    made = np.zeros((len(SIDES), piece, tall * GRID), np.float32)
    for index, side in enumerate(SIDES):
        for row in range(tall):
            for col in range(side):
                made[index, row * side + col, row * GRID + col] = 1.0
    return made


def fold_rows(values):
    rows, columns = values.shape
    return jnp.sum(values.reshape(rows // 8, 8, columns), axis=0)


def image_kernel(
    columns,
    heads,
    hidden_units,
    started,
    sizes_ref,
    gate_ref,
    xct_ref,
    tiles_in,
    small_in,
    sel_refs,
    selt_refs,
    place_hbm,
    weight_hbm,
    gains_ref,
    biases_ref,
    fc1b_ref,
    outig_ref,
    tiles_ref,
    small_ref,
    proj_s,
    projt_s,
    da_s,
    dat_s,
    cont_s,
    mix_s,
    attt_s,
    gt_s,
    act_s,
    gb_s,
    vec_s,
    fc1g_s,
    racc_s,
    gqkv_ref,
    gout_ref,
    g1_ref,
    g2t_ref,
    gsum_refs,
    gm_s,
    gc_s,
    place_refs,
    weight_refs,
    copy_sem,
):
    wqkv_ref, wback_ref, wout_ref, w1_ref, w2t_ref = weight_refs
    step = pl.program_id(0)
    steps = pl.num_programs(0)
    head_size = columns // heads
    width = wqkv_ref.shape[1] // 3
    window = 256
    score_scale = head_size ** (-0.5)
    chunk = 256
    chunks = w1_ref.shape[1] // chunk

    table = (gqkv_ref, gout_ref, g1_ref, g2t_ref)
    across = sum(ref.shape[1] // LANE for ref in table)
    row_tiles = columns // SUB

    sources = list(weight_hbm) + list(place_hbm)
    targets = list(weight_refs) + list(place_refs)
    loads = [
        pltpu.make_async_copy(source, target, copy_sem.at[1 + index])
        for index, (source, target) in enumerate(zip(sources, targets))
    ]
    load_qkv, load_back, load_out, load_w1, load_w2 = loads[:5]
    load_places = loads[5:]

    def once(*copies):
        @pl.when(step == 0)
        def _():
            for copy in copies:
                copy.wait()

    @pl.when(step == 0)
    def _():
        if started:
            load = pltpu.make_async_copy(tiles_in, tiles_ref, copy_sem.at[0])
            load.start()
        for copy in [load_qkv] + load_places + [load_out, load_w1, load_w2, load_back]:
            copy.start()
        if started:
            load.wait()

            def absorb(index, carry):
                at = pl.ds(pl.multiple_of(index * SUB, SUB), SUB)
                place = index * across
                for ref in table:
                    for col in range(ref.shape[1] // LANE):
                        ref[at, col * LANE : (col + 1) * LANE] = tiles_ref[place].astype(F32)
                        place = place + 1
                return carry

            lax.fori_loop(0, row_tiles, absorb, 0)
        else:
            for ref in table:
                ref[...] = jnp.zeros_like(ref)
        vec_s[...] = jnp.zeros_like(vec_s)
        fc1g_s[...] = jnp.zeros_like(fc1g_s)
        racc_s[...] = jnp.zeros_like(racc_s)
        for ref in gsum_refs:
            ref[...] = jnp.zeros_like(ref)

    def head_place(head):
        first_lane = head * head_size
        start = min(first_lane // LANE * LANE, width - window)
        lanes = lax.broadcasted_iota(jnp.int32, (1, window), 1) + start
        mask = (lanes >= first_lane) & (lanes < first_lane + head_size)
        return start, mask, first_lane

    def skewed(*stages):
        for index in range(heads + len(stages) - 1):
            for late, stage in enumerate(stages):
                if 0 <= index - late < heads:
                    stage(index - late)

    def image(side, sel_ref, selt_ref, place_ref, gsum_ref):
        live, rows, lanes = side_sizes(side)
        edge = live // 8 * 8
        tall = outig_ref.shape[3]

        def norm(values):
            averaged = jnp.mean(values, axis=-1, keepdims=True)
            centered = values - averaged
            variance = jnp.mean(centered * centered, axis=-1, keepdims=True)
            inverse = lax.rsqrt(variance + NORM_FLOOR)
            return centered * inverse, inverse

        def norm_back(grad, unit, inverse, gain):
            scaled = grad * gain
            first_mean = jnp.mean(scaled, axis=-1, keepdims=True)
            second_mean = jnp.mean(scaled * unit, axis=-1, keepdims=True)
            return inverse * (scaled - first_mean - unit * second_mean)

        x = dot_nn(sel_ref[...], xct_ref[:, 0, 0].reshape(-1, columns))
        unit_one, inverse_one = norm(x)
        first_b = (unit_one * gains_ref[0:1, :] + biases_ref[0:1, :]).astype(BF16)
        once(load_qkv)
        proj_s[:rows, :] = dot_nn(first_b, wqkv_ref[...]).astype(BF16)
        once(*load_places)
        if lanes > rows:
            proj_s[rows:lanes, :] = jnp.zeros((lanes - rows, 3 * width), BF16)
        for part in range(3):
            piece = proj_s[:lanes, part * width : (part + 1) * width]
            projt_s[part, :, :lanes] = piece.T

        def score_head(head):
            start, mask, row = head_place(head)
            query = jnp.where(mask, proj_s[:lanes, start : start + window], 0)
            key = proj_s[:rows, width + start : width + start + window]
            cont_s[head, :rows, :lanes] = dot_nt(key, query)

        def soft_head(head):
            score = cont_s[head, :rows, :lanes] * (score_scale * math.log2(math.e))
            tail = lax.broadcasted_iota(jnp.int32, (rows - edge, lanes), 0) < live - edge
            score = jnp.concatenate(
                [score[:edge], jnp.where(tail, score[edge:], MASKED)], axis=0
            )
            top = jnp.max(score, axis=0, keepdims=True)
            raised = jnp.exp2(score - top)
            total = jnp.sum(raised, axis=0, keepdims=True)
            content = raised * (gate_ref[head] / total)
            cont_s[head, :rows, :lanes] = content
            mix_s[head, :rows, :lanes] = (content + place_ref[head]).astype(BF16)

        def attend_head(head):
            row = head * head_size
            value_t = projt_s[2, row : row + head_size, :rows]
            mixed = mix_s[head, :rows, :lanes]
            attt_s[row : row + head_size, :lanes] = dot_nn(value_t, mixed).astype(BF16)

        skewed(score_head, soft_head, attend_head)

        once(load_out, load_w1, load_w2, load_back)
        attended = attt_s[:, :lanes].T[:rows]
        hidden = x + (dot_nn(attended, wout_ref[:columns, :]) + biases_ref[2:3, :])
        unit_two, inverse_two = norm(hidden)
        second_b = (unit_two * gains_ref[1:2, :] + biases_ref[1:2, :]).astype(BF16)
        ct_b = dot_nn(sel_ref[...], xct_ref[:, 1, 0].reshape(-1, columns)).astype(BF16)

        for index in range(chunks):
            at = slice(index * chunk, (index + 1) * chunk)
            before = dot_nn(second_b, w1_ref[:, at]) + fc1b_ref[:, at]
            grad_act = dot_nn(ct_b, w2t_ref[:, at])
            square = before * before
            inner = before * (
                math.sqrt(2.0 / math.pi) + (math.sqrt(2.0 / math.pi) * 0.044715) * square
            )
            half = 0.5 * jnp.tanh(inner) + 0.5
            activated = before * half
            slope = half + activated * (1.0 - half) * (
                2.0 * math.sqrt(2.0 / math.pi)
                + (6.0 * math.sqrt(2.0 / math.pi) * 0.044715) * square
            )
            act_s[:rows, at] = activated.astype(BF16)
            grad_b = (grad_act * slope).astype(BF16)
            gb_s[:rows, at] = grad_b
            fc1g_s[:, at] += fold_rows(grad_b.astype(F32))

        result = (
            hidden + dot_nt(act_s[:rows, :], w2t_ref[...]) + biases_ref[3:4, :]
        )
        outig_ref[:, 0, 0] = (
            dot_nn(selt_ref[...], result.astype(BF16)).astype(BF16).reshape(-1, tall, columns)
        )

        ct_t = ct_b.T
        second_t = second_b.T
        units = hidden_units
        for index in range(chunks):
            low, high = index * chunk, min((index + 1) * chunk, units)
            g1_ref[:, low:high] += dot_nn(second_t, gb_s[:rows, low:high])
            g2t_ref[:, low:high] += dot_nn(ct_t, act_s[:rows, low:high])

        ct_f = ct_b.astype(F32)
        grad_second = dot_nt(gb_s[:rows, :], w1_ref[...])
        grad_hidden = ct_f + norm_back(grad_second, unit_two, inverse_two, gains_ref[1:2, :])
        branch_b = grad_hidden.astype(BF16)
        vec_s[1] += fold_rows(grad_second * unit_two)
        vec_s[3] += fold_rows(grad_second)
        vec_s[4] += fold_rows(branch_b.astype(F32))
        vec_s[5] += fold_rows(ct_f)
        gout_ref[:, :columns] += dot_nn(attt_s[:, :rows], branch_b)
        da_s[:rows, :] = dot_nt(branch_b, wout_ref[...]).astype(BF16)
        if lanes > rows:
            da_s[rows:lanes, :] = jnp.zeros((lanes - rows, width), BF16)
        dat_s[:, :lanes] = da_s[:lanes, :].T

        def grad_head(head):
            start, mask, row = head_place(head)
            grad_att = jnp.where(mask, da_s[:lanes, start : start + window], 0)
            value = proj_s[:rows, 2 * width + start : 2 * width + start + window]
            gm_s[head % 2, :rows, :lanes] = dot_nt(value, grad_att)

        def soft_back_head(head):
            grad_mixed = gm_s[head % 2, :rows, :lanes]
            gsum_ref[head] += grad_mixed
            content = cont_s[head, :rows, :lanes]
            product = grad_mixed * content
            total = jnp.sum(product, axis=0, keepdims=True) / gate_ref[head]
            racc_s[head, :, :lanes] += total
            gc_s[head % 2, :rows, :lanes] = (product - content * total).astype(BF16)

        def back_head(head):
            row = head * head_size
            here = slice(row, row + head_size)
            mixed = mix_s[head, :rows, :lanes]
            grad_content = gc_s[head % 2, :rows, :lanes]
            gt_s[2 * columns + row : 2 * columns + row + head_size, :rows] = dot_nt(
                dat_s[here, :lanes], mixed
            ).astype(BF16)
            gt_s[columns + row : columns + row + head_size, :rows] = (
                dot_nt(projt_s[0, here, :lanes], grad_content) * score_scale
            ).astype(BF16)
            gt_s[here, :lanes] = (
                dot_nn(projt_s[1, here, :rows], grad_content) * score_scale
            ).astype(BF16)

        skewed(grad_head, soft_back_head, back_head)

        first_t = first_b.T
        grad_proj = gt_s[:, :lanes].T[:rows]
        gqkv_ref[:, : 3 * columns] += dot_nn(first_t, grad_proj)
        grad_first = dot_nt(grad_proj, wback_ref[...])
        vec_s[0] += fold_rows(grad_first * unit_one)
        vec_s[2] += fold_rows(grad_first)
        input_grad = grad_hidden + norm_back(grad_first, unit_one, inverse_one, gains_ref[0:1, :])
        outig_ref[:, 1, 0] = (
            dot_nn(selt_ref[...], input_grad.astype(BF16))
            .astype(BF16)
            .reshape(-1, tall, columns)
        )

    for index, side in enumerate(SIDES):

        @pl.when(sizes_ref[step] == side)
        def _(index=index, side=side):
            image(side, sel_refs[index], selt_refs[index], place_refs[index], gsum_refs[index])

    @pl.when(step == steps - 1)
    def _():
        def emit(index, carry):
            at = pl.ds(pl.multiple_of(index * SUB, SUB), SUB)
            place = index * across
            for ref in table:
                for col in range(ref.shape[1] // LANE):
                    tiles_ref[place] = ref[at, col * LANE : (col + 1) * LANE].astype(BF16)
                    place = place + 1
            return carry

        lax.fori_loop(0, row_tiles, emit, 0)
        for spare in range(row_tiles * across, tiles_ref.shape[0]):
            tiles_ref[spare] = jnp.zeros((SUB, LANE), BF16)

        small_ref[...] = jnp.zeros_like(small_ref)
        for row in range(6):
            small_ref[row : row + 1, :columns] = jnp.sum(vec_s[row], axis=0, keepdims=True)
        fc1_row = jnp.sum(fc1g_s[...], axis=0, keepdims=True)
        parts = hidden_units // columns
        for part in range(parts):
            small_ref[6 + part : 7 + part, :columns] = fc1_row[
                :, part * columns : (part + 1) * columns
            ]

        tile_rows = lax.broadcasted_iota(jnp.int32, (8, LANE), 0)
        tile_lanes = lax.broadcasted_iota(jnp.int32, (8, LANE), 1)
        grids = []
        for side in SIDES:
            rows, lanes = side_sizes(side)[1:]
            middle = 0.5 * (side - 1)
            key_ids = lax.broadcasted_iota(jnp.int32, (rows, LANE), 0).astype(F32)
            key_row = jnp.floor((key_ids + 0.5) * (1.0 / side))
            key_x, key_y = key_ids - side * key_row - middle, key_row - middle
            query_ids = lax.broadcasted_iota(jnp.int32, (1, lanes), 1).astype(F32)
            query_row = jnp.floor((query_ids + 0.5) * (1.0 / side))
            query_x, query_y = query_ids - side * query_row - middle, query_row - middle
            grids.append((key_x, key_y, key_x * key_x + key_y * key_y, query_x, query_y))

        def head_sums(head, carry):
            pieces = [jnp.zeros((1, LANE), F32) for _ in range(4)]
            gate_open = 1.0 - gate_ref[head]
            for index, side in enumerate(SIDES):
                lanes = side_sizes(side)[2]
                key_x, key_y, radius, query_x, query_y = grids[index]

                def total(values):
                    return jnp.sum(values, axis=0, keepdims=True)

                for strip in range(lanes // LANE):
                    at = slice(strip * LANE, (strip + 1) * LANE)
                    place = place_refs[index][head, :, at]
                    weighted = gsum_refs[index][head, :, at] * place
                    base = total(weighted)
                    scaled = base / gate_open
                    part_x = total(weighted * key_x) - total(place * key_x) * scaled
                    part_y = total(weighted * key_y) - total(place * key_y) * scaled
                    part_r = total(weighted * radius) - total(place * radius) * scaled
                    part_r -= 2.0 * (query_x[:, at] * part_x + query_y[:, at] * part_y)
                    for row, part in enumerate((part_x, part_y, part_r, gate_ref[head] * base)):
                        pieces[row] += part
            pieces = [jnp.sum(piece, axis=1, keepdims=True) for piece in pieces]
            pieces[3] -= gate_open * gate_ref[head] * jnp.sum(racc_s[head], axis=1, keepdims=True)
            for row in range(4):
                carry = carry + jnp.where(
                    (tile_rows == row) & (tile_lanes == head), pieces[row], 0.0
                )
            return carry

        head_tile = lax.fori_loop(0, heads, head_sums, jnp.zeros((8, LANE), F32))
        first_row = 6 + parts
        small_ref[first_row : first_row + 4, :LANE] = head_tile[:4]
        if started:
            small_ref[...] += small_in[...]


def run_images(xct, sizes, start, shared, previous, units, tile_count):
    bands, _, images, piece, columns = xct.shape
    places, gate_open, matrices, gains, biases, fc1b = shared
    heads = gate_open.shape[0]
    width = matrices[0].shape[1] // 3
    padded = matrices[3].shape[1]
    sels = [jnp.asarray(select_matrix(side, bands), BF16) for side in SIDES]
    selts = [jnp.asarray(select_matrix(side, bands).T, BF16) for side in SIDES]
    sizes_all = [side_sizes(side) for side in SIDES]
    most_rows = max(size[1] for size in sizes_all)
    most_lanes = max(size[2] for size in sizes_all)
    started = previous is not None

    def whole(array):
        rank = len(array.shape)
        return pl.BlockSpec(
            array.shape, lambda i, *_: (0,) * rank, pipeline_mode=pl.Buffered(1)
        )

    image_spec = pl.BlockSpec((bands, 2, 1, piece, columns), lambda i, *_: (0, 0, i, 0, 0))
    out_shapes = [
        jax.ShapeDtypeStruct(xct.shape, BF16),
        jax.ShapeDtypeStruct((tile_count, SUB, LANE), BF16),
        jax.ShapeDtypeStruct((SMALL_ROWS, width), F32),
    ]
    if not started:
        previous = (jnp.zeros((1, SUB, LANE), BF16), jnp.zeros((8, LANE), F32))
    scratch = [
        pltpu.VMEM((most_lanes, 3 * width), BF16),
        pltpu.VMEM((3, width, most_lanes), BF16),
        pltpu.VMEM((most_lanes, width), BF16),
        pltpu.VMEM((width, most_lanes), BF16),
        pltpu.VMEM((heads, most_rows, most_lanes), F32),
        pltpu.VMEM((heads, most_rows, most_lanes), BF16),
        pltpu.VMEM((columns, most_lanes), BF16),
        pltpu.VMEM((3 * columns, most_lanes), BF16),
        pltpu.VMEM((most_rows, padded), BF16),
        pltpu.VMEM((most_rows, padded), BF16),
        pltpu.VMEM((6, 8, columns), F32),
        pltpu.VMEM((8, padded), F32),
        pltpu.VMEM((heads, 1, most_lanes), F32),
        pltpu.VMEM((columns, round_up(3 * columns, LANE)), F32),
        pltpu.VMEM((columns, width), F32),
        pltpu.VMEM((columns, padded), F32),
        pltpu.VMEM((columns, padded), F32),
        [pltpu.VMEM((heads, size[1], size[2]), F32) for size in sizes_all],
        pltpu.VMEM((2, most_rows, most_lanes), F32),
        pltpu.VMEM((2, most_rows, most_lanes), BF16),
        [pltpu.VMEM(place.shape, F32) for place in places],
        [pltpu.VMEM(matrix.shape, BF16) for matrix in matrices],
        pltpu.SemaphoreType.DMA((1 + len(places) + len(matrices),)),
    ]
    smalls = [sels, selts, list(places), list(matrices), gains, biases, fc1b]
    body = functools.partial(image_kernel, columns, heads, units, started)
    hbm = lambda _: pl.BlockSpec(memory_space=pl.ANY)
    specs = [
        hbm(None),
        whole(previous[1]),
        jax.tree.map(whole, sels),
        jax.tree.map(whole, selts),
        [hbm(None) for _ in places],
        [hbm(None) for _ in matrices],
        whole(gains),
        whole(biases),
        whole(fc1b),
    ]
    return pl.pallas_call(
        body,
        grid_spec=pltpu.PrefetchScalarGridSpec(
            num_scalar_prefetch=2,
            grid=(images,),
            in_specs=[image_spec] + specs,
            out_specs=[image_spec] + [whole(shape) for shape in out_shapes[1:]],
            scratch_shapes=scratch,
        ),
        out_shape=out_shapes,
        compiler_params=pltpu.CompilerParams(vmem_limit_bytes=VMEM_LIMIT),
        cost_estimate=pl.CostEstimate(
            flops=images * 8_000_000_000, bytes_accessed=40_000_000, transcendentals=0
        ),
    )(lax.slice_in_dim(sizes, start, start + images), gate_open, xct, *previous, *smalls)


def lane_tiles(columns):
    return [
        (index, low, min(low + LANE, columns))
        for index, low in enumerate(range(0, columns, LANE))
    ]


def pack_kernel(chunks, order_ref, class_ref, x_ref, ct_ref, table_ref, *refs):
    outs, (wide_x, wide_ct) = refs[:-2], refs[-2:]
    band = pl.program_id(0)
    images = sum(chunks)
    rows, count, columns = x_ref.shape

    @pl.when(band == 0)
    def _():
        for source, wide in ((x_ref, wide_x), (ct_ref, wide_ct)):
            for index, low, high in lane_tiles(columns):
                wide[index, :, : high - low] = (
                    source[:, :, low:high].reshape(rows * count, high - low).astype(F32)
                )

    first = 0
    for out, size in zip(outs, chunks):

        def one(index, carry, out=out, first=first):
            place = band * images + first + index
            at = pl.ds(order_ref[place], rows, stride=count)
            select = table_ref[class_ref[place]]
            for which, wide in enumerate((wide_x, wide_ct)):
                for tile, low, high in lane_tiles(columns):
                    taken = dot_nn(select, wide[tile, at, :].astype(BF16)).astype(BF16)
                    out[0, which, index, :, low:high] = taken[:, : high - low]
            return carry

        lax.fori_loop(0, size, one, 0)
        first += size


def pack_images(x, ct, order, classes, bands, chunks):
    rows, count, columns = x.shape
    piece = piece_rows(bands)
    table = jnp.asarray(pack_matrix(bands), BF16)
    whole = lambda a: pl.BlockSpec(a.shape, lambda i, *_: (0, 0, 0), pipeline_mode=pl.Buffered(1))
    return pl.pallas_call(
        functools.partial(pack_kernel, chunks),
        grid_spec=pltpu.PrefetchScalarGridSpec(
            num_scalar_prefetch=2,
            grid=(bands,),
            in_specs=[whole(x), whole(ct), whole(table)],
            out_specs=[
                pl.BlockSpec((1, 2, size, piece, columns), lambda i, *_: (i, 0, 0, 0, 0))
                for size in chunks
            ],
            scratch_shapes=[pltpu.VMEM((round_up(columns, LANE) // LANE, rows * count, LANE), F32)] * 2,
        ),
        out_shape=[
            jax.ShapeDtypeStruct((bands, 2, size, piece, columns), BF16) for size in chunks
        ],
        compiler_params=pltpu.CompilerParams(vmem_limit_bytes=VMEM_LIMIT),
        cost_estimate=pl.CostEstimate(flops=10_000_000, bytes_accessed=14_000_000, transcendentals=0),
    )(order, classes, x, ct, table)


def unpack_kernel(chunks, order_ref, class_ref, table_ref, *refs):
    parts, (out_ref, ig_ref, wide_out, wide_ig) = refs[:-4], refs[-4:]
    band = pl.program_id(0)
    images = sum(chunks)
    rows, count, columns = out_ref.shape
    first = 0
    for part, size in zip(parts, chunks):

        def one(index, carry, part=part, first=first):
            place = band * images + first + index
            at = pl.ds(order_ref[place], rows, stride=count)
            spread = table_ref[class_ref[place]]
            for which, wide in enumerate((wide_out, wide_ig)):
                for tile, low, high in lane_tiles(columns):
                    made = dot_nn(spread, part[0, which, index, :, low:high])
                    if high - low < LANE:
                        fill = jnp.zeros((rows, LANE - (high - low)), F32)
                        made = jnp.concatenate([made, fill], axis=1)
                    wide[tile, at, :] = made
            return carry

        lax.fori_loop(0, size, one, 0)
        first += size

    @pl.when(band == pl.num_programs(0) - 1)
    def _():
        for target, wide in ((out_ref, wide_out), (ig_ref, wide_ig)):
            for tile, low, high in lane_tiles(columns):
                values = wide[tile, :, : high - low].astype(target.dtype)
                target[:, :, low:high] = values.reshape(rows, count, high - low)


def unpack_images(parts, order, classes, chunks, rows):
    bands, _, _, piece, columns = parts[0].shape
    count = bands * sum(chunks)
    table = jnp.asarray(pack_matrix(bands).transpose(0, 2, 1), BF16)
    whole = lambda a: pl.BlockSpec(a.shape, lambda i, *_: (0, 0, 0), pipeline_mode=pl.Buffered(1))
    outs = [
        jax.ShapeDtypeStruct((rows, count, columns), BF16),
        jax.ShapeDtypeStruct((rows, count, columns), F32),
    ]
    return pl.pallas_call(
        functools.partial(unpack_kernel, chunks),
        grid_spec=pltpu.PrefetchScalarGridSpec(
            num_scalar_prefetch=2,
            grid=(bands,),
            in_specs=[whole(table)]
            + [
                pl.BlockSpec((1, 2, size, piece, columns), lambda i, *_: (i, 0, 0, 0, 0))
                for size in chunks
            ],
            out_specs=[whole(shape) for shape in outs],
            scratch_shapes=[pltpu.VMEM((round_up(columns, LANE) // LANE, rows * count, LANE), F32)] * 2,
        ),
        out_shape=outs,
        compiler_params=pltpu.CompilerParams(vmem_limit_bytes=VMEM_LIMIT),
        cost_estimate=pl.CostEstimate(flops=10_000_000, bytes_accessed=16_000_000, transcendentals=0),
    )(order, classes, table, *parts)


def prep_kernel(head_ref, gate_ref, wqkv_in, wout_in, w1_in, w2t_in, *refs):
    wqkv, wback, wout, w1, w2t = refs[:5]
    places = refs[5:]
    columns = wout_in.shape[0]
    width = wout.shape[0]
    heads = head_ref.shape[1]
    wback[...] = wqkv_in[...].astype(BF16)
    for part in range(3):
        low = part * width
        wqkv[:, low : low + columns] = wqkv_in[:, part * columns : (part + 1) * columns].astype(BF16)
        wqkv[:, low + columns : low + width] = jnp.zeros((columns, width - columns), BF16)
    wout[:columns, :] = wout_in[...].astype(BF16)
    wout[columns:, :] = jnp.zeros((width - columns, columns), BF16)
    for out, source in ((w1, w1_in), (w2t, w2t_in)):
        units = source.shape[1]
        out[:, :units] = source[...].astype(BF16)
        out[:, units:] = jnp.zeros((columns, out.shape[1] - units), BF16)

    for side, place in zip(SIDES, places):
        live, rows, lanes = side_sizes(side)

        def spots(axis, rows=rows, lanes=lanes, side=side):
            ids = lax.broadcasted_iota(jnp.int32, (rows, lanes), axis)
            spot = ids.astype(F32)
            row = jnp.floor((spot + 0.5) * (1.0 / side))
            return ids, spot - side * row, row

        key_ids, key_x, key_y = spots(0)
        query_ids, query_x, query_y = spots(1)
        delta_x, delta_y = key_x - query_x, key_y - query_y
        distance = delta_x * delta_x + delta_y * delta_y
        dead_key = key_ids >= live
        inside = (key_ids < live) & (query_ids < live)

        def one(head, carry, place=place):
            scores = head_ref[0, head] * delta_x + head_ref[1, head] * delta_y
            scores = jnp.where(dead_key, MASKED, scores + head_ref[2, head] * distance)
            top = jnp.max(scores, axis=0, keepdims=True)
            raised = jnp.exp(scores - top)
            total = jnp.sum(raised, axis=0, keepdims=True)
            place[head] = jnp.where(inside, raised * (gate_ref[head] / total), 0.0)
            return carry

        lax.fori_loop(0, heads, one, 0)


def prepare(w_qkv, w_out, w_fc1, w_fc2t, head_params, gate_value):
    columns, heads = w_out.shape[0], head_params.shape[1]
    width = round_up(columns, LANE)
    padded = round_up(w_fc1.shape[1], 256)
    vmem = pl.BlockSpec(memory_space=pltpu.VMEM)
    smem = pl.BlockSpec(memory_space=pltpu.SMEM)
    shapes = [
        (columns, 3 * width),
        (columns, 3 * columns),
        (width, columns),
        (columns, padded),
        (columns, padded),
    ]
    outs = [jax.ShapeDtypeStruct(shape, BF16) for shape in shapes]
    outs += [jax.ShapeDtypeStruct((heads,) + side_sizes(side)[1:], F32) for side in SIDES]
    made = pl.pallas_call(
        prep_kernel,
        out_shape=outs,
        in_specs=[smem, smem] + [vmem] * 4,
        out_specs=[vmem] * len(outs),
        compiler_params=pltpu.CompilerParams(vmem_limit_bytes=VMEM_LIMIT),
        cost_estimate=pl.CostEstimate(
            flops=50_000_000, bytes_accessed=22_000_000, transcendentals=2_000_000
        ),
    )(head_params, gate_value, w_qkv, w_out, w_fc1, w_fc2t)
    return made[:5], made[5:]


def reduce_plan(tile_total, devices):
    each = -(-tile_total // devices)
    waves = []
    base = 0
    for wave in range(WAVES):
        share = each // WAVES + (1 if wave < each % WAVES else 0)
        if share:
            waves.append((base, share))
            base += devices * share
    return waves, each * devices


def reduce_kernel(
    waves,
    rank_z,
    own_ref,
    small_ref,
    full_out,
    small_out,
    own,
    full,
    recv0,
    recv1,
    small_own,
    small_recv,
    send_sem,
    recv_sem,
    small_send,
    small_got,
    copy_sem,
):
    img = lax.axis_index("img")
    band = lax.axis_index("band")
    z, y = img // 2, img % 2
    x, c = band // 2, band % 2
    low_z, high_z = z % 2, z // 2
    high_count = rank_z // 2
    mesh_ids = pl.DeviceIdType.MESH
    axes = {
        "c": (c, 2, lambda k: (img, x * 2 + 1 - c)),
        "y": (y, 2, lambda k: (z * 2 + 1 - y, band)),
        "x": (x, 2, lambda k: (img, (1 - x) * 2 + c)),
        "l": (low_z, 2, lambda k: ((high_z * 2 + 1 - low_z) * 2 + y, band)),
        "h": (
            high_z,
            high_count,
            lambda k: ((lax.rem(high_z + k, high_count) * 2 + low_z) * 2 + y, band),
        ),
    }
    order = [name for name in AXIS_ORDER if axes[name][1] > 1]
    partners = [axes[name][2](k) for name in order for k in range(1, axes[name][1])]
    devices = 1
    for name in order:
        devices *= axes[name][1]

    loads = []
    for w, (base, share) in enumerate(waves):
        at = pl.ds(base, devices * share)
        loads.append(pltpu.make_async_copy(own_ref.at[at], own.at[at], copy_sem.at[w]))
        loads[-1].start()
    small_own[...] = small_ref[...]

    barrier = pltpu.get_barrier_semaphore()
    for partner in partners:
        pl.semaphore_signal(barrier, inc=1, device_id=partner, device_id_type=mesh_ids)
    pl.semaphore_wait(barrier, len(partners))

    counters = [0] * len(waves)

    def send(wave, src, dst, target):
        slot = counters[wave]
        counters[wave] += 1
        copy = pltpu.make_async_remote_copy(
            src_ref=src,
            dst_ref=dst,
            send_sem=send_sem.at[wave, slot],
            recv_sem=recv_sem.at[wave, slot],
            device_id=target,
            device_id_type=mesh_ids,
        )
        copy.start()
        return copy

    def add_tiles(dst, dst_at, parts, count, out, out_at):
        block = 8

        def one(offset, size):
            total = dst[pl.ds(dst_at + offset, size)].astype(F32)
            for ref, at in parts:
                total += ref[pl.ds(at + offset, size)].astype(F32)
            out[pl.ds(out_at + offset, size)] = total.astype(BF16)

        if count >= block:

            def step(index, carry):
                one(index * block, block)
                return carry

            lax.fori_loop(0, count // block, step, 0)
        rest = count % block
        if rest:
            one(count - rest, rest)

    stores = []

    def wave_stages(w):
        base, share = waves[w]
        state = {"at": base, "size": devices * share, "copies": [], "parts": []}
        taken = [base // 2]

        def finish():
            for copy in state["copies"]:
                copy.wait()

        def scatter(name):
            def run():
                if state["parts"]:
                    finish()
                    add_tiles(own, state["at"], state["parts"], state["size"], own, state["at"])
                else:
                    loads[w].wait()
                mine, count, target = axes[name]
                size = state["size"] // count
                state["copies"], state["parts"] = [], []
                for k in range(1, count):
                    other = lax.rem(mine + k, count)
                    if name == order[0]:
                        buffer, at = recv0, base // 2
                    else:
                        buffer, at = recv1, taken[0]
                        taken[0] += size
                    state["copies"].append(
                        send(
                            w,
                            own.at[pl.ds(state["at"] + other * size, size)],
                            buffer.at[pl.ds(at, size)],
                            target(k),
                        )
                    )
                    state["parts"].append((buffer, at))
                state["at"] = state["at"] + mine * size
                state["size"] = size

            return run

        def gather(name, first):
            def run():
                finish()
                if first:
                    at = state["at"]
                    add_tiles(own, at, state["parts"], state["size"], full, at)
                mine, count, target = axes[name]
                piece = full.at[pl.ds(state["at"], state["size"])]
                state["copies"] = [send(w, piece, piece, target(k)) for k in range(1, count)]
                state["at"] = state["at"] - mine * state["size"]
                state["size"] = state["size"] * count

            return run

        def close():
            finish()
            at = pl.ds(base, devices * share)
            stores.append(
                pltpu.make_async_copy(full.at[at], full_out.at[at], copy_sem.at[len(waves) + w])
            )
            stores[-1].start()

        steps = [scatter(name) for name in order]
        steps += [gather(name, name == order[-1]) for name in reversed(order)]
        return steps + [close]

    small_slots = [0]
    small_state = {}

    def small_start(name):
        mine, count, target = axes[name]
        first = small_slots[0]
        small_slots[0] += count - 1
        small_state["copies"] = []
        for k in range(1, count):
            slot = first + k - 1
            copy = pltpu.make_async_remote_copy(
                src_ref=small_own,
                dst_ref=small_recv.at[slot],
                send_sem=small_send.at[slot],
                recv_sem=small_got.at[slot],
                device_id=target(k),
                device_id_type=mesh_ids,
            )
            copy.start()
            small_state["copies"].append(copy)
        small_state["first"] = first

    def small_end(name):
        mine, count, _ = axes[name]
        first = small_state["first"]
        for copy in small_state["copies"]:
            copy.wait()
        if count == 2:
            small_own[...] = small_own[...] + small_recv[first]
        else:
            last = small_recv.shape[0] - 1
            small_recv[last] = small_own[...]

            def add_line(index, total):
                k = lax.rem(mine - index + count, count)
                slot = jnp.where(k == 0, last, first + k - 1)
                return total + small_recv[slot]

            small_own[...] = lax.fori_loop(0, count, add_line, jnp.zeros_like(small_own))

    programs = [wave_stages(w) for w in range(len(waves))]
    depth = len(programs[0])
    for time in range(max(depth + len(waves) - 1, len(order) + 2)):
        for w in range(len(waves)):
            if 0 <= time - w < depth:
                programs[w][time - w]()
        if 1 <= time <= len(order) + 1:
            if time > 1:
                small_end(order[time - 2])
            if time <= len(order):
                small_start(order[time - 1])
    small_out[...] = small_own[...]
    for store in stores:
        store.wait()


def reduce_all(tiles, small, waves, img_count):
    total = tiles.shape[0]
    rank_z = img_count // 2
    copies = 2 * (4 + max(rank_z // 2 - 1, 0))
    hops = 4 + max(rank_z // 2 - 1, 0)
    return pl.pallas_call(
        functools.partial(reduce_kernel, waves, rank_z),
        out_shape=[
            jax.ShapeDtypeStruct(tiles.shape, BF16),
            jax.ShapeDtypeStruct(small.shape, F32),
        ],
        in_specs=[pl.BlockSpec(memory_space=pl.ANY), pl.BlockSpec(memory_space=pltpu.VMEM)],
        out_specs=[pl.BlockSpec(memory_space=pl.ANY), pl.BlockSpec(memory_space=pltpu.VMEM)],
        scratch_shapes=[
            pltpu.VMEM(tiles.shape, BF16),
            pltpu.VMEM(tiles.shape, BF16),
            pltpu.VMEM((total // 2, SUB, LANE), BF16),
            pltpu.VMEM((total // 2, SUB, LANE), BF16),
            pltpu.VMEM(small.shape, F32),
            pltpu.VMEM((hops + 1,) + small.shape, F32),
            pltpu.SemaphoreType.DMA((len(waves), copies)),
            pltpu.SemaphoreType.DMA((len(waves), copies)),
            pltpu.SemaphoreType.DMA((hops,)),
            pltpu.SemaphoreType.DMA((hops,)),
            pltpu.SemaphoreType.DMA((2 * len(waves),)),
        ],
        compiler_params=pltpu.CompilerParams(
            collective_id=1, has_side_effects=True, vmem_limit_bytes=VMEM_LIMIT
        ),
        cost_estimate=pl.CostEstimate(
            flops=10_000_000, bytes_accessed=200_000_000, transcendentals=0
        ),
    )(tiles, small)


def update_kernel(
    decay_rate,
    head_count,
    widths,
    tiles_ref,
    small_ref,
    weight_hbm,
    line_refs,
    vector_refs,
    moment_refs,
    norm_out,
    grad_hbm,
    new_hbm,
    vgrad_outs,
    vnew_outs,
    line_outs,
    moment_outs,
    weights,
    grads,
    news,
    row_s,
    col_s,
    copy_sem,
):
    columns = weights[0].shape[0]
    row_tiles = columns // SUB
    spans = [-(-wide // LANE) for wide in widths]
    total_span = tiles_stride(widths)
    starts = []
    at = 0
    for wide in widths:
        starts.append(at)
        at += tile_span(wide)
    loads = [
        pltpu.make_async_copy(weight_hbm[i], weights[i], copy_sem.at[i]) for i in range(4)
    ]
    for load in loads:
        load.start()

    def tile_rows(index, which):
        place = index * total_span + starts[which]
        pieces = [tiles_ref[place + col].astype(F32) for col in range(spans[which])]
        whole = jnp.concatenate(pieces, axis=1) if len(pieces) > 1 else pieces[0]
        return whole[:, : widths[which]]

    def all_sum(values):
        return jnp.sum(jnp.sum(values, axis=0, keepdims=True), axis=1, keepdims=True)

    def measure(index, carry):
        at = pl.ds(pl.multiple_of(index * SUB, SUB), SUB)
        made = []
        for which in range(4):
            grad = tile_rows(index, which)
            square = grad * grad
            row_s[which, at, :] = jnp.sum(square, axis=1, keepdims=True)
            made.append(carry[which] + fold_rows(square))
        return tuple(made)

    zeros = tuple(jnp.zeros((8, wide), F32) for wide in widths)
    folded = lax.fori_loop(0, row_tiles, measure, zeros)
    col_squares = [jnp.sum(fold, axis=0, keepdims=True) for fold in folded]
    total = jnp.zeros((1, 1), F32)
    for square in col_squares:
        total += jnp.sum(square, axis=1, keepdims=True)

    parts = vector_refs[2].shape[0]
    places = (
        (slice(0, 2), columns),
        (slice(2, 6), columns),
        (slice(6, 6 + parts), columns),
        (slice(6 + parts, 10 + parts), head_count),
    )
    vectors = [small_ref[rows, :wide] for rows, wide in places]
    for grad in vectors:
        total += all_sum(grad * grad)
    norm = jnp.sqrt(total)
    norm_out[...] = norm
    factor = 1.0 / jnp.maximum(norm, 1.0)

    for index in range(4):
        grad = vectors[index] * factor
        weight = vector_refs[index][...]
        moment = decay_rate * moment_refs[index][...] + (1.0 - decay_rate) * (
            grad * grad + FLOOR_ONE
        )
        update = grad * lax.rsqrt(moment)
        size = weight.shape[0] * weight.shape[1]
        mean_square = all_sum(update * update) / size
        update = update / jnp.maximum(1.0, jnp.sqrt(mean_square) / CLIP_RMS)
        scale = STEP_RATE * jnp.maximum(FLOOR_TWO, jnp.sqrt(all_sum(weight * weight) / size))
        vgrad_outs[index][...] = grad
        vnew_outs[index][...] = weight - scale * update
        moment_outs[index][...] = moment

    row_factors, col_factors = [], []
    for which in range(4):
        wide = widths[which]
        down_old, along_old = line_refs[which]
        down_out, along_out = line_outs[which]
        down = jnp.broadcast_to(down_old[...], (LANE, columns)).T
        down = decay_rate * down + (1.0 - decay_rate) * (
            row_s[which] * (factor * factor) / wide + FLOOR_ONE
        )
        along = decay_rate * along_old[...] + (1.0 - decay_rate) * (
            col_squares[which] * (factor * factor) / columns + FLOOR_ONE
        )
        down_out[...] = down.T[:1, :]
        along_out[...] = along
        down = down[:, :1]
        if which == 3:
            along = along / (jnp.sum(along, axis=1, keepdims=True) / wide)
        else:
            down = down / (jnp.sum(down, axis=0, keepdims=True) / columns)
        row_s[which] = lax.rsqrt(down) * factor
        col_s[which, :, :wide] = lax.rsqrt(along)

    for load in loads:
        load.wait()

    def scan(index, carry):
        at = pl.ds(pl.multiple_of(index * SUB, SUB), SUB)
        made = []
        for which in range(4):
            wide = widths[which]
            update = tile_rows(index, which) * col_s[which, :, :wide] * row_s[which, at, :]
            weight = weights[which][at, :]
            made.append(carry[2 * which] + fold_rows(update * update))
            made.append(carry[2 * which + 1] + fold_rows(weight * weight))
        return tuple(made)

    sums = lax.fori_loop(0, row_tiles, scan, tuple(z for z in zeros for _ in range(2)))
    stores = []
    for which in (2, 3, 0, 1):
        wide = widths[which]
        size = columns * wide
        scale = STEP_RATE * jnp.maximum(FLOOR_TWO, jnp.sqrt(all_sum(sums[2 * which + 1]) / size))
        scale = scale / jnp.maximum(1.0, jnp.sqrt(all_sum(sums[2 * which]) / size) / CLIP_RMS)
        col_factor = col_s[which, :, :wide] * scale

        def write(index, carry, which=which, col_factor=col_factor):
            at = pl.ds(pl.multiple_of(index * SUB, SUB), SUB)
            grad = tile_rows(index, which)
            grads[which][at, :] = grad * factor
            news[which][at, :] = weights[which][at, :] - grad * col_factor * row_s[which, at, :]
            return carry

        lax.fori_loop(0, row_tiles, write, 0)
        for source, target, slot in (
            (grads[which], grad_hbm[which], 4 + which),
            (news[which], new_hbm[which], 8 + which),
        ):
            stores.append(pltpu.make_async_copy(source, target, copy_sem.at[slot]))
            stores[-1].start()
    for store in stores:
        store.wait()


def tile_span(wide):
    return round_up(wide, 256 if wide > 1500 else LANE) // LANE


def tiles_stride(widths):
    return sum(tile_span(wide) for wide in widths)


def update_all(tiles, small, weights, rows, cols, vectors, moments, decay_rate):
    columns = weights[1].shape[0]
    head_count = vectors[3].shape[1]
    units = weights[2].shape[1]
    parts = units // columns
    flat = lambda v: v.reshape(1, -1)
    lines = [[flat(r), flat(c)] for r, c in zip(rows, cols)]
    lines[3] = lines[3][::-1]
    vectors = [v.reshape(parts, columns) if v.ndim == 1 else v for v in vectors]
    moments = [v.reshape(parts, columns) if v.ndim == 1 else v for v in moments]
    widths = [weight.shape[1] for weight in weights]
    like = lambda group: [jax.ShapeDtypeStruct(v.shape, F32) for v in group]
    outs = [
        jax.ShapeDtypeStruct((1, 1), F32),
        like(weights),
        like(weights),
        like(vectors),
        like(vectors),
        [like(pair) for pair in lines],
        like(vectors),
    ]
    vmem = pl.BlockSpec(memory_space=pltpu.VMEM)
    hbm = pl.BlockSpec(memory_space=pl.ANY)
    args = (tiles, small, list(weights), lines, vectors, moments)
    in_specs = list(jax.tree.map(lambda _: vmem, args))
    in_specs[2] = [hbm] * 4
    out_specs = jax.tree.map(lambda _: vmem, outs)
    out_specs[1] = [hbm] * 4
    out_specs[2] = [hbm] * 4
    full = lambda: [pltpu.VMEM(weight.shape, F32) for weight in weights]
    scratch = [
        full(),
        full(),
        full(),
        pltpu.VMEM((4, columns, 1), F32),
        pltpu.VMEM((4, 1, round_up(max(widths), LANE)), F32),
        pltpu.SemaphoreType.DMA((12,)),
    ]
    made = pl.pallas_call(
        functools.partial(update_kernel, decay_rate, head_count, widths),
        out_shape=outs,
        in_specs=in_specs,
        out_specs=out_specs,
        scratch_shapes=scratch,
        compiler_params=pltpu.CompilerParams(vmem_limit_bytes=VMEM_LIMIT),
    )(*args)
    norm, grads, news, vgrads, vnews, line_new, moment_new = made
    spread = lambda group: [v.reshape(-1) if i == 2 else v for i, v in enumerate(group)]
    line_new[3] = line_new[3][::-1]
    moved = [line.reshape(-1) for pair in line_new for line in pair]
    grads[3], news[3] = grads[3].T, news[3].T
    return (
        norm.reshape(1),
        *grads,
        *spread(vgrads),
        *news,
        *spread(vnews),
        *moved,
        *spread(moment_new),
    )


def deal_images(grid_sizes, devices):
    count = grid_sizes.shape[0]
    ids = jnp.arange(count, dtype=jnp.int32)
    ahead = (grid_sizes[None, :] > grid_sizes[:, None]) | (
        (grid_sizes[None, :] == grid_sizes[:, None]) & (ids[None, :] < ids[:, None])
    )
    rank = jnp.sum(ahead.astype(jnp.int32), axis=1)
    turn = rank // devices
    seat = rank % devices
    seat = jnp.where(turn % 2 == 0, seat, devices - 1 - seat)
    place = seat * (count // devices) + turn
    hit = place[None, :] == ids[:, None]
    order = jnp.sum(jnp.where(hit, ids[None, :], 0), axis=1)
    sizes = jnp.sum(jnp.where(hit, grid_sizes[None, :], 0), axis=1)
    return order, sizes


def per_device(
    inputs,
    cotangent,
    grid_sizes,
    w_qkv,
    w_out,
    w_fc1,
    w_fc2,
    norm_gains,
    biases,
    fc1_bias,
    head_params,
    rows_qkv,
    cols_qkv,
    rows_out,
    cols_out,
    rows_fc1,
    cols_fc1,
    rows_fc2,
    cols_fc2,
    gain_moment,
    bias_moment,
    fc1_bias_moment,
    head_moment,
):
    band_count = lax.axis_size("band")
    img_count = lax.axis_size("img")
    band_index = lax.axis_index("band")
    columns = inputs.shape[2]
    units = w_fc1.shape[1]
    per_band = inputs.shape[0] // band_count
    order, sizes_ordered = deal_images(grid_sizes, band_count)
    classes = sum(
        (jnp.where(sizes_ordered == side, index, 0) for index, side in enumerate(SIDES)),
        jnp.zeros_like(order),
    )
    sizes_used = lax.dynamic_slice_in_dim(sizes_ordered, band_index * per_band, per_band)
    early = max(1, per_band * 3 // 8)
    chunks = (early, per_band - early)
    packed = pack_images(
        jnp.swapaxes(inputs, 0, 1),
        jnp.swapaxes(cotangent, 0, 1),
        order,
        classes,
        band_count,
        chunks,
    )
    moved = [lax.all_to_all(part, "band", split_axis=0, concat_axis=0, tiled=True) for part in packed]
    waves, tile_count = reduce_plan(
        (columns // SUB) * tiles_stride((3 * columns, columns, units, units)),
        band_count * img_count,
    )
    w_fc2t = w_fc2.T
    gate_value = jax.nn.sigmoid(head_params[3])
    matrices, places = prepare(w_qkv, w_out, w_fc1, w_fc2t, head_params, gate_value)
    fc1b = jnp.pad(fc1_bias[None, :], ((0, 0), (0, matrices[3].shape[1] - units)))
    shared = (places, 1.0 - gate_value, matrices, norm_gains, biases, fc1b)
    previous = None
    start = 0
    results = []
    for part, size in zip(moved, chunks):
        result, *previous = run_images(part, sizes_used, start, shared, previous, units, tile_count)
        results.append(lax.all_to_all(result, "band", split_axis=0, concat_axis=0, tiled=True))
        start += size
    tiles, small = previous
    full, small = reduce_all(tiles, small, waves, img_count)
    updated = update_all(
        full,
        small,
        (w_qkv, w_out, w_fc1, w_fc2t),
        (rows_qkv, rows_out, rows_fc1, rows_fc2),
        (cols_qkv, cols_out, cols_fc1, cols_fc2),
        (norm_gains, biases, fc1_bias, head_params),
        (gain_moment, bias_moment, fc1_bias_moment, head_moment),
        1.0 - STEP ** (-0.8),
    )
    output, input_grad = unpack_images(results, order, classes, chunks, inputs.shape[1])
    return (jnp.swapaxes(output, 0, 1), jnp.swapaxes(input_grad, 0, 1), *updated)


def solution(mesh):
    split = P("img", "band", None)
    return jax.shard_map(
        per_device,
        mesh=mesh,
        in_specs=(split, split, P("img")) + (P(),) * 20,
        out_specs=(split, split) + (P(),) * 29,
        check_vma=False,
    )
```

```python
import functools
import math

import jax
import jax.numpy as jnp
import numpy as np
from jax import lax
from jax.experimental import pallas as pl
from jax.experimental.pallas import tpu as pltpu
from jax.sharding import PartitionSpec as P

GRID = 20
STEP = 10
SIDES = (18, 14, 10)

NORM_FLOOR = 1e-06
FLOOR_ONE = 1e-30
FLOOR_TWO = 0.001
STEP_RATE = 0.6
CLIP_RMS = 1.0
MASKED = -1e30

BF16 = jnp.bfloat16
F32 = jnp.float32
VMEM_LIMIT = 60 * 1024 * 1024
SUB = 16
SMALL_ROWS = 16
WAVES = (
    ("cyxlh", 7, 0),
    ("cxylh", 7, 0),
    ("clhxy", 4, 0),
    ("cyxlh", 7, 1),
    ("cxylh", 7, 1),
    ("clhxy", 5, 1),
)
LANE = 128


def round_up(value, unit):
    return (value + unit - 1) // unit * unit


def side_sizes(side):
    live = side * side
    return live, round_up(live, SUB), round_up(live, LANE)


def dot_nn(left, right):
    return lax.dot_general(left, right, (((1,), (0,)), ((), ())), preferred_element_type=F32)


def dot_nt(left, right):
    return lax.dot_general(left, right, (((1,), (1,)), ((), ())), preferred_element_type=F32)


def piece_rows(bands):
    return round_up(GRID // bands * max(SIDES), SUB)


def select_matrix(side, bands):
    live, rows, _ = side_sizes(side)
    tall, piece = GRID // bands, piece_rows(bands)
    made = np.zeros((rows, bands * piece), np.float32)
    for row in range(side):
        for col in range(side):
            at = row // tall * piece + (row % tall) * side + col
            made[row * side + col, at] = 1.0
    return made


def select_matrices(side, bands):
    made = select_matrix(side, bands).reshape(-1, bands, piece_rows(bands))
    ordered = [made[:, [own ^ step for step in range(bands)]] for own in range(bands)]
    return np.stack(ordered).reshape(bands, made.shape[0], -1)


def pack_matrix(bands):
    tall, piece = GRID // bands, piece_rows(bands)
    made = np.zeros((len(SIDES), piece, tall * GRID), np.float32)
    for index, side in enumerate(SIDES):
        for row in range(tall):
            for col in range(side):
                made[index, row * side + col, row * GRID + col] = 1.0
    return made


def fold_rows(values):
    rows, columns = values.shape
    return jnp.sum(values.reshape(rows // 8, 8, columns), axis=0)


def image_kernel(
    columns,
    heads,
    hidden_units,
    image_count,
    started,
    sizes_ref,
    band_ref,
    gate_ref,
    xct_refs,
    tiles_in,
    small_in,
    sel_refs,
    selt_refs,
    place_hbm,
    moment_refs,
    weight_hbm,
    gains_ref,
    biases_ref,
    fc1b_ref,
    outig_refs,
    tiles_ref,
    small_ref,
    proj_s,
    projt_s,
    da_s,
    dat_s,
    cont_s,
    mix_s,
    attt_s,
    gt_s,
    act_s,
    gb_s,
    vec_s,
    fc1g_s,
    racc_s,
    gqkv_ref,
    gout_ref,
    g1_ref,
    g2t_ref,
    gsum_refs,
    gm_s,
    gc_s,
    place_refs,
    weight_refs,
    copy_sem,
):
    wqkv_ref, wback_ref, wout_ref, w1_ref, w2t_ref = weight_refs
    step = pl.program_id(0)
    steps = pl.num_programs(0)
    head_size = columns // heads
    width = wqkv_ref.shape[1] // 3
    window = 256
    score_scale = head_size ** (-0.5)
    chunk = 256
    chunks = w1_ref.shape[1] // chunk

    table = (gqkv_ref, gout_ref, g1_ref, g2t_ref)
    across = sum(ref.shape[1] // LANE for ref in table)
    row_tiles = columns // SUB

    sources = list(weight_hbm) + list(place_hbm)
    targets = list(weight_refs) + list(place_refs)
    loads = [
        pltpu.make_async_copy(source, target, copy_sem.at[1 + index])
        for index, (source, target) in enumerate(zip(sources, targets))
    ]
    load_qkv, load_back, load_out, load_w1, load_w2 = loads[:5]
    load_places = loads[5:]

    def once(*copies):
        @pl.when(step == 0)
        def _():
            for copy in copies:
                copy.wait()

    @pl.when(step == 0)
    def _():
        if started:
            load = pltpu.make_async_copy(tiles_in, tiles_ref, copy_sem.at[0])
            load.start()
        for copy in [load_qkv] + load_places + [load_out, load_w1, load_w2, load_back]:
            copy.start()
        if started:
            load.wait()

            def absorb(index, carry):
                at = pl.ds(pl.multiple_of(index * SUB, SUB), SUB)
                place = index * across
                for ref in table:
                    for col in range(ref.shape[1] // LANE):
                        ref[at, col * LANE : (col + 1) * LANE] = tiles_ref[place].astype(F32)
                        place = place + 1
                return carry

            lax.fori_loop(0, row_tiles, absorb, 0)
        else:
            for ref in table:
                ref[...] = jnp.zeros_like(ref)
        vec_s[...] = jnp.zeros_like(vec_s)
        fc1g_s[...] = jnp.zeros_like(fc1g_s)
        racc_s[...] = jnp.zeros_like(racc_s)
        for ref in gsum_refs:
            ref[...] = jnp.zeros_like(ref)

    def head_place(head):
        first_lane = head * head_size
        start = min(first_lane // LANE * LANE, width - window)
        lanes = lax.broadcasted_iota(jnp.int32, (1, window), 1) + start
        mask = (lanes >= first_lane) & (lanes < first_lane + head_size)
        return start, mask, first_lane

    def skewed(*stages):
        for index in range(heads + len(stages) - 1):
            for late, stage in enumerate(stages):
                if 0 <= index - late < heads:
                    stage(index - late)

    def image(side, sel_ref, selt_ref, place_ref, gsum_ref):
        live, rows, lanes = side_sizes(side)
        edge = live // 8 * 8
        tall = outig_refs[0].shape[2]

        def gathered(which):
            pieces = jnp.concatenate([ref[which, 0] for ref in xct_refs], axis=0)
            return dot_nn(sel_ref[0], pieces)

        def spread(which, values):
            values = dot_nn(selt_ref[0], values.astype(BF16)).astype(BF16)
            for index, ref in enumerate(outig_refs):
                ref[which, 0] = values[index * tall : (index + 1) * tall]

        def norm(values):
            averaged = jnp.mean(values, axis=-1, keepdims=True)
            centered = values - averaged
            variance = jnp.mean(centered * centered, axis=-1, keepdims=True)
            inverse = lax.rsqrt(variance + NORM_FLOOR)
            return centered * inverse, inverse

        def norm_back(grad, unit, inverse, gain):
            scaled = grad * gain
            first_mean = jnp.mean(scaled, axis=-1, keepdims=True)
            second_mean = jnp.mean(scaled * unit, axis=-1, keepdims=True)
            return inverse * (scaled - first_mean - unit * second_mean)

        x = gathered(0)
        unit_one, inverse_one = norm(x)
        first_b = (unit_one * gains_ref[0:1, :] + biases_ref[0:1, :]).astype(BF16)
        once(load_qkv)
        proj_s[:rows, :] = dot_nn(first_b, wqkv_ref[...]).astype(BF16)
        once(*load_places)
        if lanes > rows:
            proj_s[rows:lanes, :] = jnp.zeros((lanes - rows, 3 * width), BF16)
        for part in range(3):
            piece = proj_s[:lanes, part * width : (part + 1) * width]
            projt_s[part, :, :lanes] = piece.T

        def score_head(head):
            start, mask, row = head_place(head)
            query = jnp.where(mask, proj_s[:lanes, start : start + window], 0)
            key = proj_s[:rows, width + start : width + start + window]
            cont_s[head, :rows, :lanes] = dot_nt(key, query)

        def soft_head(head):
            score = cont_s[head, :rows, :lanes] * (score_scale * math.log2(math.e))
            tail = lax.broadcasted_iota(jnp.int32, (rows - edge, lanes), 0) < live - edge
            score = jnp.concatenate(
                [score[:edge], jnp.where(tail, score[edge:], MASKED)], axis=0
            )
            top = jnp.max(score, axis=0, keepdims=True)
            raised = jnp.exp2(score - top)
            total = jnp.sum(raised, axis=0, keepdims=True)
            content = raised * (gate_ref[head] / total)
            cont_s[head, :rows, :lanes] = content
            mix_s[head, :rows, :lanes] = (content + place_ref[head]).astype(BF16)

        def attend_head(head):
            row = head * head_size
            value_t = projt_s[2, row : row + head_size, :rows]
            mixed = mix_s[head, :rows, :lanes]
            attt_s[row : row + head_size, :lanes] = dot_nn(value_t, mixed).astype(BF16)

        skewed(score_head, soft_head, attend_head)

        once(load_out, load_w1, load_w2, load_back)
        attended = attt_s[:, :lanes].T[:rows]
        hidden = x + (dot_nn(attended, wout_ref[:columns, :]) + biases_ref[2:3, :])
        unit_two, inverse_two = norm(hidden)
        second_b = (unit_two * gains_ref[1:2, :] + biases_ref[1:2, :]).astype(BF16)
        ct_b = gathered(1).astype(BF16)

        for index in range(chunks):
            at = slice(index * chunk, (index + 1) * chunk)
            before = dot_nn(second_b, w1_ref[:, at]) + fc1b_ref[:, at]
            grad_act = dot_nn(ct_b, w2t_ref[:, at])
            square = before * before
            inner = before * (
                math.sqrt(2.0 / math.pi) + (math.sqrt(2.0 / math.pi) * 0.044715) * square
            )
            half = 0.5 * jnp.tanh(inner) + 0.5
            activated = before * half
            slope = half + activated * (1.0 - half) * (
                2.0 * math.sqrt(2.0 / math.pi)
                + (6.0 * math.sqrt(2.0 / math.pi) * 0.044715) * square
            )
            act_s[:rows, at] = activated.astype(BF16)
            grad_b = (grad_act * slope).astype(BF16)
            gb_s[:rows, at] = grad_b
            fc1g_s[:, at] += fold_rows(grad_b.astype(F32))

        result = (
            hidden + dot_nt(act_s[:rows, :], w2t_ref[...]) + biases_ref[3:4, :]
        )
        spread(0, result)

        ct_t = ct_b.T
        second_t = second_b.T
        units = hidden_units
        for index in range(chunks):
            low, high = index * chunk, min((index + 1) * chunk, units)
            g1_ref[:, low:high] += dot_nn(second_t, gb_s[:rows, low:high])
            g2t_ref[:, low:high] += dot_nn(ct_t, act_s[:rows, low:high])

        ct_f = ct_b.astype(F32)
        grad_second = dot_nt(gb_s[:rows, :], w1_ref[...])
        grad_hidden = ct_f + norm_back(grad_second, unit_two, inverse_two, gains_ref[1:2, :])
        branch_b = grad_hidden.astype(BF16)
        vec_s[1] += fold_rows(grad_second * unit_two)
        vec_s[3] += fold_rows(grad_second)
        vec_s[4] += fold_rows(branch_b.astype(F32))
        vec_s[5] += fold_rows(ct_f)
        gout_ref[:, :columns] += dot_nn(attt_s[:, :rows], branch_b)
        da_s[:rows, :] = dot_nt(branch_b, wout_ref[...]).astype(BF16)
        if lanes > rows:
            da_s[rows:lanes, :] = jnp.zeros((lanes - rows, width), BF16)
        dat_s[:, :lanes] = da_s[:lanes, :].T

        def grad_head(head):
            start, mask, row = head_place(head)
            grad_att = jnp.where(mask, da_s[:lanes, start : start + window], 0)
            value = proj_s[:rows, 2 * width + start : 2 * width + start + window]
            gm_s[head % 2, :rows, :lanes] = dot_nt(value, grad_att)

        def soft_back_head(head):
            grad_mixed = gm_s[head % 2, :rows, :lanes]
            gsum_ref[head] += grad_mixed
            content = cont_s[head, :rows, :lanes]
            product = grad_mixed * content
            total = jnp.sum(product, axis=0, keepdims=True) / gate_ref[head]
            racc_s[SIDES.index(side), head, :, :lanes] += total
            gc_s[head % 2, :rows, :lanes] = (product - content * total).astype(BF16)

        def back_head(head):
            row = head * head_size
            here = slice(row, row + head_size)
            mixed = mix_s[head, :rows, :lanes]
            grad_content = gc_s[head % 2, :rows, :lanes]
            gt_s[2 * columns + row : 2 * columns + row + head_size, :rows] = dot_nt(
                dat_s[here, :lanes], mixed
            ).astype(BF16)
            gt_s[columns + row : columns + row + head_size, :rows] = (
                dot_nt(projt_s[0, here, :lanes], grad_content) * score_scale
            ).astype(BF16)
            gt_s[here, :lanes] = (
                dot_nn(projt_s[1, here, :rows], grad_content) * score_scale
            ).astype(BF16)

        skewed(grad_head, soft_back_head, back_head)

        first_t = first_b.T
        grad_proj = gt_s[:, :lanes].T[:rows]
        gqkv_ref[:, : 3 * columns] += dot_nn(first_t, grad_proj)
        grad_first = dot_nt(grad_proj, wback_ref[...])
        vec_s[0] += fold_rows(grad_first * unit_one)
        vec_s[2] += fold_rows(grad_first)
        input_grad = grad_hidden + norm_back(grad_first, unit_one, inverse_one, gains_ref[0:1, :])
        spread(1, input_grad)

    for index, side in enumerate(SIDES):

        @pl.when(sizes_ref[step] == side)
        def _(index=index, side=side):
            image(side, sel_refs[index], selt_refs[index], place_refs[index], gsum_refs[index])

    @pl.when(step == steps - 1)
    def _():
        def emit(index, carry):
            at = pl.ds(pl.multiple_of(index * SUB, SUB), SUB)
            place = index * across
            for ref in table:
                for col in range(ref.shape[1] // LANE):
                    tiles_ref[place] = ref[at, col * LANE : (col + 1) * LANE].astype(BF16)
                    place = place + 1
            return carry

        lax.fori_loop(0, row_tiles, emit, 0)
        for spare in range(row_tiles * across, tiles_ref.shape[0]):
            tiles_ref[spare] = jnp.zeros((SUB, LANE), BF16)

        small_ref[...] = jnp.zeros_like(small_ref)
        for row in range(6):
            small_ref[row : row + 1, :columns] = jnp.sum(vec_s[row], axis=0, keepdims=True)
        fc1_row = jnp.sum(fc1g_s[...], axis=0, keepdims=True)
        parts = hidden_units // columns
        for part in range(parts):
            small_ref[6 + part : 7 + part, :columns] = fc1_row[
                :, part * columns : (part + 1) * columns
            ]

        tile_rows = lax.broadcasted_iota(jnp.int32, (8, LANE), 0)
        tile_lanes = lax.broadcasted_iota(jnp.int32, (8, LANE), 1)
        grids = []
        for side in SIDES:
            rows, lanes = side_sizes(side)[1:]
            middle = 0.5 * (side - 1)
            key_ids = lax.broadcasted_iota(jnp.int32, (rows, LANE), 0).astype(F32)
            key_row = jnp.floor((key_ids + 0.5) * (1.0 / side))
            key_x, key_y = key_ids - side * key_row - middle, key_row - middle
            query_ids = lax.broadcasted_iota(jnp.int32, (1, lanes), 1).astype(F32)
            query_row = jnp.floor((query_ids + 0.5) * (1.0 / side))
            query_x, query_y = query_ids - side * query_row - middle, query_row - middle
            grids.append((key_x, key_y, key_x * key_x + key_y * key_y, query_x, query_y))

        def head_sums(index, head, carry):
            pieces = [jnp.zeros((1, LANE), F32) for _ in range(4)]
            gate_open = 1.0 - gate_ref[head]
            lanes = side_sizes(SIDES[index])[2]
            key_x, key_y, radius, query_x, query_y = grids[index]

            def total(values):
                return jnp.sum(values, axis=0, keepdims=True)

            for strip in range(lanes // LANE):
                at = slice(strip * LANE, (strip + 1) * LANE)
                weighted = gsum_refs[index][head, :, at] * place_refs[index][head, :, at]
                base = total(weighted)
                scaled = base / gate_open
                mean_x, mean_y, mean_r = (
                    moment_refs[index][head, row : row + 1, at] for row in range(3)
                )
                part_x = total(weighted * key_x) - mean_x * scaled
                part_y = total(weighted * key_y) - mean_y * scaled
                part_r = total(weighted * radius) - mean_r * scaled
                part_r -= 2.0 * (query_x[:, at] * part_x + query_y[:, at] * part_y)
                for row, part in enumerate((part_x, part_y, part_r, gate_ref[head] * base)):
                    pieces[row] += part
            pieces = [jnp.sum(piece, axis=1, keepdims=True) for piece in pieces]
            rests = jnp.sum(racc_s[index, head], axis=1, keepdims=True)
            pieces[3] -= gate_open * gate_ref[head] * rests
            for row in range(4):
                carry = carry + jnp.where(
                    (tile_rows == row) & (tile_lanes == head), pieces[row], 0.0
                )
            return carry

        first_row = 6 + parts
        for index, side in enumerate(SIDES):
            present = sizes_ref[0] == side
            for place in range(1, image_count):
                present = present | (sizes_ref[place] == side)
            @pl.when(present)
            def _(index=index):
                head_tile = lax.fori_loop(
                    0,
                    heads,
                    functools.partial(head_sums, index),
                    jnp.zeros((8, LANE), F32),
                )
                small_ref[first_row : first_row + 4, :LANE] += head_tile[:4]

        if started:
            small_ref[...] += small_in[...]


def run_images(xct, sizes, start, band, shared, previous, units, tile_count):
    bands = len(xct)
    _, images, piece, columns = xct[0].shape
    places, moments, gate_open, matrices, gains, biases, fc1b = shared
    heads = gate_open.shape[0]
    width = matrices[0].shape[1] // 3
    padded = matrices[3].shape[1]
    chosen = [select_matrices(side, bands) for side in SIDES]
    sels = [jnp.asarray(made, BF16) for made in chosen]
    selts = [jnp.asarray(made.transpose(0, 2, 1), BF16) for made in chosen]
    sizes_all = [side_sizes(side) for side in SIDES]
    most_rows = max(size[1] for size in sizes_all)
    most_lanes = max(size[2] for size in sizes_all)
    started = previous is not None

    def whole(array):
        rank = len(array.shape)
        return pl.BlockSpec(
            array.shape, lambda i, *_: (0,) * rank, pipeline_mode=pl.Buffered(1)
        )

    def own(array):
        return pl.BlockSpec(
            (1,) + array.shape[1:],
            lambda i, sizes, band, *_: (band[0], 0, 0),
            pipeline_mode=pl.Buffered(1),
        )

    image_specs = [pl.BlockSpec((2, 1, piece, columns), lambda i, *_: (0, i, 0, 0))] * bands
    out_shapes = [
        [jax.ShapeDtypeStruct(part.shape, BF16) for part in xct],
        jax.ShapeDtypeStruct((tile_count, SUB, LANE), BF16),
        jax.ShapeDtypeStruct((SMALL_ROWS, width), F32),
    ]
    if not started:
        previous = (jnp.zeros((1, SUB, LANE), BF16), jnp.zeros((8, LANE), F32))
    scratch = [
        pltpu.VMEM((most_lanes, 3 * width), BF16),
        pltpu.VMEM((3, width, most_lanes), BF16),
        pltpu.VMEM((most_lanes, width), BF16),
        pltpu.VMEM((width, most_lanes), BF16),
        pltpu.VMEM((heads, most_rows, most_lanes), F32),
        pltpu.VMEM((heads, most_rows, most_lanes), BF16),
        pltpu.VMEM((columns, most_lanes), BF16),
        pltpu.VMEM((3 * columns, most_lanes), BF16),
        pltpu.VMEM((most_rows, padded), BF16),
        pltpu.VMEM((most_rows, padded), BF16),
        pltpu.VMEM((6, 8, columns), F32),
        pltpu.VMEM((8, padded), F32),
        pltpu.VMEM((len(SIDES), heads, 1, most_lanes), F32),
        pltpu.VMEM((columns, round_up(3 * columns, LANE)), F32),
        pltpu.VMEM((columns, width), F32),
        pltpu.VMEM((columns, padded), F32),
        pltpu.VMEM((columns, padded), F32),
        [pltpu.VMEM((heads, size[1], size[2]), F32) for size in sizes_all],
        pltpu.VMEM((2, most_rows, most_lanes), F32),
        pltpu.VMEM((2, most_rows, most_lanes), BF16),
        [pltpu.VMEM(place.shape, F32) for place in places],
        [pltpu.VMEM(matrix.shape, BF16) for matrix in matrices],
        pltpu.SemaphoreType.DMA((1 + len(places) + len(matrices),)),
    ]
    smalls = [sels, selts, list(places), list(moments), list(matrices), gains, biases, fc1b]
    body = functools.partial(image_kernel, columns, heads, units, images, started)
    hbm = lambda _: pl.BlockSpec(memory_space=pl.ANY)
    specs = [
        hbm(None),
        whole(previous[1]),
        jax.tree.map(own, sels),
        jax.tree.map(own, selts),
        [hbm(None) for _ in places],
        jax.tree.map(whole, list(moments)),
        [hbm(None) for _ in matrices],
        whole(gains),
        whole(biases),
        whole(fc1b),
    ]
    return pl.pallas_call(
        body,
        grid_spec=pltpu.PrefetchScalarGridSpec(
            num_scalar_prefetch=3,
            grid=(images,),
            in_specs=[image_specs] + specs,
            out_specs=[image_specs] + [whole(shape) for shape in out_shapes[1:]],
            scratch_shapes=scratch,
        ),
        out_shape=out_shapes,
        compiler_params=pltpu.CompilerParams(vmem_limit_bytes=VMEM_LIMIT),
        cost_estimate=pl.CostEstimate(
            flops=images * 8_000_000_000, bytes_accessed=40_000_000, transcendentals=0
        ),
    )(lax.slice_in_dim(sizes, start, start + images), band, gate_open, list(xct), *previous, *smalls)


def lane_tiles(columns):
    return [
        (index, low, min(low + LANE, columns))
        for index, low in enumerate(range(0, columns, LANE))
    ]


def pack_kernel(first, order_ref, class_ref, band_ref, x_ref, ct_ref, table_ref, *refs):
    outs, wides = refs[:-2], refs[-2:]
    rows, count, columns = x_ref.shape
    images = count // len(outs)

    for source, wide in zip((x_ref, ct_ref), wides):
        for row in range(rows):
            for index, low, high in lane_tiles(columns):
                at = slice(row * (count + 1), row * (count + 1) + count)
                wide[index, at, : high - low] = source[row, :, low:high].astype(F32)

    for step, out in enumerate(outs):

        def one(index, carry, out=out, step=step):
            place = (band_ref[0] ^ step) * images + first + index
            at = pl.ds(order_ref[place], rows, stride=count + 1)
            select = table_ref[class_ref[place]]
            for which, wide in enumerate(wides):
                for tile, low, high in lane_tiles(columns):
                    taken = dot_nn(select, wide[tile, at, :].astype(BF16)).astype(BF16)
                    out[which, index, :, low:high] = taken[:, : high - low]
            return carry

        lax.fori_loop(0, out.shape[1], one, 0)


def pack_images(x, ct, order, classes, band, bands, first, size):
    rows, count, columns = x.shape
    piece = piece_rows(bands)
    table = jnp.asarray(pack_matrix(bands), BF16)
    vmem = pl.BlockSpec(memory_space=pltpu.VMEM)
    return pl.pallas_call(
        functools.partial(pack_kernel, first),
        grid_spec=pltpu.PrefetchScalarGridSpec(
            num_scalar_prefetch=3,
            grid=(),
            in_specs=[vmem] * 3,
            out_specs=[vmem] * bands,
            scratch_shapes=[
                pltpu.VMEM(
                    (round_up(columns, LANE) // LANE, round_up(rows * (count + 1), 8), LANE), F32
                )
            ]
            * 2,
        ),
        out_shape=[jax.ShapeDtypeStruct((2, size, piece, columns), BF16)] * bands,
        compiler_params=pltpu.CompilerParams(vmem_limit_bytes=VMEM_LIMIT),
        cost_estimate=pl.CostEstimate(flops=10_000_000, bytes_accessed=10_000_000, transcendentals=0),
    )(order, classes, band, x, ct, table)


def unpack_kernel(chunks, bands, order_ref, class_ref, band_ref, table_ref, *refs):
    parts, (out_ref, ig_ref), wides = refs[:-4], refs[-4:-2], refs[-2:]
    images = sum(chunks)
    rows, count, columns = out_ref.shape
    first = 0
    for chunk, size in enumerate(chunks):
        for step in range(bands):
            part = parts[chunk * bands + step]

            def one(index, carry, part=part, first=first, step=step):
                place = (band_ref[0] ^ step) * images + first + index
                at = pl.ds(order_ref[place], rows, stride=count + 1)
                spread = table_ref[class_ref[place]]
                for which, wide in enumerate(wides):
                    for tile, low, high in lane_tiles(columns):
                        made = dot_nn(spread, part[which, index, :, low:high])
                        if high - low < LANE:
                            fill = jnp.zeros((rows, LANE - (high - low)), F32)
                            made = jnp.concatenate([made, fill], axis=1)
                        wide[tile, at, :] = made
                return carry

            lax.fori_loop(0, size, one, 0)
        first += size

    for target, wide in zip((out_ref, ig_ref), wides):
        for row in range(rows):
            for tile, low, high in lane_tiles(columns):
                at = slice(row * (count + 1), row * (count + 1) + count)
                target[row, :, low:high] = wide[tile, at, : high - low].astype(target.dtype)


def unpack_images(parts, order, classes, band, chunks, rows):
    bands = len(parts[0])
    columns = parts[0][0].shape[-1]
    count = bands * sum(chunks)
    table = jnp.asarray(pack_matrix(bands).transpose(0, 2, 1), BF16)
    vmem = pl.BlockSpec(memory_space=pltpu.VMEM)
    flat = [piece for part in parts for piece in part]
    return pl.pallas_call(
        functools.partial(unpack_kernel, chunks, bands),
        grid_spec=pltpu.PrefetchScalarGridSpec(
            num_scalar_prefetch=3,
            grid=(),
            in_specs=[vmem] * (1 + len(flat)),
            out_specs=[vmem] * 2,
            scratch_shapes=[
                pltpu.VMEM(
                    (round_up(columns, LANE) // LANE, round_up(rows * (count + 1), 8), LANE), F32
                )
            ]
            * 2,
        ),
        out_shape=[
            jax.ShapeDtypeStruct((rows, count, columns), BF16),
            jax.ShapeDtypeStruct((rows, count, columns), F32),
        ],
        compiler_params=pltpu.CompilerParams(vmem_limit_bytes=VMEM_LIMIT),
        cost_estimate=pl.CostEstimate(flops=10_000_000, bytes_accessed=16_000_000, transcendentals=0),
    )(order, classes, band, table, *flat)


def prep_kernel(head_ref, gate_ref, wqkv_in, wout_in, w1_in, w2t_in, *refs):
    wqkv, wback, wout, w1, w2t = refs[:5]
    places, moments = refs[5:8], refs[8:11]
    columns = wout_in.shape[0]
    width = wout.shape[0]
    heads = head_ref.shape[1]
    wback[...] = wqkv_in[...].astype(BF16)
    for part in range(3):
        low = part * width
        wqkv[:, low : low + columns] = wqkv_in[:, part * columns : (part + 1) * columns].astype(BF16)
        wqkv[:, low + columns : low + width] = jnp.zeros((columns, width - columns), BF16)
    wout[:columns, :] = wout_in[...].astype(BF16)
    wout[columns:, :] = jnp.zeros((width - columns, columns), BF16)
    for out, source in ((w1, w1_in), (w2t, w2t_in)):
        units = source.shape[1]
        out[:, :units] = source[...].astype(BF16)
        out[:, units:] = jnp.zeros((columns, out.shape[1] - units), BF16)

    for side, place, moment in zip(SIDES, places, moments):
        live, rows, lanes = side_sizes(side)

        def spots(axis, rows=rows, lanes=lanes, side=side):
            ids = lax.broadcasted_iota(jnp.int32, (rows, lanes), axis)
            spot = ids.astype(F32)
            row = jnp.floor((spot + 0.5) * (1.0 / side))
            return ids, spot - side * row, row

        key_ids, key_x, key_y = spots(0)
        query_ids, query_x, query_y = spots(1)
        delta_x, delta_y = key_x - query_x, key_y - query_y
        distance = delta_x * delta_x + delta_y * delta_y
        dead_key = key_ids >= live
        inside = (key_ids < live) & (query_ids < live)
        middle = 0.5 * (side - 1)
        from_x, from_y = key_x - middle, key_y - middle

        def one(head, carry, place=place, moment=moment, from_x=from_x, from_y=from_y):
            scores = head_ref[0, head] * delta_x + head_ref[1, head] * delta_y
            scores = jnp.where(dead_key, MASKED, scores + head_ref[2, head] * distance)
            top = jnp.max(scores, axis=0, keepdims=True)
            raised = jnp.exp(scores - top)
            total = jnp.sum(raised, axis=0, keepdims=True)
            made = jnp.where(inside, raised * (gate_ref[head] / total), 0.0)
            place[head] = made
            for row, factor in enumerate((from_x, from_y, from_x * from_x + from_y * from_y)):
                moment[head, row : row + 1, :] = jnp.sum(made * factor, axis=0, keepdims=True)
            return carry

        lax.fori_loop(0, heads, one, 0)


def prepare(w_qkv, w_out, w_fc1, w_fc2t, head_params, gate_value):
    columns, heads = w_out.shape[0], head_params.shape[1]
    width = round_up(columns, LANE)
    padded = round_up(w_fc1.shape[1], 256)
    vmem = pl.BlockSpec(memory_space=pltpu.VMEM)
    smem = pl.BlockSpec(memory_space=pltpu.SMEM)
    shapes = [
        (columns, 3 * width),
        (columns, 3 * columns),
        (width, columns),
        (columns, padded),
        (columns, padded),
    ]
    outs = [jax.ShapeDtypeStruct(shape, BF16) for shape in shapes]
    outs += [jax.ShapeDtypeStruct((heads,) + side_sizes(side)[1:], F32) for side in SIDES]
    outs += [jax.ShapeDtypeStruct((heads, 8, side_sizes(side)[2]), F32) for side in SIDES]
    made = pl.pallas_call(
        prep_kernel,
        out_shape=outs,
        in_specs=[smem, smem] + [vmem] * 4,
        out_specs=[vmem] * len(outs),
        compiler_params=pltpu.CompilerParams(vmem_limit_bytes=VMEM_LIMIT),
        cost_estimate=pl.CostEstimate(
            flops=50_000_000, bytes_accessed=22_000_000, transcendentals=2_000_000
        ),
    )(head_params, gate_value, w_qkv, w_out, w_fc1, w_fc2t)
    return made[:5], made[5:8], made[8:]


def reduce_plan(tile_total, devices):
    each = -(-tile_total // devices)
    weight = sum(wave[1] for wave in WAVES)
    waves = []
    base = before = taken = 0
    for order, part, start in WAVES:
        before += part
        share = -(-each * before // weight) - taken
        if share:
            waves.append((base, share, order, start))
            base += devices * share
            taken += share
    return waves, each * devices


def reduce_kernel(
    waves,
    rank_z,
    own_ref,
    small_ref,
    full_out,
    small_out,
    own,
    full,
    recv0,
    recv1,
    small_own,
    small_recv,
    send_sem,
    recv_sem,
    small_send,
    small_got,
    copy_sem,
):
    img = lax.axis_index("img")
    band = lax.axis_index("band")
    z, y = img // 2, img % 2
    x, c = band // 2, band % 2
    low_z, high_z = z % 2, z // 2
    high_count = rank_z // 2
    mesh_ids = pl.DeviceIdType.MESH
    axes = {
        "c": (c, 2, lambda k: (img, x * 2 + 1 - c)),
        "y": (y, 2, lambda k: (z * 2 + 1 - y, band)),
        "x": (x, 2, lambda k: (img, (1 - x) * 2 + c)),
        "l": (low_z, 2, lambda k: ((high_z * 2 + 1 - low_z) * 2 + y, band)),
        "h": (
            high_z,
            high_count,
            lambda k: ((lax.rem(high_z + k, high_count) * 2 + low_z) * 2 + y, band),
        ),
    }
    order = [name for name in "cyxlh" if axes[name][1] > 1]
    partners = [axes[name][2](k) for name in order for k in range(1, axes[name][1])]
    devices = 1
    for name in order:
        devices *= axes[name][1]

    loads = []
    for w, (base, share, _, _) in enumerate(waves):
        at = pl.ds(base, devices * share)
        loads.append(pltpu.make_async_copy(own_ref.at[at], own.at[at], copy_sem.at[w]))
        loads[-1].start()
    small_own[...] = small_ref[...]

    barrier = pltpu.get_barrier_semaphore()
    for partner in partners:
        pl.semaphore_signal(barrier, inc=1, device_id=partner, device_id_type=mesh_ids)
    pl.semaphore_wait(barrier, len(partners))

    counters = [0] * len(waves)

    def send(wave, src, dst, target):
        slot = counters[wave]
        counters[wave] += 1
        copy = pltpu.make_async_remote_copy(
            src_ref=src,
            dst_ref=dst,
            send_sem=send_sem.at[wave, slot],
            recv_sem=recv_sem.at[wave, slot],
            device_id=target,
            device_id_type=mesh_ids,
        )
        copy.start()
        return copy

    def add_tiles(dst, dst_at, parts, count, out, out_at):
        block = 8

        def one(offset, size):
            total = dst[pl.ds(dst_at + offset, size)].astype(F32)
            for ref, at in parts:
                total += ref[pl.ds(at + offset, size)].astype(F32)
            out[pl.ds(out_at + offset, size)] = total.astype(BF16)

        if count >= block:

            def step(index, carry):
                one(index * block, block)
                return carry

            lax.fori_loop(0, count // block, step, 0)
        rest = count % block
        if rest:
            one(count - rest, rest)

    stores = []

    def wave_stages(w):
        base, share, axis_order, _ = waves[w]
        order = [name for name in axis_order if axes[name][1] > 1]
        state = {"at": base, "size": devices * share, "copies": [], "parts": []}
        taken = [base // 2]

        def finish():
            for copy in state["copies"]:
                copy.wait()

        def scatter(name):
            def run():
                if state["parts"]:
                    finish()
                    add_tiles(own, state["at"], state["parts"], state["size"], own, state["at"])
                else:
                    loads[w].wait()
                mine, count, target = axes[name]
                size = state["size"] // count
                state["copies"], state["parts"] = [], []
                for k in range(1, count):
                    other = lax.rem(mine + k, count)
                    if name == order[0]:
                        buffer, at = recv0, base // 2
                    else:
                        buffer, at = recv1, taken[0]
                        taken[0] += size
                    state["copies"].append(
                        send(
                            w,
                            own.at[pl.ds(state["at"] + other * size, size)],
                            buffer.at[pl.ds(at, size)],
                            target(k),
                        )
                    )
                    state["parts"].append((buffer, at))
                state["at"] = state["at"] + mine * size
                state["size"] = size

            return run

        def gather(name, first):
            def run():
                finish()
                if first:
                    at = state["at"]
                    add_tiles(own, at, state["parts"], state["size"], full, at)
                mine, count, target = axes[name]
                piece = full.at[pl.ds(state["at"], state["size"])]
                state["copies"] = [send(w, piece, piece, target(k)) for k in range(1, count)]
                state["at"] = state["at"] - mine * state["size"]
                state["size"] = state["size"] * count

            return run

        def close():
            finish()
            at = pl.ds(base, devices * share)
            stores.append(
                pltpu.make_async_copy(full.at[at], full_out.at[at], copy_sem.at[len(waves) + w])
            )
            stores[-1].start()

        steps = [scatter(name) for name in order]
        steps += [gather(name, name == order[-1]) for name in reversed(order)]
        return steps + [close]

    small_slots = [0]
    small_state = {}

    def small_start(name):
        mine, count, target = axes[name]
        first = small_slots[0]
        small_slots[0] += count - 1
        small_state["copies"] = []
        for k in range(1, count):
            slot = first + k - 1
            copy = pltpu.make_async_remote_copy(
                src_ref=small_own,
                dst_ref=small_recv.at[slot],
                send_sem=small_send.at[slot],
                recv_sem=small_got.at[slot],
                device_id=target(k),
                device_id_type=mesh_ids,
            )
            copy.start()
            small_state["copies"].append(copy)
        small_state["first"] = first

    def small_end(name):
        mine, count, _ = axes[name]
        first = small_state["first"]
        for copy in small_state["copies"]:
            copy.wait()
        if count == 2:
            small_own[...] = small_own[...] + small_recv[first]
        else:
            last = small_recv.shape[0] - 1
            small_recv[last] = small_own[...]

            def add_line(index, total):
                k = lax.rem(mine - index + count, count)
                slot = jnp.where(k == 0, last, first + k - 1)
                return total + small_recv[slot]

            small_own[...] = lax.fori_loop(0, count, add_line, jnp.zeros_like(small_own))

    programs = [wave_stages(w) for w in range(len(waves))]
    depth = len(programs[0])
    for program in programs:
        program[0]()
    last = max(wave[3] for wave in waves) + depth
    for time in range(1, max(last, len(order) + 2)):
        for w, wave in enumerate(waves):
            if 1 <= time - wave[3] < depth:
                programs[w][time - wave[3]]()
        if 1 <= time <= len(order) + 1:
            if time > 1:
                small_end(order[time - 2])
            if time <= len(order):
                small_start(order[time - 1])
    small_out[...] = small_own[...]
    for store in stores:
        store.wait()


def reduce_all(tiles, small, waves, img_count):
    total = tiles.shape[0]
    rank_z = img_count // 2
    copies = 2 * (4 + max(rank_z // 2 - 1, 0))
    hops = 4 + max(rank_z // 2 - 1, 0)
    return pl.pallas_call(
        functools.partial(reduce_kernel, waves, rank_z),
        out_shape=[
            jax.ShapeDtypeStruct(tiles.shape, BF16),
            jax.ShapeDtypeStruct(small.shape, F32),
        ],
        in_specs=[pl.BlockSpec(memory_space=pl.ANY), pl.BlockSpec(memory_space=pltpu.VMEM)],
        out_specs=[pl.BlockSpec(memory_space=pl.ANY), pl.BlockSpec(memory_space=pltpu.VMEM)],
        scratch_shapes=[
            pltpu.VMEM(tiles.shape, BF16),
            pltpu.VMEM(tiles.shape, BF16),
            pltpu.VMEM((total // 2, SUB, LANE), BF16),
            pltpu.VMEM((total // 2, SUB, LANE), BF16),
            pltpu.VMEM(small.shape, F32),
            pltpu.VMEM((hops + 1,) + small.shape, F32),
            pltpu.SemaphoreType.DMA((len(waves), copies)),
            pltpu.SemaphoreType.DMA((len(waves), copies)),
            pltpu.SemaphoreType.DMA((hops,)),
            pltpu.SemaphoreType.DMA((hops,)),
            pltpu.SemaphoreType.DMA((2 * len(waves),)),
        ],
        compiler_params=pltpu.CompilerParams(
            collective_id=1, has_side_effects=True, vmem_limit_bytes=VMEM_LIMIT
        ),
        cost_estimate=pl.CostEstimate(
            flops=10_000_000, bytes_accessed=200_000_000, transcendentals=0
        ),
    )(tiles, small)


def update_kernel(
    decay_rate,
    head_count,
    widths,
    tiles_ref,
    small_ref,
    weight_hbm,
    line_refs,
    vector_refs,
    moment_refs,
    norm_out,
    grad_hbm,
    new_hbm,
    vgrad_outs,
    vnew_outs,
    line_outs,
    moment_outs,
    weights,
    grads,
    news,
    row_s,
    col_s,
    copy_sem,
):
    columns = weights[0].shape[0]
    row_tiles = columns // SUB
    spans = [-(-wide // LANE) for wide in widths]
    total_span = tiles_stride(widths)
    starts = []
    at = 0
    for wide in widths:
        starts.append(at)
        at += tile_span(wide)
    loads = [
        pltpu.make_async_copy(weight_hbm[i], weights[i], copy_sem.at[i]) for i in range(4)
    ]
    for load in loads:
        load.start()

    def tile_rows(index, which):
        place = index * total_span + starts[which]
        pieces = [tiles_ref[place + col].astype(F32) for col in range(spans[which])]
        whole = jnp.concatenate(pieces, axis=1) if len(pieces) > 1 else pieces[0]
        return whole[:, : widths[which]]

    def all_sum(values):
        return jnp.sum(jnp.sum(values, axis=0, keepdims=True), axis=1, keepdims=True)

    def measure(index, carry):
        at = pl.ds(pl.multiple_of(index * SUB, SUB), SUB)
        made = []
        for which in range(4):
            grad = tile_rows(index, which)
            square = grad * grad
            row_s[which, at, :] = jnp.sum(square, axis=1, keepdims=True)
            made.append(carry[which] + fold_rows(square))
        return tuple(made)

    zeros = tuple(jnp.zeros((8, wide), F32) for wide in widths)
    folded = lax.fori_loop(0, row_tiles, measure, zeros)
    col_squares = [jnp.sum(fold, axis=0, keepdims=True) for fold in folded]
    total = jnp.zeros((1, 1), F32)
    for square in col_squares:
        total += jnp.sum(square, axis=1, keepdims=True)

    parts = vector_refs[2].shape[0]
    places = (
        (slice(0, 2), columns),
        (slice(2, 6), columns),
        (slice(6, 6 + parts), columns),
        (slice(6 + parts, 10 + parts), head_count),
    )
    vectors = [small_ref[rows, :wide] for rows, wide in places]
    for grad in vectors:
        total += all_sum(grad * grad)
    norm = jnp.sqrt(total)
    norm_out[...] = norm
    factor = 1.0 / jnp.maximum(norm, 1.0)

    for index in range(4):
        grad = vectors[index] * factor
        weight = vector_refs[index][...]
        moment = decay_rate * moment_refs[index][...] + (1.0 - decay_rate) * (
            grad * grad + FLOOR_ONE
        )
        update = grad * lax.rsqrt(moment)
        size = weight.shape[0] * weight.shape[1]
        mean_square = all_sum(update * update) / size
        update = update / jnp.maximum(1.0, jnp.sqrt(mean_square) / CLIP_RMS)
        scale = STEP_RATE * jnp.maximum(FLOOR_TWO, jnp.sqrt(all_sum(weight * weight) / size))
        vgrad_outs[index][...] = grad
        vnew_outs[index][...] = weight - scale * update
        moment_outs[index][...] = moment

    row_factors, col_factors = [], []
    for which in range(4):
        wide = widths[which]
        down_old, along_old = line_refs[which]
        down_out, along_out = line_outs[which]
        down = jnp.broadcast_to(down_old[...], (LANE, columns)).T
        down = decay_rate * down + (1.0 - decay_rate) * (
            row_s[which] * (factor * factor) / wide + FLOOR_ONE
        )
        along = decay_rate * along_old[...] + (1.0 - decay_rate) * (
            col_squares[which] * (factor * factor) / columns + FLOOR_ONE
        )
        down_out[...] = down.T[:1, :]
        along_out[...] = along
        down = down[:, :1]
        if which == 3:
            along = along / (jnp.sum(along, axis=1, keepdims=True) / wide)
        else:
            down = down / (jnp.sum(down, axis=0, keepdims=True) / columns)
        row_s[which] = lax.rsqrt(down) * factor
        col_s[which, :, :wide] = lax.rsqrt(along)

    for load in loads:
        load.wait()

    def scan(index, carry):
        at = pl.ds(pl.multiple_of(index * SUB, SUB), SUB)
        made = []
        for which in range(4):
            wide = widths[which]
            update = tile_rows(index, which) * col_s[which, :, :wide] * row_s[which, at, :]
            weight = weights[which][at, :]
            made.append(carry[2 * which] + fold_rows(update * update))
            made.append(carry[2 * which + 1] + fold_rows(weight * weight))
        return tuple(made)

    sums = lax.fori_loop(0, row_tiles, scan, tuple(z for z in zeros for _ in range(2)))
    stores = []
    for which in (2, 3, 0, 1):
        wide = widths[which]
        size = columns * wide
        scale = STEP_RATE * jnp.maximum(FLOOR_TWO, jnp.sqrt(all_sum(sums[2 * which + 1]) / size))
        scale = scale / jnp.maximum(1.0, jnp.sqrt(all_sum(sums[2 * which]) / size) / CLIP_RMS)
        col_factor = col_s[which, :, :wide] * scale

        def write(index, carry, which=which, col_factor=col_factor):
            at = pl.ds(pl.multiple_of(index * SUB, SUB), SUB)
            grad = tile_rows(index, which)
            grads[which][at, :] = grad * factor
            news[which][at, :] = weights[which][at, :] - grad * col_factor * row_s[which, at, :]
            return carry

        lax.fori_loop(0, row_tiles, write, 0)
        for source, target, slot in (
            (grads[which], grad_hbm[which], 4 + which),
            (news[which], new_hbm[which], 8 + which),
        ):
            stores.append(pltpu.make_async_copy(source, target, copy_sem.at[slot]))
            stores[-1].start()
    for store in stores:
        store.wait()


def tile_span(wide):
    return round_up(wide, 256 if wide > 1500 else LANE) // LANE


def tiles_stride(widths):
    return sum(tile_span(wide) for wide in widths)


def update_all(tiles, small, weights, rows, cols, vectors, moments, decay_rate):
    columns = weights[1].shape[0]
    head_count = vectors[3].shape[1]
    units = weights[2].shape[1]
    parts = units // columns
    flat = lambda v: v.reshape(1, -1)
    lines = [[flat(r), flat(c)] for r, c in zip(rows, cols)]
    lines[3] = lines[3][::-1]
    vectors = [v.reshape(parts, columns) if v.ndim == 1 else v for v in vectors]
    moments = [v.reshape(parts, columns) if v.ndim == 1 else v for v in moments]
    widths = [weight.shape[1] for weight in weights]
    like = lambda group: [jax.ShapeDtypeStruct(v.shape, F32) for v in group]
    outs = [
        jax.ShapeDtypeStruct((1, 1), F32),
        like(weights),
        like(weights),
        like(vectors),
        like(vectors),
        [like(pair) for pair in lines],
        like(vectors),
    ]
    vmem = pl.BlockSpec(memory_space=pltpu.VMEM)
    hbm = pl.BlockSpec(memory_space=pl.ANY)
    args = (tiles, small, list(weights), lines, vectors, moments)
    in_specs = list(jax.tree.map(lambda _: vmem, args))
    in_specs[2] = [hbm] * 4
    out_specs = jax.tree.map(lambda _: vmem, outs)
    out_specs[1] = [hbm] * 4
    out_specs[2] = [hbm] * 4
    full = lambda: [pltpu.VMEM(weight.shape, F32) for weight in weights]
    scratch = [
        full(),
        full(),
        full(),
        pltpu.VMEM((4, columns, 1), F32),
        pltpu.VMEM((4, 1, round_up(max(widths), LANE)), F32),
        pltpu.SemaphoreType.DMA((12,)),
    ]
    made = pl.pallas_call(
        functools.partial(update_kernel, decay_rate, head_count, widths),
        out_shape=outs,
        in_specs=in_specs,
        out_specs=out_specs,
        scratch_shapes=scratch,
        compiler_params=pltpu.CompilerParams(vmem_limit_bytes=VMEM_LIMIT),
    )(*args)
    norm, grads, news, vgrads, vnews, line_new, moment_new = made
    spread = lambda group: [v.reshape(-1) if i == 2 else v for i, v in enumerate(group)]
    line_new[3] = line_new[3][::-1]
    moved = [line.reshape(-1) for pair in line_new for line in pair]
    grads[3], news[3] = grads[3].T, news[3].T
    return (
        norm.reshape(1),
        *grads,
        *spread(vgrads),
        *news,
        *spread(vnews),
        *moved,
        *spread(moment_new),
    )


def deal_images(grid_sizes, devices):
    count = grid_sizes.shape[0]
    ids = jnp.arange(count, dtype=jnp.int32)
    ahead = (grid_sizes[None, :] > grid_sizes[:, None]) | (
        (grid_sizes[None, :] == grid_sizes[:, None]) & (ids[None, :] < ids[:, None])
    )
    rank = jnp.sum(ahead.astype(jnp.int32), axis=1)
    turn = rank // devices
    seat = rank % devices
    seat = jnp.where(turn % 2 == 0, seat, devices - 1 - seat)
    place = seat * (count // devices) + turn
    hit = place[None, :] == ids[:, None]
    order = jnp.sum(jnp.where(hit, ids[None, :], 0), axis=1)
    sizes = jnp.sum(jnp.where(hit, grid_sizes[None, :], 0), axis=1)
    return order, sizes


def per_device(
    inputs,
    cotangent,
    grid_sizes,
    w_qkv,
    w_out,
    w_fc1,
    w_fc2,
    norm_gains,
    biases,
    fc1_bias,
    head_params,
    rows_qkv,
    cols_qkv,
    rows_out,
    cols_out,
    rows_fc1,
    cols_fc1,
    rows_fc2,
    cols_fc2,
    gain_moment,
    bias_moment,
    fc1_bias_moment,
    head_moment,
):
    band_count = lax.axis_size("band")
    img_count = lax.axis_size("img")
    band_index = lax.axis_index("band")
    columns = inputs.shape[2]
    units = w_fc1.shape[1]
    per_band = inputs.shape[0] // band_count
    order, sizes_ordered = deal_images(grid_sizes, band_count)
    classes = sum(
        (jnp.where(sizes_ordered == side, index, 0) for index, side in enumerate(SIDES)),
        jnp.zeros_like(order),
    )
    sizes_used = lax.dynamic_slice_in_dim(sizes_ordered, band_index * per_band, per_band)
    early = max(1, per_band // 2)
    chunks = (early, per_band - early)
    band = band_index.astype(jnp.int32).reshape(1)
    x_stored, ct_stored = jnp.swapaxes(inputs, 0, 1), jnp.swapaxes(cotangent, 0, 1)
    pack = lambda first, size: pack_images(
        x_stored, ct_stored, order, classes, band, band_count, first, size
    )

    def exchange(parts):
        swaps = [[(i, i ^ step) for i in range(band_count)] for step in range(band_count)]
        return [parts[0]] + [
            lax.ppermute(parts[step], "band", swaps[step]) for step in range(1, band_count)
        ]

    waves, tile_count = reduce_plan(
        (columns // SUB) * tiles_stride((3 * columns, columns, units, units)),
        band_count * img_count,
    )
    w_fc2t = w_fc2.T
    gate_value = jax.nn.sigmoid(head_params[3])
    matrices, places, spots = prepare(w_qkv, w_out, w_fc1, w_fc2t, head_params, gate_value)
    first_part = pack(0, early)
    first_moved = exchange(first_part)
    later_part = pack(early, per_band - early)
    later_part, matrices, first_moved = lax.optimization_barrier(
        (later_part, matrices, first_moved)
    )
    moved = [first_moved, exchange(later_part)]
    fc1b = jnp.pad(fc1_bias[None, :], ((0, 0), (0, matrices[3].shape[1] - units)))
    shared = (places, spots, 1.0 - gate_value, matrices, norm_gains, biases, fc1b)
    previous = None
    start = 0
    results = []
    for part, size in zip(moved, chunks):
        result, *previous = run_images(
            part, sizes_used, start, band, shared, previous, units, tile_count
        )
        results.append(result)
        start += size
    tiles, small = previous
    results[0], tiles = lax.optimization_barrier((exchange(results[0]), tiles))
    full, small = reduce_all(tiles, small, waves, img_count)
    results[1], full = lax.optimization_barrier((results[1], full))
    results[1] = exchange(results[1])
    updated = update_all(
        full,
        small,
        (w_qkv, w_out, w_fc1, w_fc2t),
        (rows_qkv, rows_out, rows_fc1, rows_fc2),
        (cols_qkv, cols_out, cols_fc1, cols_fc2),
        (norm_gains, biases, fc1_bias, head_params),
        (gain_moment, bias_moment, fc1_bias_moment, head_moment),
        1.0 - STEP ** (-0.8),
    )
    output, input_grad = unpack_images(
        results, order, classes, band, chunks, inputs.shape[1]
    )
    return (jnp.swapaxes(output, 0, 1), jnp.swapaxes(input_grad, 0, 1), *updated)


def solution(mesh):
    split = P("img", "band", None)
    return jax.shard_map(
        per_device,
        mesh=mesh,
        in_specs=(split, split, P("img")) + (P(),) * 20,
        out_specs=(split, split) + (P(),) * 29,
        check_vma=False,
    )
```

```python
import functools
import math

import jax
import jax.numpy as jnp
import numpy as np
from jax import lax
from jax.experimental import pallas as pl
from jax.experimental.pallas import tpu as pltpu
from jax.sharding import PartitionSpec as P

GRID = 20
STEP = 10
SIDES = (18, 14, 10)

NORM_FLOOR = 1e-06
FLOOR_ONE = 1e-30
FLOOR_TWO = 0.001
STEP_RATE = 0.6
CLIP_RMS = 1.0
MASKED = -1e30

BF16 = jnp.bfloat16
F32 = jnp.float32
VMEM_LIMIT = 60 * 1024 * 1024
SUB = 16
SMALL_ROWS = 16
WAVES = (
    ("cyxlh", 7),
    ("cxylh", 7),
    ("clhxy", 4),
    ("cyxlh", 7),
    ("cxylh", 7),
    ("clhxy", 5),
)
LANE = 128


def round_up(value, unit):
    return (value + unit - 1) // unit * unit


def side_sizes(side):
    live = side * side
    return live, round_up(live, SUB), round_up(live, LANE)


def dot_nn(left, right):
    return lax.dot_general(left, right, (((1,), (0,)), ((), ())), preferred_element_type=F32)


def dot_nt(left, right):
    return lax.dot_general(left, right, (((1,), (1,)), ((), ())), preferred_element_type=F32)


def piece_rows(bands):
    return round_up(GRID // bands * max(SIDES), SUB)


def select_matrix(side, bands):
    live, rows, _ = side_sizes(side)
    tall, piece = GRID // bands, piece_rows(bands)
    made = np.zeros((rows, bands * piece), np.float32)
    for row in range(side):
        for col in range(side):
            at = row // tall * piece + (row % tall) * side + col
            made[row * side + col, at] = 1.0
    return made


def select_matrices(side, bands):
    made = select_matrix(side, bands).reshape(-1, bands, piece_rows(bands))
    ordered = [made[:, [own ^ step for step in range(bands)]] for own in range(bands)]
    return np.stack(ordered).reshape(bands, made.shape[0], -1)


def rest_matrices(side, bands):
    piece = piece_rows(bands)
    made = select_matrices(side, bands).reshape(bands, -1, bands, piece)
    halves = [made[..., : piece // 2], made[..., piece // 2 :]]
    return np.stack([half.reshape(bands, made.shape[1], -1) for half in halves], axis=1)


def stored_shape(piece, columns):
    main = columns // LANE * LANE
    return piece + piece // 2 * LANE // main, main


def folded(ref, which, index, piece):
    rows, main = ref.shape[2:]
    pieces = [ref[which, index, piece:, low : low + LANE] for low in range(0, main, LANE)]
    return jnp.concatenate(pieces, axis=0)


def fold(ref, which, index, piece, block):
    rows, main = ref.shape[2:]
    each = rows - piece
    for tile in range(main // LANE):
        at = slice(tile * LANE, (tile + 1) * LANE)
        ref[which, index, piece:, at] = block[tile * each : (tile + 1) * each]


def pack_matrix(bands):
    tall, piece = GRID // bands, piece_rows(bands)
    made = np.zeros((len(SIDES), piece, tall * GRID), np.float32)
    for index, side in enumerate(SIDES):
        for row in range(tall):
            for col in range(side):
                made[index, row * side + col, row * GRID + col] = 1.0
    return made


def fold_rows(values):
    rows, columns = values.shape
    return jnp.sum(values.reshape(rows // 8, 8, columns), axis=0)


def image_kernel(
    columns,
    heads,
    hidden_units,
    image_count,
    started,
    sizes_ref,
    band_ref,
    gate_ref,
    xct_refs,
    tiles_in,
    small_in,
    sel_refs,
    selt_refs,
    rest_refs,
    restt_refs,
    place_hbm,
    moment_refs,
    weight_hbm,
    gains_ref,
    biases_ref,
    fc1b_ref,
    outig_refs,
    tiles_ref,
    small_ref,
    proj_s,
    projt_s,
    da_s,
    dat_s,
    cont_s,
    mix_s,
    attt_s,
    gt_s,
    act_s,
    gb_s,
    vec_s,
    fc1g_s,
    racc_s,
    gqkv_ref,
    gout_ref,
    g1_ref,
    g2t_ref,
    gsum_refs,
    gm_refs,
    gc_refs,
    second_s,
    ct_s,
    secondt_s,
    ctt_s,
    place_refs,
    weight_refs,
    copy_sem,
):
    wqkv_ref, wback_ref, wout_ref, w1_ref, w2t_ref = weight_refs
    step = pl.program_id(0)
    steps = pl.num_programs(0)
    head_size = columns // heads
    width = wqkv_ref.shape[1] // 3
    window = 256
    score_scale = head_size ** (-0.5)
    chunk = 256
    chunks = w1_ref.shape[1] // chunk

    table = (gqkv_ref, gout_ref, g1_ref, g2t_ref)
    across = sum(ref.shape[1] // LANE for ref in table)
    row_tiles = columns // SUB

    sources = list(weight_hbm) + list(place_hbm)
    targets = list(weight_refs) + list(place_refs)
    loads = [
        pltpu.make_async_copy(source, target, copy_sem.at[1 + index])
        for index, (source, target) in enumerate(zip(sources, targets))
    ]
    load_qkv, load_back, load_out, load_w1, load_w2 = loads[:5]
    load_places = loads[5:]

    def once(*copies):
        @pl.when(step == 0)
        def _():
            for copy in copies:
                copy.wait()

    @pl.when(step == 0)
    def _():
        if started:
            load = pltpu.make_async_copy(tiles_in, tiles_ref, copy_sem.at[0])
            load.start()
        for copy in [load_qkv] + load_places + [load_out, load_w1, load_w2, load_back]:
            copy.start()
        if started:
            load.wait()

            def absorb(index, carry):
                at = pl.ds(pl.multiple_of(index * SUB, SUB), SUB)
                place = index * across
                for ref in table:
                    for col in range(ref.shape[1] // LANE):
                        ref[at, col * LANE : (col + 1) * LANE] = tiles_ref[place].astype(F32)
                        place = place + 1
                return carry

            lax.fori_loop(0, row_tiles, absorb, 0)
        else:
            for ref in table:
                ref[...] = jnp.zeros_like(ref)
        vec_s[...] = jnp.zeros_like(vec_s)
        fc1g_s[...] = jnp.zeros_like(fc1g_s)
        racc_s[...] = jnp.zeros_like(racc_s)
        for ref in gsum_refs:
            ref[...] = jnp.zeros_like(ref)

    def aligned(value, unit):
        return value if isinstance(value, int) else pl.multiple_of(value, unit)

    def head_place(head):
        first_lane = head * head_size
        if isinstance(head, int):
            start = min(first_lane // LANE * LANE, width - window)
        else:
            start = jnp.minimum(first_lane // LANE * LANE, width - window)
        lanes = lax.broadcasted_iota(jnp.int32, (1, window), 1) + start
        mask = (lanes >= first_lane) & (lanes < first_lane + head_size)
        return start, mask

    def part_lanes(part, start):
        return pl.ds(aligned(part * width + start, LANE), window)

    def head_rows(part, head):
        return pl.ds(aligned(part * columns + head * head_size, SUB), head_size)

    def skewed(compact, enter, middle, leave):
        if not compact:
            for index in range(heads + 2):
                if index < heads:
                    enter(index, index % 2)
                if 1 <= index <= heads:
                    middle(index - 1, (index - 1) % 2)
                if index >= 2:
                    leave(index - 2, index % 2)
            return
        enter(0, 0)

        def pair(index, carry):
            for odd in range(2):
                head = index * 2 + odd
                leave(jnp.maximum(head - 1, 0), 1 - odd)
                enter(head + 1, 1 - odd)
                middle(head, odd)
            return carry

        pairs = (heads - 1) // 2
        lax.fori_loop(0, pairs, pair, 0)
        for head in range(2 * pairs, heads):
            leave(head - 1, (head - 1) % 2)
            if head + 1 < heads:
                enter(head + 1, (head + 1) % 2)
            middle(head, head % 2)
        leave(heads - 1, (heads - 1) % 2)

    def image(side, sel_ref, selt_ref, rest_ref, restt_ref, place_ref, gsum_ref):
        live, rows, lanes = side_sizes(side)
        edge = live // 8 * 8
        compact = (side != SIDES[0]) != started
        tall = sel_ref.shape[2] // len(xct_refs)
        main = xct_refs[0].shape[3]

        def gathered(which):
            pieces = jnp.concatenate([ref[which, 0, :tall] for ref in xct_refs], axis=0)
            blocks = [folded(ref, which, 0, tall) for ref in xct_refs]
            block = jnp.concatenate(blocks, axis=0)
            rest = dot_nn(rest_ref[0, 0], block)
            rest += pltpu.roll(dot_nn(rest_ref[0, 1], block), LANE // 2, 1)
            return jnp.concatenate(
                [dot_nn(sel_ref[0], pieces), rest[:, : columns - main]], axis=1
            )

        def spread(which, values):
            values = values.astype(BF16)
            fill = jnp.zeros((rows, LANE - (columns - main)), BF16)
            rest = jnp.concatenate([values[:, main:], fill], axis=1)
            values = dot_nn(selt_ref[0], values[:, :main]).astype(BF16)
            block = dot_nn(restt_ref[0, 0], rest)
            block += pltpu.roll(dot_nn(restt_ref[0, 1], rest), LANE // 2, 1)
            block = block.astype(BF16)
            for index, ref in enumerate(outig_refs):
                ref[which, 0, :tall] = values[index * tall : (index + 1) * tall]
                half = tall // 2
                fold(ref, which, 0, tall, block[index * half : (index + 1) * half])

        def norm(values):
            averaged = jnp.mean(values, axis=-1, keepdims=True)
            centered = values - averaged
            variance = jnp.mean(centered * centered, axis=-1, keepdims=True)
            inverse = lax.rsqrt(variance + NORM_FLOOR)
            return centered * inverse, inverse

        def norm_back(grad, unit, inverse, gain):
            scaled = grad * gain
            first_mean = jnp.mean(scaled, axis=-1, keepdims=True)
            second_mean = jnp.mean(scaled * unit, axis=-1, keepdims=True)
            return inverse * (scaled - first_mean - unit * second_mean)

        x = gathered(0)
        unit_one, inverse_one = norm(x)
        first_b = (unit_one * gains_ref[0:1, :] + biases_ref[0:1, :]).astype(BF16)
        once(load_qkv)
        proj_s[:rows, :] = dot_nn(first_b, wqkv_ref[...]).astype(BF16)
        once(*load_places)
        if lanes > rows:
            proj_s[rows:lanes, :] = jnp.zeros((lanes - rows, 3 * width), BF16)
        for part in range(3):
            piece = proj_s[:lanes, part * width : (part + 1) * width]
            projt_s[part, :, :lanes] = piece.T

        tops = {}

        def score_head(head, slot):
            start, mask = head_place(head)
            query = jnp.where(mask, proj_s[:lanes, part_lanes(0, start)], 0)
            key = proj_s[:rows, part_lanes(1, start)]
            score = dot_nt(key, query)
            tail = lax.broadcasted_iota(jnp.int32, (rows - edge, lanes), 0) < live - edge
            score = jnp.concatenate(
                [score[:edge], jnp.where(tail, score[edge:], MASKED)], axis=0
            )
            gm_refs[slot][:rows, :lanes] = score
            if not compact:
                tops[head] = jnp.max(score, axis=0, keepdims=True)

        def soft_head(head, slot):
            factor = score_scale * math.log2(math.e)
            score = gm_refs[slot][:rows, :lanes]
            top = jnp.max(score, axis=0, keepdims=True) if compact else tops[head]
            raised = jnp.exp2(score * factor - top * factor)
            total = jnp.sum(raised, axis=0, keepdims=True)
            content = raised * (gate_ref[head] / total)
            cont_s[head, :rows, :lanes] = content
            mix_s[head, :rows, :lanes] = (content + place_ref[head]).astype(BF16)

        def attend_head(head, slot):
            here = head_rows(0, head)
            value_t = projt_s[2, here, :rows]
            mixed = mix_s[head, :rows, :lanes]
            attt_s[here, :lanes] = dot_nn(value_t, mixed).astype(BF16)

        skewed(compact, score_head, soft_head, attend_head)

        once(load_out, load_w1, load_w2, load_back)
        attended = attt_s[:, :lanes].T[:rows]
        hidden = x + (dot_nn(attended, wout_ref[:columns, :]) + biases_ref[2:3, :])
        unit_two, inverse_two = norm(hidden)
        second_b = (unit_two * gains_ref[1:2, :] + biases_ref[1:2, :]).astype(BF16)
        ct_b = gathered(1).astype(BF16)

        second_s[:rows, :] = second_b
        ct_s[:rows, :] = ct_b

        def mlp_chunk(index):
            at = pl.ds(aligned(index * chunk, chunk), chunk)
            before = dot_nn(second_s[:rows, :], w1_ref[:, at]) + fc1b_ref[:, at]
            grad_act = dot_nn(ct_s[:rows, :], w2t_ref[:, at])
            square = before * before
            inner = before * (
                math.sqrt(2.0 / math.pi) + (math.sqrt(2.0 / math.pi) * 0.044715) * square
            )
            half = 0.5 * jnp.tanh(inner) + 0.5
            activated = before * half
            slope = half + activated * (1.0 - half) * (
                2.0 * math.sqrt(2.0 / math.pi)
                + (6.0 * math.sqrt(2.0 / math.pi) * 0.044715) * square
            )
            act_s[:rows, at] = activated.astype(BF16)
            grad_b = (grad_act * slope).astype(BF16)
            gb_s[:rows, at] = grad_b
            fc1g_s[:, at] += fold_rows(grad_b.astype(F32))

        def weight_chunk(index):
            at = pl.ds(aligned(index * chunk, chunk), chunk)
            g1_ref[:, at] += dot_nn(secondt_s[:, :rows], gb_s[:rows, at])
            g2t_ref[:, at] += dot_nn(ctt_s[:, :rows], act_s[:rows, at])

        def mlp_step(index, carry):
            weight_chunk(index - 1)
            mlp_chunk(index)
            return carry

        if compact:
            ctt_s[:, :rows] = ct_b.T
            secondt_s[:, :rows] = second_b.T
            mlp_chunk(0)
            lax.fori_loop(1, chunks, mlp_step, 0)
            weight_chunk(chunks - 1)
        else:
            for index in range(chunks):
                mlp_chunk(index)

        result = (
            hidden + dot_nt(act_s[:rows, :], w2t_ref[...]) + biases_ref[3:4, :]
        )
        spread(0, result)

        if not compact:
            ct_t = ct_b.T
            second_t = second_b.T
            for index in range(chunks):
                low, high = index * chunk, min((index + 1) * chunk, hidden_units)
                g1_ref[:, low:high] += dot_nn(second_t, gb_s[:rows, low:high])
                g2t_ref[:, low:high] += dot_nn(ct_t, act_s[:rows, low:high])

        ct_f = ct_b.astype(F32)
        grad_second = dot_nt(gb_s[:rows, :], w1_ref[...])
        grad_hidden = ct_f + norm_back(grad_second, unit_two, inverse_two, gains_ref[1:2, :])
        branch_b = grad_hidden.astype(BF16)
        vec_s[1] += fold_rows(grad_second * unit_two)
        vec_s[3] += fold_rows(grad_second)
        vec_s[4] += fold_rows(branch_b.astype(F32))
        vec_s[5] += fold_rows(ct_f)
        gout_ref[:, :columns] += dot_nn(attt_s[:, :rows], branch_b)
        da_s[:rows, :] = dot_nt(branch_b, wout_ref[...]).astype(BF16)
        if lanes > rows:
            da_s[rows:lanes, :] = jnp.zeros((lanes - rows, width), BF16)
        dat_s[:, :lanes] = da_s[:lanes, :].T

        totals = {}

        def grad_head(head, slot):
            start, mask = head_place(head)
            grad_att = jnp.where(mask, da_s[:lanes, part_lanes(0, start)], 0)
            value = proj_s[:rows, part_lanes(2, start)]
            grad_mixed = dot_nt(value, grad_att)
            gsum_ref[head] += grad_mixed
            product = grad_mixed * cont_s[head, :rows, :lanes]
            gm_refs[slot][:rows, :lanes] = product
            if not compact:
                totals[head] = jnp.sum(product, axis=0, keepdims=True) / gate_ref[head]

        def soft_back_head(head, slot):
            product = gm_refs[slot][:rows, :lanes]
            if compact:
                total = jnp.sum(product, axis=0, keepdims=True) / gate_ref[head]
            else:
                total = totals[head]
            racc_s[SIDES.index(side), head, :, :lanes] += total
            content = cont_s[head, :rows, :lanes]
            gc_refs[slot][:rows, :lanes] = (product - content * total).astype(BF16)

        def back_head(head, slot):
            here = head_rows(0, head)
            mixed = mix_s[head, :rows, :lanes]
            grad_content = gc_refs[slot][:rows, :lanes]
            gt_s[head_rows(2, head), :rows] = dot_nt(dat_s[here, :lanes], mixed).astype(BF16)
            gt_s[head_rows(1, head), :rows] = (
                dot_nt(projt_s[0, here, :lanes], grad_content) * score_scale
            ).astype(BF16)
            gt_s[here, :lanes] = (
                dot_nn(projt_s[1, here, :rows], grad_content) * score_scale
            ).astype(BF16)

        skewed(compact, grad_head, soft_back_head, back_head)

        first_t = first_b.T
        grad_proj = gt_s[:, :lanes].T[:rows]
        gqkv_ref[:, : 3 * columns] += dot_nn(first_t, grad_proj)
        grad_first = dot_nt(grad_proj, wback_ref[...])
        vec_s[0] += fold_rows(grad_first * unit_one)
        vec_s[2] += fold_rows(grad_first)
        input_grad = grad_hidden + norm_back(grad_first, unit_one, inverse_one, gains_ref[0:1, :])
        spread(1, input_grad)

    for index, side in enumerate(SIDES):

        @pl.when(sizes_ref[step] == side)
        def _(index=index, side=side):
            image(
                side,
                sel_refs[index],
                selt_refs[index],
                rest_refs[index],
                restt_refs[index],
                place_refs[index],
                gsum_refs[index],
            )

    @pl.when(step == steps - 1)
    def _():
        def emit(index, carry):
            at = pl.ds(pl.multiple_of(index * SUB, SUB), SUB)
            place = index * across
            for ref in table:
                for col in range(ref.shape[1] // LANE):
                    tiles_ref[place] = ref[at, col * LANE : (col + 1) * LANE].astype(BF16)
                    place = place + 1
            return carry

        lax.fori_loop(0, row_tiles, emit, 0)
        for spare in range(row_tiles * across, tiles_ref.shape[0]):
            tiles_ref[spare] = jnp.zeros((SUB, LANE), BF16)

        small_ref[...] = jnp.zeros_like(small_ref)
        for row in range(6):
            small_ref[row : row + 1, :columns] = jnp.sum(vec_s[row], axis=0, keepdims=True)
        fc1_row = jnp.sum(fc1g_s[...], axis=0, keepdims=True)
        parts = hidden_units // columns
        for part in range(parts):
            small_ref[6 + part : 7 + part, :columns] = fc1_row[
                :, part * columns : (part + 1) * columns
            ]

        tile_rows = lax.broadcasted_iota(jnp.int32, (8, LANE), 0)
        tile_lanes = lax.broadcasted_iota(jnp.int32, (8, LANE), 1)
        grids = []
        for side in SIDES:
            rows, lanes = side_sizes(side)[1:]
            middle = 0.5 * (side - 1)
            key_ids = lax.broadcasted_iota(jnp.int32, (rows, LANE), 0).astype(F32)
            key_row = jnp.floor((key_ids + 0.5) * (1.0 / side))
            key_x, key_y = key_ids - side * key_row - middle, key_row - middle
            query_ids = lax.broadcasted_iota(jnp.int32, (1, lanes), 1).astype(F32)
            query_row = jnp.floor((query_ids + 0.5) * (1.0 / side))
            query_x, query_y = query_ids - side * query_row - middle, query_row - middle
            grids.append((key_x, key_y, key_x * key_x + key_y * key_y, query_x, query_y))

        def head_sums(index, head, carry):
            pieces = [jnp.zeros((1, LANE), F32) for _ in range(4)]
            gate_open = 1.0 - gate_ref[head]
            lanes = side_sizes(SIDES[index])[2]
            key_x, key_y, radius, query_x, query_y = grids[index]

            def total(values):
                return jnp.sum(values, axis=0, keepdims=True)

            for strip in range(lanes // LANE):
                at = slice(strip * LANE, (strip + 1) * LANE)
                weighted = gsum_refs[index][head, :, at] * place_refs[index][head, :, at]
                base = total(weighted)
                scaled = base / gate_open
                mean_x, mean_y, mean_r = (
                    moment_refs[index][head, row : row + 1, at] for row in range(3)
                )
                part_x = total(weighted * key_x) - mean_x * scaled
                part_y = total(weighted * key_y) - mean_y * scaled
                part_r = total(weighted * radius) - mean_r * scaled
                part_r -= 2.0 * (query_x[:, at] * part_x + query_y[:, at] * part_y)
                for row, part in enumerate((part_x, part_y, part_r, gate_ref[head] * base)):
                    pieces[row] += part
            pieces = [jnp.sum(piece, axis=1, keepdims=True) for piece in pieces]
            rests = jnp.sum(racc_s[index, head], axis=1, keepdims=True)
            pieces[3] -= gate_open * gate_ref[head] * rests
            for row in range(4):
                carry = carry + jnp.where(
                    (tile_rows == row) & (tile_lanes == head), pieces[row], 0.0
                )
            return carry

        first_row = 6 + parts
        for index, side in enumerate(SIDES):
            present = sizes_ref[0] == side
            for place in range(1, image_count):
                present = present | (sizes_ref[place] == side)
            @pl.when(present)
            def _(index=index):
                head_tile = lax.fori_loop(
                    0,
                    heads,
                    functools.partial(head_sums, index),
                    jnp.zeros((8, LANE), F32),
                )
                small_ref[first_row : first_row + 4, :LANE] += head_tile[:4]

        if started:
            small_ref[...] += small_in[...]


def matrices_columns(shared):
    return shared[3][0].shape[0]


def run_images(xct, sizes, start, band, shared, previous, units, tile_count):
    bands = len(xct)
    _, images, stored, main = xct[0].shape
    columns = matrices_columns(shared)
    places, moments, gate_open, matrices, gains, biases, fc1b = shared
    heads = gate_open.shape[0]
    width = matrices[0].shape[1] // 3
    padded = matrices[3].shape[1]
    chosen = [select_matrices(side, bands) for side in SIDES]
    sels = [jnp.asarray(made, BF16) for made in chosen]
    selts = [jnp.asarray(made.transpose(0, 2, 1), BF16) for made in chosen]
    chosen = [rest_matrices(side, bands) for side in SIDES]
    rests = [jnp.asarray(made, BF16) for made in chosen]
    restts = [jnp.asarray(made.transpose(0, 1, 3, 2), BF16) for made in chosen]
    sizes_all = [side_sizes(side) for side in SIDES]
    most_rows = max(size[1] for size in sizes_all)
    most_lanes = max(size[2] for size in sizes_all)
    started = previous is not None

    def whole(array):
        rank = len(array.shape)
        return pl.BlockSpec(
            array.shape, lambda i, *_: (0,) * rank, pipeline_mode=pl.Buffered(1)
        )

    def own(array):
        return pl.BlockSpec(
            (1,) + array.shape[1:],
            lambda i, sizes, band, *_: (band[0],) + (0,) * (array.ndim - 1),
            pipeline_mode=pl.Buffered(1),
        )

    image_specs = [pl.BlockSpec((2, 1, stored, main), lambda i, *_: (0, i, 0, 0))] * bands
    out_shapes = [
        [jax.ShapeDtypeStruct(part.shape, BF16) for part in xct],
        jax.ShapeDtypeStruct((tile_count, SUB, LANE), BF16),
        jax.ShapeDtypeStruct((SMALL_ROWS, width), F32),
    ]
    if not started:
        previous = (jnp.zeros((1, SUB, LANE), BF16), jnp.zeros((8, LANE), F32))
    scratch = [
        pltpu.VMEM((most_lanes, 3 * width), BF16),
        pltpu.VMEM((3, width, most_lanes), BF16),
        pltpu.VMEM((most_lanes, width), BF16),
        pltpu.VMEM((width, most_lanes), BF16),
        pltpu.VMEM((heads, most_rows, most_lanes), F32),
        pltpu.VMEM((heads, most_rows, most_lanes), BF16),
        pltpu.VMEM((columns, most_lanes), BF16),
        pltpu.VMEM((3 * columns, most_lanes), BF16),
        pltpu.VMEM((most_rows, padded), BF16),
        pltpu.VMEM((most_rows, padded), BF16),
        pltpu.VMEM((6, 8, columns), F32),
        pltpu.VMEM((8, padded), F32),
        pltpu.VMEM((len(SIDES), heads, 1, most_lanes), F32),
        pltpu.VMEM((columns, round_up(3 * columns, LANE)), F32),
        pltpu.VMEM((columns, width), F32),
        pltpu.VMEM((columns, padded), F32),
        pltpu.VMEM((columns, padded), F32),
        [pltpu.VMEM((heads, size[1], size[2]), F32) for size in sizes_all],
        [pltpu.VMEM((most_rows, most_lanes), F32)] * 2,
        [pltpu.VMEM((most_rows, most_lanes), BF16)] * 2,
        pltpu.VMEM((most_rows, columns), BF16),
        pltpu.VMEM((most_rows, columns), BF16),
        pltpu.VMEM((columns, most_lanes), BF16),
        pltpu.VMEM((columns, most_lanes), BF16),
        [pltpu.VMEM(place.shape, F32) for place in places],
        [pltpu.VMEM(matrix.shape, BF16) for matrix in matrices],
        pltpu.SemaphoreType.DMA((1 + len(places) + len(matrices),)),
    ]
    smalls = [sels, selts, rests, restts, list(places), list(moments), list(matrices), gains, biases, fc1b]
    body = functools.partial(image_kernel, columns, heads, units, images, started)
    hbm = lambda _: pl.BlockSpec(memory_space=pl.ANY)
    specs = [
        hbm(None),
        whole(previous[1]),
        jax.tree.map(own, sels),
        jax.tree.map(own, selts),
        jax.tree.map(own, rests),
        jax.tree.map(own, restts),
        [hbm(None) for _ in places],
        jax.tree.map(whole, list(moments)),
        [hbm(None) for _ in matrices],
        whole(gains),
        whole(biases),
        whole(fc1b),
    ]
    return pl.pallas_call(
        body,
        grid_spec=pltpu.PrefetchScalarGridSpec(
            num_scalar_prefetch=3,
            grid=(images,),
            in_specs=[image_specs] + specs,
            out_specs=[image_specs] + [whole(shape) for shape in out_shapes[1:]],
            scratch_shapes=scratch,
        ),
        out_shape=out_shapes,
        compiler_params=pltpu.CompilerParams(vmem_limit_bytes=VMEM_LIMIT),
        cost_estimate=pl.CostEstimate(
            flops=images * 8_000_000_000, bytes_accessed=40_000_000, transcendentals=0
        ),
    )(lax.slice_in_dim(sizes, start, start + images), band, gate_open, list(xct), *previous, *smalls)


def lane_tiles(columns):
    return [
        (index, low, min(low + LANE, columns))
        for index, low in enumerate(range(0, columns, LANE))
    ]


def loop_rows(rows, count, body, after=None):
    def step(index, carry):
        for row in range(8):
            start = pl.multiple_of(index * (8 * (count + 1)), 8) + row * (count + 1)
            body(index * 8 + row, pl.ds(start, count))
        if after is not None:
            after(pl.ds(index * 8, 8))
        return carry

    lax.fori_loop(0, rows // 8, step, 0)
    for row in range(rows // 8 * 8, rows):
        body(row, pl.ds(row * (count + 1), count))
    if after is not None and rows % 8:
        after(pl.ds(rows // 8 * 8, rows % 8))


def pack_kernel(first, order_ref, class_ref, band_ref, x_ref, ct_ref, table_ref, *refs):
    outs, wides, held, copy_sem = refs[:-4], refs[-4:-2], refs[-2], refs[-1]
    rows, count, columns = x_ref.shape
    images = count // len(outs)
    loads = [
        pltpu.make_async_copy(source, held.at[index], copy_sem.at[index])
        for index, source in enumerate((x_ref, ct_ref))
    ]
    for load in loads:
        load.start()

    for load, index, wide in zip(loads, range(2), wides):
        load.wait()

        def widen(row, at, index=index, wide=wide):
            for tile, low, high in lane_tiles(columns):
                wide[tile, at, : high - low] = held[index, row, :, low:high].astype(F32)

        loop_rows(rows, count, widen)

    for step, out in enumerate(outs):

        def one(index, carry, out=out, step=step):
            place = (band_ref[0] ^ step) * images + first + index
            at = pl.ds(order_ref[place], rows, stride=count + 1)
            select = table_ref[class_ref[place]]
            piece = table_ref.shape[1]
            low_lanes = lax.broadcasted_iota(jnp.int32, (piece // 2, LANE), 1) < LANE // 2
            for which, wide in enumerate(wides):
                for tile, low, high in lane_tiles(columns):
                    taken = dot_nn(select, wide[tile, at, :].astype(BF16))
                    if high - low == LANE:
                        out[which, index, :piece, low:high] = taken.astype(BF16)
                    else:
                        upper = pltpu.roll(taken[piece // 2 :], LANE // 2, 1)
                        block = jnp.where(low_lanes, taken[: piece // 2], upper)
                        fold(out, which, index, piece, block.astype(BF16))
            return carry

        lax.fori_loop(0, out.shape[1], one, 0, unroll=2)


def pack_images(x, ct, order, classes, band, bands, first, size):
    rows, count, columns = x.shape
    piece = piece_rows(bands)
    table = jnp.asarray(pack_matrix(bands), BF16)
    vmem = pl.BlockSpec(memory_space=pltpu.VMEM)
    return pl.pallas_call(
        functools.partial(pack_kernel, first),
        grid_spec=pltpu.PrefetchScalarGridSpec(
            num_scalar_prefetch=3,
            grid=(),
            in_specs=[pl.BlockSpec(memory_space=pl.ANY)] * 2 + [vmem],
            out_specs=[vmem] * bands,
            scratch_shapes=[
                pltpu.VMEM(
                    (round_up(columns, LANE) // LANE, round_up(rows, 8) * (count + 1), LANE), F32
                )
            ]
            * 2
            + [pltpu.VMEM((2, rows, count, columns), BF16), pltpu.SemaphoreType.DMA((2,))],
        ),
        out_shape=[jax.ShapeDtypeStruct((2, size) + stored_shape(piece, columns), BF16)] * bands,
        compiler_params=pltpu.CompilerParams(vmem_limit_bytes=VMEM_LIMIT),
        cost_estimate=pl.CostEstimate(flops=10_000_000, bytes_accessed=10_000_000, transcendentals=0),
    )(order, classes, band, x, ct, table)


def unpack_kernel(
    chunks, bands, order_ref, class_ref, band_ref, table_ref, low_ref, high_ref, *refs
):
    parts, targets, wides, held, copy_sem = refs[:-7], refs[-7:-5], refs[-5:-3], refs[-3:-1], refs[-1]
    images = sum(chunks)
    rows, count, columns = targets[0].shape
    piece = table_ref.shape[2]
    first = 0
    for chunk, size in enumerate(chunks):
        for step in range(bands):
            part = parts[chunk * bands + step]

            def one(index, carry, part=part, first=first, step=step):
                place = (band_ref[0] ^ step) * images + first + index
                at = pl.ds(order_ref[place], rows, stride=count + 1)
                kind = class_ref[place]
                for which, wide in enumerate(wides):
                    for tile, low, high in lane_tiles(columns):
                        if high - low == LANE:
                            made = dot_nn(table_ref[kind], part[which, index, :piece, low:high])
                        else:
                            rest = folded(part, which, index, piece)
                            made = dot_nn(low_ref[kind], rest)
                            made += pltpu.roll(dot_nn(high_ref[kind], rest), LANE // 2, 1)
                        wide[tile, at, :] = made
                return carry

            lax.fori_loop(0, size, one, 0, unroll=2)
        first += size

    for index, wide in enumerate(wides):

        def narrow(row, at, index=index, wide=wide):
            for tile, low, high in lane_tiles(columns):
                values = wide[tile, at, : high - low]
                held[index][row, :, low:high] = values.astype(held[index].dtype)

        def leave(at, index=index):
            pltpu.make_async_copy(
                held[index].at[at], targets[index].at[at], copy_sem.at[index]
            ).start()

        loop_rows(rows, count, narrow, leave)
    for index in range(2):
        pltpu.make_async_copy(held[index], targets[index], copy_sem.at[index]).wait()


def unpack_images(parts, order, classes, band, chunks, rows, columns):
    bands = len(parts[0])
    count = bands * sum(chunks)
    made = pack_matrix(bands).transpose(0, 2, 1)
    half = made.shape[2] // 2
    tables = [jnp.asarray(t, BF16) for t in (made, made[..., :half], made[..., half:])]
    vmem = pl.BlockSpec(memory_space=pltpu.VMEM)
    flat = [piece for part in parts for piece in part]
    shape = (rows, count, columns)
    wide = (round_up(columns, LANE) // LANE, round_up(rows, 8) * (count + 1), LANE)
    return pl.pallas_call(
        functools.partial(unpack_kernel, chunks, bands),
        grid_spec=pltpu.PrefetchScalarGridSpec(
            num_scalar_prefetch=3,
            grid=(),
            in_specs=[vmem] * (3 + len(flat)),
            out_specs=[pl.BlockSpec(memory_space=pl.ANY)] * 2,
            scratch_shapes=[
                pltpu.VMEM(wide, F32),
                pltpu.VMEM(wide, F32),
                pltpu.VMEM(shape, BF16),
                pltpu.VMEM(shape, F32),
                pltpu.SemaphoreType.DMA((2,)),
            ],
        ),
        out_shape=[jax.ShapeDtypeStruct(shape, BF16), jax.ShapeDtypeStruct(shape, F32)],
        compiler_params=pltpu.CompilerParams(vmem_limit_bytes=VMEM_LIMIT),
        cost_estimate=pl.CostEstimate(flops=10_000_000, bytes_accessed=16_000_000, transcendentals=0),
    )(order, classes, band, *tables, *flat)


def prep_kernel(head_ref, gate_ref, wqkv_in, wout_in, w1_in, w2t_in, *refs):
    wqkv, wback, wout, w1, w2t = refs[:5]
    places, moments = refs[5:8], refs[8:11]
    columns = wout_in.shape[0]
    width = wout.shape[0]
    heads = head_ref.shape[1]
    wback[...] = wqkv_in[...].astype(BF16)
    for part in range(3):
        low = part * width
        wqkv[:, low : low + columns] = wqkv_in[:, part * columns : (part + 1) * columns].astype(BF16)
        wqkv[:, low + columns : low + width] = jnp.zeros((columns, width - columns), BF16)
    wout[:columns, :] = wout_in[...].astype(BF16)
    wout[columns:, :] = jnp.zeros((width - columns, columns), BF16)
    for out, source in ((w1, w1_in), (w2t, w2t_in)):
        units = source.shape[1]
        out[:, :units] = source[...].astype(BF16)
        out[:, units:] = jnp.zeros((columns, out.shape[1] - units), BF16)

    for side, place, moment in zip(SIDES, places, moments):
        live, rows, lanes = side_sizes(side)

        def spots(axis, rows=rows, lanes=lanes, side=side):
            ids = lax.broadcasted_iota(jnp.int32, (rows, lanes), axis)
            spot = ids.astype(F32)
            row = jnp.floor((spot + 0.5) * (1.0 / side))
            return ids, spot - side * row, row

        key_ids, key_x, key_y = spots(0)
        query_ids, query_x, query_y = spots(1)
        delta_x, delta_y = key_x - query_x, key_y - query_y
        distance = delta_x * delta_x + delta_y * delta_y
        dead_key = key_ids >= live
        inside = (key_ids < live) & (query_ids < live)
        middle = 0.5 * (side - 1)
        from_x, from_y = key_x - middle, key_y - middle

        def one(head, carry, place=place, moment=moment, from_x=from_x, from_y=from_y):
            scores = head_ref[0, head] * delta_x + head_ref[1, head] * delta_y
            scores = jnp.where(dead_key, MASKED, scores + head_ref[2, head] * distance)
            top = jnp.max(scores, axis=0, keepdims=True)
            raised = jnp.exp(scores - top)
            total = jnp.sum(raised, axis=0, keepdims=True)
            made = jnp.where(inside, raised * (gate_ref[head] / total), 0.0)
            place[head] = made
            for row, factor in enumerate((from_x, from_y, from_x * from_x + from_y * from_y)):
                moment[head, row : row + 1, :] = jnp.sum(made * factor, axis=0, keepdims=True)
            return carry

        lax.fori_loop(0, heads, one, 0)


def prepare(w_qkv, w_out, w_fc1, w_fc2t, head_params, gate_value):
    columns, heads = w_out.shape[0], head_params.shape[1]
    width = round_up(columns, LANE)
    padded = round_up(w_fc1.shape[1], 256)
    vmem = pl.BlockSpec(memory_space=pltpu.VMEM)
    smem = pl.BlockSpec(memory_space=pltpu.SMEM)
    shapes = [
        (columns, 3 * width),
        (columns, 3 * columns),
        (width, columns),
        (columns, padded),
        (columns, padded),
    ]
    outs = [jax.ShapeDtypeStruct(shape, BF16) for shape in shapes]
    outs += [jax.ShapeDtypeStruct((heads,) + side_sizes(side)[1:], F32) for side in SIDES]
    outs += [jax.ShapeDtypeStruct((heads, 8, side_sizes(side)[2]), F32) for side in SIDES]
    made = pl.pallas_call(
        prep_kernel,
        out_shape=outs,
        in_specs=[smem, smem] + [vmem] * 4,
        out_specs=[vmem] * len(outs),
        compiler_params=pltpu.CompilerParams(vmem_limit_bytes=VMEM_LIMIT),
        cost_estimate=pl.CostEstimate(
            flops=50_000_000, bytes_accessed=22_000_000, transcendentals=2_000_000
        ),
    )(head_params, gate_value, w_qkv, w_out, w_fc1, w_fc2t)
    return made[:5], made[5:8], made[8:]


def reduce_plan(tile_total, devices):
    each = -(-tile_total // devices)
    weight = sum(wave[1] for wave in WAVES)
    waves = []
    base = before = taken = 0
    for order, part in WAVES:
        before += part
        share = -(-each * before // weight) - taken
        if share:
            waves.append((base, share, order))
            base += devices * share
            taken += share
    return waves, each * devices


def reduce_kernel(
    waves,
    rank_z,
    own_ref,
    small_ref,
    full_out,
    small_out,
    own,
    full,
    recv0,
    recv1,
    small_own,
    small_recv,
    send_sem,
    recv_sem,
    small_send,
    small_got,
    copy_sem,
):
    img = lax.axis_index("img")
    band = lax.axis_index("band")
    z, y = img // 2, img % 2
    x, c = band // 2, band % 2
    low_z, high_z = z % 2, z // 2
    high_count = rank_z // 2
    mesh_ids = pl.DeviceIdType.MESH
    axes = {
        "c": (c, 2, lambda k: (img, x * 2 + 1 - c)),
        "y": (y, 2, lambda k: (z * 2 + 1 - y, band)),
        "x": (x, 2, lambda k: (img, (1 - x) * 2 + c)),
        "l": (low_z, 2, lambda k: ((high_z * 2 + 1 - low_z) * 2 + y, band)),
        "h": (
            high_z,
            high_count,
            lambda k: ((lax.rem(high_z + k, high_count) * 2 + low_z) * 2 + y, band),
        ),
    }
    order = [name for name in "cyxlh" if axes[name][1] > 1]
    partners = [axes[name][2](k) for name in order for k in range(1, axes[name][1])]
    devices = 1
    for name in order:
        devices *= axes[name][1]

    loads = []
    for w, (base, share, _) in enumerate(waves):
        at = pl.ds(base, devices * share)
        loads.append(pltpu.make_async_copy(own_ref.at[at], own.at[at], copy_sem.at[w]))
        loads[-1].start()
    small_own[...] = small_ref[...]

    barrier = pltpu.get_barrier_semaphore()
    for partner in partners:
        pl.semaphore_signal(barrier, inc=1, device_id=partner, device_id_type=mesh_ids)
    pl.semaphore_wait(barrier, len(partners))

    counters = [0] * len(waves)

    def send(wave, src, dst, target):
        slot = counters[wave]
        counters[wave] += 1
        copy = pltpu.make_async_remote_copy(
            src_ref=src,
            dst_ref=dst,
            send_sem=send_sem.at[wave, slot],
            recv_sem=recv_sem.at[wave, slot],
            device_id=target,
            device_id_type=mesh_ids,
        )
        copy.start()
        return copy

    def add_tiles(dst, dst_at, parts, count, out, out_at):
        block = 8

        def one(offset, size):
            total = dst[pl.ds(dst_at + offset, size)].astype(F32)
            for ref, at in parts:
                total += ref[pl.ds(at + offset, size)].astype(F32)
            out[pl.ds(out_at + offset, size)] = total.astype(BF16)

        if count >= block:

            def step(index, carry):
                one(index * block, block)
                return carry

            lax.fori_loop(0, count // block, step, 0)
        rest = count % block
        if rest:
            one(count - rest, rest)

    stores = []

    def wave_stages(w):
        base, share, axis_order = waves[w]
        order = [name for name in axis_order if axes[name][1] > 1]
        state = {"at": base, "size": devices * share, "copies": [], "parts": []}
        taken = [base // 2]

        def finish():
            for copy in state["copies"]:
                copy.wait()

        def scatter(name):
            def run():
                if state["parts"]:
                    finish()
                    add_tiles(own, state["at"], state["parts"], state["size"], own, state["at"])
                else:
                    loads[w].wait()
                mine, count, target = axes[name]
                size = state["size"] // count
                state["copies"], state["parts"] = [], []
                for k in range(1, count):
                    other = lax.rem(mine + k, count)
                    if name == order[0]:
                        buffer, at = recv0, base // 2
                    else:
                        buffer, at = recv1, taken[0]
                        taken[0] += size
                    state["copies"].append(
                        send(
                            w,
                            own.at[pl.ds(state["at"] + other * size, size)],
                            buffer.at[pl.ds(at, size)],
                            target(k),
                        )
                    )
                    state["parts"].append((buffer, at))
                state["at"] = state["at"] + mine * size
                state["size"] = size

            return run

        def gather(name, first):
            def run():
                finish()
                if first:
                    at = state["at"]
                    add_tiles(own, at, state["parts"], state["size"], full, at)
                mine, count, target = axes[name]
                piece = full.at[pl.ds(state["at"], state["size"])]
                state["copies"] = [send(w, piece, piece, target(k)) for k in range(1, count)]
                state["at"] = state["at"] - mine * state["size"]
                state["size"] = state["size"] * count

            return run

        def close():
            finish()
            at = pl.ds(base, devices * share)
            stores.append(
                pltpu.make_async_copy(full.at[at], full_out.at[at], copy_sem.at[len(waves) + w])
            )
            stores[-1].start()

        steps = [scatter(name) for name in order]
        steps += [gather(name, name == order[-1]) for name in reversed(order)]
        return steps + [close]

    small_slots = [0]
    small_state = {}

    def small_start(name):
        mine, count, target = axes[name]
        first = small_slots[0]
        small_slots[0] += count - 1
        small_state["copies"] = []
        for k in range(1, count):
            slot = first + k - 1
            copy = pltpu.make_async_remote_copy(
                src_ref=small_own,
                dst_ref=small_recv.at[slot],
                send_sem=small_send.at[slot],
                recv_sem=small_got.at[slot],
                device_id=target(k),
                device_id_type=mesh_ids,
            )
            copy.start()
            small_state["copies"].append(copy)
        small_state["first"] = first

    def small_end(name):
        mine, count, _ = axes[name]
        first = small_state["first"]
        for copy in small_state["copies"]:
            copy.wait()
        if count == 2:
            small_own[...] = small_own[...] + small_recv[first]
        else:
            last = small_recv.shape[0] - 1
            small_recv[last] = small_own[...]

            def add_line(index, total):
                k = lax.rem(mine - index + count, count)
                slot = jnp.where(k == 0, last, first + k - 1)
                return total + small_recv[slot]

            small_own[...] = lax.fori_loop(0, count, add_line, jnp.zeros_like(small_own))

    programs = [wave_stages(w) for w in range(len(waves))]
    depth = len(programs[0])
    for program in programs:
        program[0]()
    for time in range(1, max(depth, len(order) + 2)):
        if time < depth:
            for program in programs:
                program[time]()
        if 1 <= time <= len(order) + 1:
            if time > 1:
                small_end(order[time - 2])
            if time <= len(order):
                small_start(order[time - 1])
    small_out[...] = small_own[...]
    for store in stores:
        store.wait()


def reduce_all(tiles, small, waves, img_count):
    total = tiles.shape[0]
    rank_z = img_count // 2
    copies = 2 * (4 + max(rank_z // 2 - 1, 0))
    hops = 4 + max(rank_z // 2 - 1, 0)
    return pl.pallas_call(
        functools.partial(reduce_kernel, waves, rank_z),
        out_shape=[
            jax.ShapeDtypeStruct(tiles.shape, BF16),
            jax.ShapeDtypeStruct(small.shape, F32),
        ],
        in_specs=[pl.BlockSpec(memory_space=pl.ANY), pl.BlockSpec(memory_space=pltpu.VMEM)],
        out_specs=[pl.BlockSpec(memory_space=pl.ANY), pl.BlockSpec(memory_space=pltpu.VMEM)],
        scratch_shapes=[
            pltpu.VMEM(tiles.shape, BF16),
            pltpu.VMEM(tiles.shape, BF16),
            pltpu.VMEM((total // 2, SUB, LANE), BF16),
            pltpu.VMEM((total // 2, SUB, LANE), BF16),
            pltpu.VMEM(small.shape, F32),
            pltpu.VMEM((hops + 1,) + small.shape, F32),
            pltpu.SemaphoreType.DMA((len(waves), copies)),
            pltpu.SemaphoreType.DMA((len(waves), copies)),
            pltpu.SemaphoreType.DMA((hops,)),
            pltpu.SemaphoreType.DMA((hops,)),
            pltpu.SemaphoreType.DMA((2 * len(waves),)),
        ],
        compiler_params=pltpu.CompilerParams(
            collective_id=1, has_side_effects=True, vmem_limit_bytes=VMEM_LIMIT
        ),
        cost_estimate=pl.CostEstimate(
            flops=10_000_000, bytes_accessed=200_000_000, transcendentals=0
        ),
    )(tiles, small)


def update_kernel(
    decay_rate,
    head_count,
    widths,
    tiles_ref,
    small_ref,
    weight_hbm,
    line_refs,
    vector_refs,
    moment_refs,
    norm_out,
    grad_hbm,
    new_hbm,
    vgrad_outs,
    vnew_outs,
    line_outs,
    moment_outs,
    weights,
    grads,
    news,
    row_s,
    col_s,
    copy_sem,
):
    columns = weights[0].shape[0]
    row_tiles = columns // SUB
    spans = [-(-wide // LANE) for wide in widths]
    total_span = tiles_stride(widths)
    starts = []
    at = 0
    for wide in widths:
        starts.append(at)
        at += tile_span(wide)
    loads = [
        pltpu.make_async_copy(weight_hbm[i], weights[i], copy_sem.at[i]) for i in range(4)
    ]
    for load in loads:
        load.start()

    def tile_rows(index, which):
        place = index * total_span + starts[which]
        pieces = [tiles_ref[place + col].astype(F32) for col in range(spans[which])]
        whole = jnp.concatenate(pieces, axis=1) if len(pieces) > 1 else pieces[0]
        return whole[:, : widths[which]]

    def all_sum(values):
        return jnp.sum(jnp.sum(values, axis=0, keepdims=True), axis=1, keepdims=True)

    def measure(index, carry):
        at = pl.ds(pl.multiple_of(index * SUB, SUB), SUB)
        made = []
        for which in range(4):
            grad = tile_rows(index, which)
            square = grad * grad
            row_s[which, at, :] = jnp.sum(square, axis=1, keepdims=True)
            made.append(carry[which] + fold_rows(square))
        return tuple(made)

    zeros = tuple(jnp.zeros((8, wide), F32) for wide in widths)
    folded = lax.fori_loop(0, row_tiles, measure, zeros)
    col_squares = [jnp.sum(fold, axis=0, keepdims=True) for fold in folded]
    total = jnp.zeros((1, 1), F32)
    for square in col_squares:
        total += jnp.sum(square, axis=1, keepdims=True)

    parts = vector_refs[2].shape[0]
    places = (
        (slice(0, 2), columns),
        (slice(2, 6), columns),
        (slice(6, 6 + parts), columns),
        (slice(6 + parts, 10 + parts), head_count),
    )
    vectors = [small_ref[rows, :wide] for rows, wide in places]
    for grad in vectors:
        total += all_sum(grad * grad)
    norm = jnp.sqrt(total)
    norm_out[...] = norm
    factor = 1.0 / jnp.maximum(norm, 1.0)

    for index in range(4):
        grad = vectors[index] * factor
        weight = vector_refs[index][...]
        moment = decay_rate * moment_refs[index][...] + (1.0 - decay_rate) * (
            grad * grad + FLOOR_ONE
        )
        update = grad * lax.rsqrt(moment)
        size = weight.shape[0] * weight.shape[1]
        mean_square = all_sum(update * update) / size
        update = update / jnp.maximum(1.0, jnp.sqrt(mean_square) / CLIP_RMS)
        scale = STEP_RATE * jnp.maximum(FLOOR_TWO, jnp.sqrt(all_sum(weight * weight) / size))
        vgrad_outs[index][...] = grad
        vnew_outs[index][...] = weight - scale * update
        moment_outs[index][...] = moment

    row_factors, col_factors = [], []
    for which in range(4):
        wide = widths[which]
        down_old, along_old = line_refs[which]
        down_out, along_out = line_outs[which]
        down = jnp.broadcast_to(down_old[...].reshape(1, columns), (LANE, columns)).T
        down = decay_rate * down + (1.0 - decay_rate) * (
            row_s[which] * (factor * factor) / wide + FLOOR_ONE
        )
        along = decay_rate * along_old[...].reshape(1, wide) + (1.0 - decay_rate) * (
            col_squares[which] * (factor * factor) / columns + FLOOR_ONE
        )
        down_out[...] = down.T[:1, :].reshape(columns)
        along_out[...] = along.reshape(wide)
        down = down[:, :1]
        if which == 3:
            along = along / (jnp.sum(along, axis=1, keepdims=True) / wide)
        else:
            down = down / (jnp.sum(down, axis=0, keepdims=True) / columns)
        row_s[which] = lax.rsqrt(down) * factor
        col_s[which, :, :wide] = lax.rsqrt(along)

    for load in loads:
        load.wait()

    def scan(index, carry):
        at = pl.ds(pl.multiple_of(index * SUB, SUB), SUB)
        made = []
        for which in range(4):
            wide = widths[which]
            update = tile_rows(index, which) * col_s[which, :, :wide] * row_s[which, at, :]
            weight = weights[which][at, :]
            made.append(carry[2 * which] + fold_rows(update * update))
            made.append(carry[2 * which + 1] + fold_rows(weight * weight))
        return tuple(made)

    sums = lax.fori_loop(0, row_tiles, scan, tuple(z for z in zeros for _ in range(2)))
    stores = []
    for which in (2, 3, 0, 1):
        wide = widths[which]
        size = columns * wide
        scale = STEP_RATE * jnp.maximum(FLOOR_TWO, jnp.sqrt(all_sum(sums[2 * which + 1]) / size))
        scale = scale / jnp.maximum(1.0, jnp.sqrt(all_sum(sums[2 * which]) / size) / CLIP_RMS)
        col_factor = col_s[which, :, :wide] * scale

        def write(index, carry, which=which, col_factor=col_factor):
            at = pl.ds(pl.multiple_of(index * SUB, SUB), SUB)
            grad = tile_rows(index, which)
            grads[which][at, :] = grad * factor
            news[which][at, :] = weights[which][at, :] - grad * col_factor * row_s[which, at, :]
            return carry

        lax.fori_loop(0, row_tiles, write, 0)
        for source, target, slot in (
            (grads[which], grad_hbm[which], 4 + which),
            (news[which], new_hbm[which], 8 + which),
        ):
            stores.append(pltpu.make_async_copy(source, target, copy_sem.at[slot]))
            stores[-1].start()
    for store in stores:
        store.wait()


def tile_span(wide):
    return round_up(wide, 256 if wide > 1500 else LANE) // LANE


def tiles_stride(widths):
    return sum(tile_span(wide) for wide in widths)


def update_all(tiles, small, weights, rows, cols, vectors, moments, decay_rate):
    columns = weights[1].shape[0]
    head_count = vectors[3].shape[1]
    units = weights[2].shape[1]
    parts = units // columns
    lines = [[r, c] for r, c in zip(rows, cols)]
    lines[3] = lines[3][::-1]
    vectors = [v.reshape(parts, columns) if v.ndim == 1 else v for v in vectors]
    moments = [v.reshape(parts, columns) if v.ndim == 1 else v for v in moments]
    widths = [weight.shape[1] for weight in weights]
    like = lambda group: [jax.ShapeDtypeStruct(v.shape, F32) for v in group]
    outs = [
        jax.ShapeDtypeStruct((1, 1), F32),
        like(weights),
        like(weights),
        like(vectors),
        like(vectors),
        [like(pair) for pair in lines],
        like(vectors),
    ]
    vmem = pl.BlockSpec(memory_space=pltpu.VMEM)
    hbm = pl.BlockSpec(memory_space=pl.ANY)
    args = (tiles, small, list(weights), lines, vectors, moments)
    in_specs = list(jax.tree.map(lambda _: vmem, args))
    in_specs[2] = [hbm] * 4
    out_specs = jax.tree.map(lambda _: vmem, outs)
    out_specs[1] = [hbm] * 4
    out_specs[2] = [hbm] * 4
    full = lambda: [pltpu.VMEM(weight.shape, F32) for weight in weights]
    scratch = [
        full(),
        full(),
        full(),
        pltpu.VMEM((4, columns, 1), F32),
        pltpu.VMEM((4, 1, round_up(max(widths), LANE)), F32),
        pltpu.SemaphoreType.DMA((12,)),
    ]
    made = pl.pallas_call(
        functools.partial(update_kernel, decay_rate, head_count, widths),
        out_shape=outs,
        in_specs=in_specs,
        out_specs=out_specs,
        scratch_shapes=scratch,
        compiler_params=pltpu.CompilerParams(vmem_limit_bytes=VMEM_LIMIT),
    )(*args)
    norm, grads, news, vgrads, vnews, line_new, moment_new = made
    spread = lambda group: [v.reshape(-1) if i == 2 else v for i, v in enumerate(group)]
    line_new[3] = line_new[3][::-1]
    moved = [line for pair in line_new for line in pair]
    grads[3], news[3] = grads[3].T, news[3].T
    return (
        norm.reshape(1),
        *grads,
        *spread(vgrads),
        *news,
        *spread(vnews),
        *moved,
        *spread(moment_new),
    )


def deal_images(grid_sizes, devices):
    count = grid_sizes.shape[0]
    ids = jnp.arange(count, dtype=jnp.int32)
    ahead = (grid_sizes[None, :] > grid_sizes[:, None]) | (
        (grid_sizes[None, :] == grid_sizes[:, None]) & (ids[None, :] < ids[:, None])
    )
    rank = jnp.sum(ahead.astype(jnp.int32), axis=1)
    turn = rank // devices
    seat = rank % devices
    seat = jnp.where(turn % 2 == 0, seat, devices - 1 - seat)
    place = seat * (count // devices) + turn
    hit = place[None, :] == ids[:, None]
    order = jnp.sum(jnp.where(hit, ids[None, :], 0), axis=1)
    sizes = jnp.sum(jnp.where(hit, grid_sizes[None, :], 0), axis=1)
    return order, sizes


def per_device(
    inputs,
    cotangent,
    grid_sizes,
    w_qkv,
    w_out,
    w_fc1,
    w_fc2,
    norm_gains,
    biases,
    fc1_bias,
    head_params,
    rows_qkv,
    cols_qkv,
    rows_out,
    cols_out,
    rows_fc1,
    cols_fc1,
    rows_fc2,
    cols_fc2,
    gain_moment,
    bias_moment,
    fc1_bias_moment,
    head_moment,
):
    band_count = lax.axis_size("band")
    img_count = lax.axis_size("img")
    band_index = lax.axis_index("band")
    columns = inputs.shape[2]
    units = w_fc1.shape[1]
    per_band = inputs.shape[0] // band_count
    order, sizes_ordered = deal_images(grid_sizes, band_count)
    classes = sum(
        (jnp.where(sizes_ordered == side, index, 0) for index, side in enumerate(SIDES)),
        jnp.zeros_like(order),
    )
    sizes_used = lax.dynamic_slice_in_dim(sizes_ordered, band_index * per_band, per_band)
    early = max(1, per_band // 2)
    chunks = (early, per_band - early)
    band = band_index.astype(jnp.int32).reshape(1)
    x_stored, ct_stored = jnp.swapaxes(inputs, 0, 1), jnp.swapaxes(cotangent, 0, 1)
    pack = lambda first, size: pack_images(
        x_stored, ct_stored, order, classes, band, band_count, first, size
    )

    def exchange(parts):
        swaps = [[(i, i ^ step) for i in range(band_count)] for step in range(band_count)]
        return [parts[0]] + [
            lax.ppermute(parts[step], "band", swaps[step]) for step in range(1, band_count)
        ]

    waves, tile_count = reduce_plan(
        (columns // SUB) * tiles_stride((3 * columns, columns, units, units)),
        band_count * img_count,
    )
    w_fc2t = w_fc2.T
    gate_value = jax.nn.sigmoid(head_params[3])
    matrices, places, spots = prepare(w_qkv, w_out, w_fc1, w_fc2t, head_params, gate_value)
    first_part = pack(0, early)
    first_moved = exchange(first_part)
    later_part = pack(early, per_band - early)
    later_part, matrices, first_moved = lax.optimization_barrier(
        (later_part, matrices, first_moved)
    )
    moved = [first_moved, exchange(later_part)]
    fc1b = jnp.pad(fc1_bias[None, :], ((0, 0), (0, matrices[3].shape[1] - units)))
    shared = (places, spots, 1.0 - gate_value, matrices, norm_gains, biases, fc1b)
    previous = None
    start = 0
    results = []
    for part, size in zip(moved, chunks):
        result, *previous = run_images(
            part, sizes_used, start, band, shared, previous, units, tile_count
        )
        results.append(result)
        start += size
    tiles, small = previous
    results[0], tiles = lax.optimization_barrier((exchange(results[0]), tiles))
    full, small = reduce_all(tiles, small, waves, img_count)
    results[1], full = lax.optimization_barrier((results[1], full))
    results[1] = exchange(results[1])
    updated = update_all(
        full,
        small,
        (w_qkv, w_out, w_fc1, w_fc2t),
        (rows_qkv, rows_out, rows_fc1, rows_fc2),
        (cols_qkv, cols_out, cols_fc1, cols_fc2),
        (norm_gains, biases, fc1_bias, head_params),
        (gain_moment, bias_moment, fc1_bias_moment, head_moment),
        1.0 - STEP ** (-0.8),
    )
    output, input_grad = unpack_images(
        results, order, classes, band, chunks, inputs.shape[1], columns
    )
    return (jnp.swapaxes(output, 0, 1), jnp.swapaxes(input_grad, 0, 1), *updated)


def solution(mesh):
    split = P("img", "band", None)
    return jax.shard_map(
        per_device,
        mesh=mesh,
        in_specs=(split, split, P("img")) + (P(),) * 20,
        out_specs=(split, split) + (P(),) * 29,
        check_vma=False,
    )
```

```python
import functools
import math

import jax
import jax.numpy as jnp
import numpy as np
from jax import lax
from jax.experimental import pallas as pl
from jax.experimental.pallas import tpu as pltpu
from jax.sharding import PartitionSpec as P

GRID = 20
STEP = 10
SIDES = (18, 14, 10)

NORM_FLOOR = 1e-06
FLOOR_ONE = 1e-30
FLOOR_TWO = 0.001
STEP_RATE = 0.6
CLIP_RMS = 1.0
MASKED = -1e30

BF16 = jnp.bfloat16
F32 = jnp.float32
VMEM_LIMIT = 60 * 1024 * 1024
SUB = 16
SMALL_ROWS = 16
WAVES = (
    ("cyxlh", 6),
    ("cxylh", 6),
    ("clhxy", 3),
    ("clhyx", 3),
    ("cyxlh", 6),
    ("cxylh", 6),
    ("clhxy", 3),
    ("clhyx", 4),
)
LANE = 128


def round_up(value, unit):
    return (value + unit - 1) // unit * unit


def side_sizes(side):
    live = side * side
    return live, round_up(live, SUB), round_up(live, LANE)


def dot_nn(left, right):
    return lax.dot_general(left, right, (((1,), (0,)), ((), ())), preferred_element_type=F32)


def dot_nt(left, right):
    return lax.dot_general(left, right, (((1,), (1,)), ((), ())), preferred_element_type=F32)


def piece_rows(bands):
    return round_up(GRID // bands * max(SIDES), SUB)


def select_matrix(side, bands):
    live, rows, _ = side_sizes(side)
    tall, piece = GRID // bands, piece_rows(bands)
    made = np.zeros((rows, bands * piece), np.float32)
    for row in range(side):
        for col in range(side):
            at = row // tall * piece + (row % tall) * side + col
            made[row * side + col, at] = 1.0
    return made


def select_matrices(side, bands):
    made = select_matrix(side, bands).reshape(-1, bands, piece_rows(bands))
    ordered = [made[:, [own ^ step for step in range(bands)]] for own in range(bands)]
    return np.stack(ordered).reshape(bands, made.shape[0], -1)


def rest_matrices(side, bands):
    piece = piece_rows(bands)
    made = select_matrices(side, bands).reshape(bands, -1, bands, piece)
    halves = [made[..., : piece // 2], made[..., piece // 2 :]]
    return np.stack([half.reshape(bands, made.shape[1], -1) for half in halves], axis=1)


def stored_shape(piece, columns):
    main = columns // LANE * LANE
    return piece + piece // 2 * LANE // main, main


def folded(ref, which, index, piece):
    rows, main = ref.shape[2:]
    pieces = [ref[which, index, piece:, low : low + LANE] for low in range(0, main, LANE)]
    return jnp.concatenate(pieces, axis=0)


def fold(ref, which, index, piece, block):
    rows, main = ref.shape[2:]
    each = rows - piece
    for tile in range(main // LANE):
        at = slice(tile * LANE, (tile + 1) * LANE)
        ref[which, index, piece:, at] = block[tile * each : (tile + 1) * each]


def pack_matrix(bands):
    tall, piece = GRID // bands, piece_rows(bands)
    made = np.zeros((len(SIDES), piece, tall * GRID), np.float32)
    for index, side in enumerate(SIDES):
        for row in range(tall):
            for col in range(side):
                made[index, row * side + col, row * GRID + col] = 1.0
    return made


def fold_rows(values):
    rows, columns = values.shape
    return jnp.sum(values.reshape(rows // 8, 8, columns), axis=0)


def image_kernel(
    columns,
    heads,
    hidden_units,
    image_count,
    started,
    sizes_ref,
    band_ref,
    gate_ref,
    xct_refs,
    tiles_in,
    small_in,
    sel_refs,
    selt_refs,
    rest_refs,
    restt_refs,
    place_hbm,
    moment_refs,
    weight_hbm,
    gains_ref,
    biases_ref,
    fc1b_ref,
    outig_refs,
    tiles_ref,
    small_ref,
    proj_s,
    projt_s,
    da_s,
    dat_s,
    cont_s,
    mix_s,
    attt_s,
    gt_s,
    act_s,
    gb_s,
    vec_s,
    fc1g_s,
    racc_s,
    gqkv_ref,
    gout_ref,
    g1_ref,
    g2t_ref,
    gsum_refs,
    gm_refs,
    gc_refs,
    second_s,
    ct_s,
    secondt_s,
    ctt_s,
    place_refs,
    weight_refs,
    copy_sem,
):
    wqkv_ref, wback_ref, wout_ref, w1_ref, w2t_ref = weight_refs
    step = pl.program_id(0)
    steps = pl.num_programs(0)
    head_size = columns // heads
    width = wqkv_ref.shape[1] // 3
    window = 256
    score_scale = head_size ** (-0.5)
    chunk = 256
    chunks = w1_ref.shape[1] // chunk

    table = (gqkv_ref, gout_ref, g1_ref, g2t_ref)
    across = sum(ref.shape[1] // LANE for ref in table)
    row_tiles = columns // SUB

    sources = list(weight_hbm) + list(place_hbm)
    targets = list(weight_refs) + list(place_refs)
    loads = [
        pltpu.make_async_copy(source, target, copy_sem.at[1 + index])
        for index, (source, target) in enumerate(zip(sources, targets))
    ]
    load_qkv, load_back, load_out, load_w1, load_w2 = loads[:5]
    load_places = loads[5:]

    def once(*copies):
        @pl.when(step == 0)
        def _():
            for copy in copies:
                copy.wait()

    @pl.when(step == 0)
    def _():
        if started:
            load = pltpu.make_async_copy(tiles_in, tiles_ref, copy_sem.at[0])
            load.start()
        for copy in [load_qkv] + load_places + [load_out, load_w1, load_w2, load_back]:
            copy.start()
        if started:
            load.wait()

            def absorb(index, carry):
                at = pl.ds(pl.multiple_of(index * SUB, SUB), SUB)
                place = index * across
                for ref in table:
                    for col in range(ref.shape[1] // LANE):
                        ref[at, col * LANE : (col + 1) * LANE] = tiles_ref[place].astype(F32)
                        place = place + 1
                return carry

            lax.fori_loop(0, row_tiles, absorb, 0)
        else:
            for ref in table:
                ref[...] = jnp.zeros_like(ref)
        vec_s[...] = jnp.zeros_like(vec_s)
        fc1g_s[...] = jnp.zeros_like(fc1g_s)
        racc_s[...] = jnp.zeros_like(racc_s)
        for ref in gsum_refs:
            ref[...] = jnp.zeros_like(ref)

    def aligned(value, unit):
        return value if isinstance(value, int) else pl.multiple_of(value, unit)

    def head_place(head):
        first_lane = head * head_size
        if isinstance(head, int):
            start = min(first_lane // LANE * LANE, width - window)
        else:
            start = jnp.minimum(first_lane // LANE * LANE, width - window)
        lanes = lax.broadcasted_iota(jnp.int32, (1, window), 1) + start
        mask = (lanes >= first_lane) & (lanes < first_lane + head_size)
        return start, mask

    def part_lanes(part, start):
        return pl.ds(aligned(part * width + start, LANE), window)

    def head_rows(part, head):
        return pl.ds(aligned(part * columns + head * head_size, SUB), head_size)

    def skewed(compact, enter, middle, leave):
        if not compact:
            for index in range(heads + 2):
                if index < heads:
                    enter(index, index % 2)
                if 1 <= index <= heads:
                    middle(index - 1, (index - 1) % 2)
                if index >= 2:
                    leave(index - 2, index % 2)
            return
        enter(0, 0)

        def pair(index, carry):
            for odd in range(2):
                head = index * 2 + odd
                leave(jnp.maximum(head - 1, 0), 1 - odd)
                enter(head + 1, 1 - odd)
                middle(head, odd)
            return carry

        pairs = (heads - 1) // 2
        lax.fori_loop(0, pairs, pair, 0)
        for head in range(2 * pairs, heads):
            leave(head - 1, (head - 1) % 2)
            if head + 1 < heads:
                enter(head + 1, (head + 1) % 2)
            middle(head, head % 2)
        leave(heads - 1, (heads - 1) % 2)

    def image(side, sel_ref, selt_ref, rest_ref, restt_ref, place_ref, gsum_ref):
        live, rows, lanes = side_sizes(side)
        edge = live // 8 * 8
        compact = (side != SIDES[0]) != started
        tall = sel_ref.shape[2] // len(xct_refs)
        main = xct_refs[0].shape[3]

        def gathered(which):
            pieces = jnp.concatenate([ref[which, 0, :tall] for ref in xct_refs], axis=0)
            blocks = [folded(ref, which, 0, tall) for ref in xct_refs]
            block = jnp.concatenate(blocks, axis=0)
            rest = dot_nn(rest_ref[0, 0], block)
            rest += pltpu.roll(dot_nn(rest_ref[0, 1], block), LANE // 2, 1)
            return jnp.concatenate(
                [dot_nn(sel_ref[0], pieces), rest[:, : columns - main]], axis=1
            )

        def spread(which, values):
            values = values.astype(BF16)
            fill = jnp.zeros((rows, LANE - (columns - main)), BF16)
            rest = jnp.concatenate([values[:, main:], fill], axis=1)
            values = dot_nn(selt_ref[0], values[:, :main]).astype(BF16)
            block = dot_nn(restt_ref[0, 0], rest)
            block += pltpu.roll(dot_nn(restt_ref[0, 1], rest), LANE // 2, 1)
            block = block.astype(BF16)
            for index, ref in enumerate(outig_refs):
                ref[which, 0, :tall] = values[index * tall : (index + 1) * tall]
                half = tall // 2
                fold(ref, which, 0, tall, block[index * half : (index + 1) * half])

        def norm(values):
            averaged = jnp.mean(values, axis=-1, keepdims=True)
            centered = values - averaged
            variance = jnp.mean(centered * centered, axis=-1, keepdims=True)
            inverse = lax.rsqrt(variance + NORM_FLOOR)
            return centered * inverse, inverse

        def norm_back(grad, unit, inverse, gain):
            scaled = grad * gain
            first_mean = jnp.mean(scaled, axis=-1, keepdims=True)
            second_mean = jnp.mean(scaled * unit, axis=-1, keepdims=True)
            return inverse * (scaled - first_mean - unit * second_mean)

        x = gathered(0)
        unit_one, inverse_one = norm(x)
        first_b = (unit_one * gains_ref[0:1, :] + biases_ref[0:1, :]).astype(BF16)
        once(load_qkv)
        proj_s[:rows, :] = dot_nn(first_b, wqkv_ref[...]).astype(BF16)
        once(*load_places)
        if lanes > rows:
            proj_s[rows:lanes, :] = jnp.zeros((lanes - rows, 3 * width), BF16)
        for part in range(3):
            piece = proj_s[:lanes, part * width : (part + 1) * width]
            projt_s[part, :, :lanes] = piece.T

        tops = {}

        def score_head(head, slot):
            start, mask = head_place(head)
            query = jnp.where(mask, proj_s[:lanes, part_lanes(0, start)], 0)
            key = proj_s[:rows, part_lanes(1, start)]
            score = dot_nt(key, query)
            tail = lax.broadcasted_iota(jnp.int32, (rows - edge, lanes), 0) < live - edge
            score = jnp.concatenate(
                [score[:edge], jnp.where(tail, score[edge:], MASKED)], axis=0
            )
            gm_refs[slot][:rows, :lanes] = score
            if not compact:
                tops[head] = jnp.max(score, axis=0, keepdims=True)

        def soft_head(head, slot):
            factor = score_scale * math.log2(math.e)
            score = gm_refs[slot][:rows, :lanes]
            top = jnp.max(score, axis=0, keepdims=True) if compact else tops[head]
            raised = jnp.exp2(score * factor - top * factor)
            total = jnp.sum(raised, axis=0, keepdims=True)
            content = raised * (gate_ref[head] / total)
            cont_s[head, :rows, :lanes] = content
            mix_s[head, :rows, :lanes] = (content + place_ref[head]).astype(BF16)

        def attend_head(head, slot):
            here = head_rows(0, head)
            value_t = projt_s[2, here, :rows]
            mixed = mix_s[head, :rows, :lanes]
            attt_s[here, :lanes] = dot_nn(value_t, mixed).astype(BF16)

        skewed(compact, score_head, soft_head, attend_head)

        once(load_out, load_w1, load_w2, load_back)
        attended = attt_s[:, :lanes].T[:rows]
        hidden = x + (dot_nn(attended, wout_ref[:columns, :]) + biases_ref[2:3, :])
        unit_two, inverse_two = norm(hidden)
        second_b = (unit_two * gains_ref[1:2, :] + biases_ref[1:2, :]).astype(BF16)
        ct_b = gathered(1).astype(BF16)

        second_s[:rows, :] = second_b
        ct_s[:rows, :] = ct_b

        def mlp_chunk(index):
            at = pl.ds(aligned(index * chunk, chunk), chunk)
            before = dot_nn(second_s[:rows, :], w1_ref[:, at]) + fc1b_ref[:, at]
            grad_act = dot_nn(ct_s[:rows, :], w2t_ref[:, at])
            square = before * before
            inner = before * (
                math.sqrt(2.0 / math.pi) + (math.sqrt(2.0 / math.pi) * 0.044715) * square
            )
            half = 0.5 * jnp.tanh(inner) + 0.5
            activated = before * half
            slope = half + activated * (1.0 - half) * (
                2.0 * math.sqrt(2.0 / math.pi)
                + (6.0 * math.sqrt(2.0 / math.pi) * 0.044715) * square
            )
            act_s[:rows, at] = activated.astype(BF16)
            grad_b = (grad_act * slope).astype(BF16)
            gb_s[:rows, at] = grad_b
            fc1g_s[:, at] += fold_rows(grad_b.astype(F32))

        def weight_chunk(index):
            at = pl.ds(aligned(index * chunk, chunk), chunk)
            g1_ref[:, at] += dot_nn(secondt_s[:, :rows], gb_s[:rows, at])
            g2t_ref[:, at] += dot_nn(ctt_s[:, :rows], act_s[:rows, at])

        def mlp_step(index, carry):
            weight_chunk(index - 1)
            mlp_chunk(index)
            return carry

        if compact:
            ctt_s[:, :rows] = ct_b.T
            secondt_s[:, :rows] = second_b.T
            mlp_chunk(0)
            lax.fori_loop(1, chunks, mlp_step, 0)
            weight_chunk(chunks - 1)
        else:
            for index in range(chunks):
                mlp_chunk(index)

        result = (
            hidden + dot_nt(act_s[:rows, :], w2t_ref[...]) + biases_ref[3:4, :]
        )
        spread(0, result)

        if not compact:
            ct_t = ct_b.T
            second_t = second_b.T
            for index in range(chunks):
                low, high = index * chunk, min((index + 1) * chunk, hidden_units)
                g1_ref[:, low:high] += dot_nn(second_t, gb_s[:rows, low:high])
                g2t_ref[:, low:high] += dot_nn(ct_t, act_s[:rows, low:high])

        ct_f = ct_b.astype(F32)
        grad_second = dot_nt(gb_s[:rows, :], w1_ref[...])
        grad_hidden = ct_f + norm_back(grad_second, unit_two, inverse_two, gains_ref[1:2, :])
        branch_b = grad_hidden.astype(BF16)
        vec_s[1] += fold_rows(grad_second * unit_two)
        vec_s[3] += fold_rows(grad_second)
        vec_s[4] += fold_rows(branch_b.astype(F32))
        vec_s[5] += fold_rows(ct_f)
        gout_ref[:, :columns] += dot_nn(attt_s[:, :rows], branch_b)
        da_s[:rows, :] = dot_nt(branch_b, wout_ref[...]).astype(BF16)
        if lanes > rows:
            da_s[rows:lanes, :] = jnp.zeros((lanes - rows, width), BF16)
        dat_s[:, :lanes] = da_s[:lanes, :].T

        totals = {}

        def grad_head(head, slot):
            start, mask = head_place(head)
            grad_att = jnp.where(mask, da_s[:lanes, part_lanes(0, start)], 0)
            value = proj_s[:rows, part_lanes(2, start)]
            grad_mixed = dot_nt(value, grad_att)
            gsum_ref[head] += grad_mixed
            product = grad_mixed * cont_s[head, :rows, :lanes]
            gm_refs[slot][:rows, :lanes] = product
            if not compact:
                totals[head] = jnp.sum(product, axis=0, keepdims=True) / gate_ref[head]

        def soft_back_head(head, slot):
            product = gm_refs[slot][:rows, :lanes]
            if compact:
                total = jnp.sum(product, axis=0, keepdims=True) / gate_ref[head]
            else:
                total = totals[head]
            racc_s[SIDES.index(side), head, :, :lanes] += total
            content = cont_s[head, :rows, :lanes]
            gc_refs[slot][:rows, :lanes] = (product - content * total).astype(BF16)

        def back_head(head, slot):
            here = head_rows(0, head)
            mixed = mix_s[head, :rows, :lanes]
            grad_content = gc_refs[slot][:rows, :lanes]
            gt_s[head_rows(2, head), :rows] = dot_nt(dat_s[here, :lanes], mixed).astype(BF16)
            gt_s[head_rows(1, head), :rows] = (
                dot_nt(projt_s[0, here, :lanes], grad_content) * score_scale
            ).astype(BF16)
            gt_s[here, :lanes] = (
                dot_nn(projt_s[1, here, :rows], grad_content) * score_scale
            ).astype(BF16)

        skewed(compact, grad_head, soft_back_head, back_head)

        first_t = first_b.T
        grad_proj = gt_s[:, :lanes].T[:rows]
        gqkv_ref[:, : 3 * columns] += dot_nn(first_t, grad_proj)
        grad_first = dot_nt(grad_proj, wback_ref[...])
        vec_s[0] += fold_rows(grad_first * unit_one)
        vec_s[2] += fold_rows(grad_first)
        input_grad = grad_hidden + norm_back(grad_first, unit_one, inverse_one, gains_ref[0:1, :])
        spread(1, input_grad)

    for index, side in enumerate(SIDES):

        @pl.when(sizes_ref[step] == side)
        def _(index=index, side=side):
            image(
                side,
                sel_refs[index],
                selt_refs[index],
                rest_refs[index],
                restt_refs[index],
                place_refs[index],
                gsum_refs[index],
            )

    @pl.when(step == steps - 1)
    def _():
        def emit(index, carry):
            at = pl.ds(pl.multiple_of(index * SUB, SUB), SUB)
            place = index * across
            for ref in table:
                for col in range(ref.shape[1] // LANE):
                    tiles_ref[place] = ref[at, col * LANE : (col + 1) * LANE].astype(BF16)
                    place = place + 1
            return carry

        lax.fori_loop(0, row_tiles, emit, 0)
        for spare in range(row_tiles * across, tiles_ref.shape[0]):
            tiles_ref[spare] = jnp.zeros((SUB, LANE), BF16)

        small_ref[...] = jnp.zeros_like(small_ref)
        for row in range(6):
            small_ref[row : row + 1, :columns] = jnp.sum(vec_s[row], axis=0, keepdims=True)
        fc1_row = jnp.sum(fc1g_s[...], axis=0, keepdims=True)
        parts = hidden_units // columns
        for part in range(parts):
            small_ref[6 + part : 7 + part, :columns] = fc1_row[
                :, part * columns : (part + 1) * columns
            ]

        tile_rows = lax.broadcasted_iota(jnp.int32, (8, LANE), 0)
        tile_lanes = lax.broadcasted_iota(jnp.int32, (8, LANE), 1)
        grids = []
        for side in SIDES:
            rows, lanes = side_sizes(side)[1:]
            middle = 0.5 * (side - 1)
            key_ids = lax.broadcasted_iota(jnp.int32, (rows, LANE), 0).astype(F32)
            key_row = jnp.floor((key_ids + 0.5) * (1.0 / side))
            key_x, key_y = key_ids - side * key_row - middle, key_row - middle
            query_ids = lax.broadcasted_iota(jnp.int32, (1, lanes), 1).astype(F32)
            query_row = jnp.floor((query_ids + 0.5) * (1.0 / side))
            query_x, query_y = query_ids - side * query_row - middle, query_row - middle
            grids.append((key_x, key_y, key_x * key_x + key_y * key_y, query_x, query_y))

        def head_sums(index, head, carry):
            pieces = [jnp.zeros((1, LANE), F32) for _ in range(4)]
            gate_open = 1.0 - gate_ref[head]
            lanes = side_sizes(SIDES[index])[2]
            key_x, key_y, radius, query_x, query_y = grids[index]

            def total(values):
                return jnp.sum(values, axis=0, keepdims=True)

            for strip in range(lanes // LANE):
                at = slice(strip * LANE, (strip + 1) * LANE)
                weighted = gsum_refs[index][head, :, at] * place_refs[index][head, :, at]
                base = total(weighted)
                scaled = base / gate_open
                mean_x, mean_y, mean_r = (
                    moment_refs[index][head, row : row + 1, at] for row in range(3)
                )
                part_x = total(weighted * key_x) - mean_x * scaled
                part_y = total(weighted * key_y) - mean_y * scaled
                part_r = total(weighted * radius) - mean_r * scaled
                part_r -= 2.0 * (query_x[:, at] * part_x + query_y[:, at] * part_y)
                for row, part in enumerate((part_x, part_y, part_r, gate_ref[head] * base)):
                    pieces[row] += part
            pieces = [jnp.sum(piece, axis=1, keepdims=True) for piece in pieces]
            rests = jnp.sum(racc_s[index, head], axis=1, keepdims=True)
            pieces[3] -= gate_open * gate_ref[head] * rests
            for row in range(4):
                carry = carry + jnp.where(
                    (tile_rows == row) & (tile_lanes == head), pieces[row], 0.0
                )
            return carry

        first_row = 6 + parts
        for index, side in enumerate(SIDES):
            present = sizes_ref[0] == side
            for place in range(1, image_count):
                present = present | (sizes_ref[place] == side)
            @pl.when(present)
            def _(index=index):
                head_tile = lax.fori_loop(
                    0,
                    heads,
                    functools.partial(head_sums, index),
                    jnp.zeros((8, LANE), F32),
                )
                small_ref[first_row : first_row + 4, :LANE] += head_tile[:4]

        if started:
            small_ref[...] += small_in[...]


def matrices_columns(shared):
    return shared[3][0].shape[0]


def run_images(xct, sizes, start, band, shared, previous, units, tile_count):
    bands = len(xct)
    _, images, stored, main = xct[0].shape
    columns = matrices_columns(shared)
    places, moments, gate_open, matrices, gains, biases, fc1b = shared
    heads = gate_open.shape[0]
    width = matrices[0].shape[1] // 3
    padded = matrices[3].shape[1]
    chosen = [select_matrices(side, bands) for side in SIDES]
    sels = [jnp.asarray(made, BF16) for made in chosen]
    selts = [jnp.asarray(made.transpose(0, 2, 1), BF16) for made in chosen]
    chosen = [rest_matrices(side, bands) for side in SIDES]
    rests = [jnp.asarray(made, BF16) for made in chosen]
    restts = [jnp.asarray(made.transpose(0, 1, 3, 2), BF16) for made in chosen]
    sizes_all = [side_sizes(side) for side in SIDES]
    most_rows = max(size[1] for size in sizes_all)
    most_lanes = max(size[2] for size in sizes_all)
    started = previous is not None

    def whole(array):
        rank = len(array.shape)
        return pl.BlockSpec(
            array.shape, lambda i, *_: (0,) * rank, pipeline_mode=pl.Buffered(1)
        )

    def own(array):
        return pl.BlockSpec(
            (1,) + array.shape[1:],
            lambda i, sizes, band, *_: (band[0],) + (0,) * (array.ndim - 1),
            pipeline_mode=pl.Buffered(1),
        )

    image_specs = [pl.BlockSpec((2, 1, stored, main), lambda i, *_: (0, i, 0, 0))] * bands
    out_shapes = [
        [jax.ShapeDtypeStruct(part.shape, BF16) for part in xct],
        jax.ShapeDtypeStruct((tile_count, SUB, LANE), BF16),
        jax.ShapeDtypeStruct((SMALL_ROWS, width), F32),
    ]
    if not started:
        previous = (matrices[0], gains)
    scratch = [
        pltpu.VMEM((most_lanes, 3 * width), BF16),
        pltpu.VMEM((3, width, most_lanes), BF16),
        pltpu.VMEM((most_lanes, width), BF16),
        pltpu.VMEM((width, most_lanes), BF16),
        pltpu.VMEM((heads, most_rows, most_lanes), F32),
        pltpu.VMEM((heads, most_rows, most_lanes), BF16),
        pltpu.VMEM((columns, most_lanes), BF16),
        pltpu.VMEM((3 * columns, most_lanes), BF16),
        pltpu.VMEM((most_rows, padded), BF16),
        pltpu.VMEM((most_rows, padded), BF16),
        pltpu.VMEM((6, 8, columns), F32),
        pltpu.VMEM((8, padded), F32),
        pltpu.VMEM((len(SIDES), heads, 1, most_lanes), F32),
        pltpu.VMEM((columns, round_up(3 * columns, LANE)), F32),
        pltpu.VMEM((columns, width), F32),
        pltpu.VMEM((columns, padded), F32),
        pltpu.VMEM((columns, padded), F32),
        [pltpu.VMEM((heads, size[1], size[2]), F32) for size in sizes_all],
        [pltpu.VMEM((most_rows, most_lanes), F32)] * 2,
        [pltpu.VMEM((most_rows, most_lanes), BF16)] * 2,
        pltpu.VMEM((most_rows, columns), BF16),
        pltpu.VMEM((most_rows, columns), BF16),
        pltpu.VMEM((columns, most_lanes), BF16),
        pltpu.VMEM((columns, most_lanes), BF16),
        [pltpu.VMEM(place.shape, F32) for place in places],
        [pltpu.VMEM(matrix.shape, BF16) for matrix in matrices],
        pltpu.SemaphoreType.DMA((1 + len(places) + len(matrices),)),
    ]
    smalls = [sels, selts, rests, restts, list(places), list(moments), list(matrices), gains, biases, fc1b]
    body = functools.partial(image_kernel, columns, heads, units, images, started)
    hbm = lambda _: pl.BlockSpec(memory_space=pl.ANY)
    specs = [
        hbm(None),
        whole(previous[1]),
        jax.tree.map(own, sels),
        jax.tree.map(own, selts),
        jax.tree.map(own, rests),
        jax.tree.map(own, restts),
        [hbm(None) for _ in places],
        jax.tree.map(whole, list(moments)),
        [hbm(None) for _ in matrices],
        whole(gains),
        whole(biases),
        whole(fc1b),
    ]
    return pl.pallas_call(
        body,
        grid_spec=pltpu.PrefetchScalarGridSpec(
            num_scalar_prefetch=3,
            grid=(images,),
            in_specs=[image_specs] + specs,
            out_specs=[image_specs] + [whole(shape) for shape in out_shapes[1:]],
            scratch_shapes=scratch,
        ),
        out_shape=out_shapes,
        compiler_params=pltpu.CompilerParams(vmem_limit_bytes=VMEM_LIMIT),
        cost_estimate=pl.CostEstimate(
            flops=images * 8_000_000_000, bytes_accessed=40_000_000, transcendentals=0
        ),
    )(lax.slice_in_dim(sizes, start, start + images), band, gate_open, list(xct), *previous, *smalls)


def lane_tiles(columns):
    return [
        (index, low, min(low + LANE, columns))
        for index, low in enumerate(range(0, columns, LANE))
    ]


def loop_rows(rows, count, body, after=None):
    def step(index, carry):
        for row in range(8):
            start = pl.multiple_of(index * (8 * (count + 1)), 8) + row * (count + 1)
            body(index * 8 + row, pl.ds(start, count))
        if after is not None:
            after(pl.ds(index * 8, 8))
        return carry

    lax.fori_loop(0, rows // 8, step, 0)
    for row in range(rows // 8 * 8, rows):
        body(row, pl.ds(row * (count + 1), count))
    if after is not None and rows % 8:
        after(pl.ds(rows // 8 * 8, rows % 8))


def pack_kernel(first, order_ref, class_ref, band_ref, x_ref, ct_ref, table_ref, *refs):
    outs, wides, held, copy_sem = refs[:-4], refs[-4:-2], refs[-2], refs[-1]
    rows, count, columns = x_ref.shape
    images = count // len(outs)
    loads = [
        pltpu.make_async_copy(source, held.at[index], copy_sem.at[index])
        for index, source in enumerate((x_ref, ct_ref))
    ]
    for load in loads:
        load.start()

    for load, index, wide in zip(loads, range(2), wides):
        load.wait()

        def widen(row, at, index=index, wide=wide):
            for tile, low, high in lane_tiles(columns):
                wide[tile, at, : high - low] = held[index, row, :, low:high].astype(F32)

        loop_rows(rows, count, widen)

    for step, out in enumerate(outs):

        def one(index, carry, out=out, step=step):
            place = (band_ref[0] ^ step) * images + first + index
            at = pl.ds(order_ref[place], rows, stride=count + 1)
            select = table_ref[class_ref[place]]
            piece = table_ref.shape[1]
            low_lanes = lax.broadcasted_iota(jnp.int32, (piece // 2, LANE), 1) < LANE // 2
            for which, wide in enumerate(wides):
                for tile, low, high in lane_tiles(columns):
                    taken = dot_nn(select, wide[tile, at, :].astype(BF16))
                    if high - low == LANE:
                        out[which, index, :piece, low:high] = taken.astype(BF16)
                    else:
                        upper = pltpu.roll(taken[piece // 2 :], LANE // 2, 1)
                        block = jnp.where(low_lanes, taken[: piece // 2], upper)
                        fold(out, which, index, piece, block.astype(BF16))
            return carry

        lax.fori_loop(0, out.shape[1], one, 0, unroll=2)


def pack_images(x, ct, order, classes, band, bands, first, size):
    rows, count, columns = x.shape
    piece = piece_rows(bands)
    table = jnp.asarray(pack_matrix(bands), BF16)
    vmem = pl.BlockSpec(memory_space=pltpu.VMEM)
    return pl.pallas_call(
        functools.partial(pack_kernel, first),
        grid_spec=pltpu.PrefetchScalarGridSpec(
            num_scalar_prefetch=3,
            grid=(),
            in_specs=[pl.BlockSpec(memory_space=pl.ANY)] * 2 + [vmem],
            out_specs=[vmem] * bands,
            scratch_shapes=[
                pltpu.VMEM(
                    (round_up(columns, LANE) // LANE, round_up(rows, 8) * (count + 1), LANE), F32
                )
            ]
            * 2
            + [pltpu.VMEM((2, rows, count, columns), BF16), pltpu.SemaphoreType.DMA((2,))],
        ),
        out_shape=[jax.ShapeDtypeStruct((2, size) + stored_shape(piece, columns), BF16)] * bands,
        compiler_params=pltpu.CompilerParams(vmem_limit_bytes=VMEM_LIMIT),
        cost_estimate=pl.CostEstimate(flops=10_000_000, bytes_accessed=10_000_000, transcendentals=0),
    )(order, classes, band, x, ct, table)


def unpack_kernel(
    chunks, bands, order_ref, class_ref, band_ref, table_ref, low_ref, high_ref, *refs
):
    flat = bands * len(chunks)
    sources, (targets, wides, held) = refs[:flat], (refs[i : i + 2] for i in range(flat, flat + 6, 2))
    parts, (copy_sem, load_sem) = refs[flat + 6 : -2], refs[-2:]
    loads = [
        pltpu.make_async_copy(source, part, load_sem.at[index])
        for index, (source, part) in enumerate(zip(sources, parts))
    ]
    for load in loads:
        load.start()
    images = sum(chunks)
    rows, count, columns = targets[0].shape
    piece = table_ref.shape[2]
    first = 0
    for chunk, size in enumerate(chunks):
        for step in range(bands):
            part = parts[chunk * bands + step]
            loads[chunk * bands + step].wait()

            def one(index, carry, part=part, first=first, step=step):
                place = (band_ref[0] ^ step) * images + first + index
                at = pl.ds(order_ref[place], rows, stride=count + 1)
                kind = class_ref[place]
                for which, wide in enumerate(wides):
                    for tile, low, high in lane_tiles(columns):
                        if high - low == LANE:
                            made = dot_nn(table_ref[kind], part[which, index, :piece, low:high])
                        else:
                            rest = folded(part, which, index, piece)
                            made = dot_nn(low_ref[kind], rest)
                            made += pltpu.roll(dot_nn(high_ref[kind], rest), LANE // 2, 1)
                        wide[tile, at, :] = made
                return carry

            lax.fori_loop(0, size, one, 0, unroll=2)
        first += size

    for index, wide in enumerate(wides):

        def narrow(row, at, index=index, wide=wide):
            for tile, low, high in lane_tiles(columns):
                values = wide[tile, at, : high - low]
                held[index][row, :, low:high] = values.astype(held[index].dtype)

        def leave(at, index=index):
            pltpu.make_async_copy(
                held[index].at[at], targets[index].at[at], copy_sem.at[index]
            ).start()

        loop_rows(rows, count, narrow, leave)
    for index in range(2):
        pltpu.make_async_copy(held[index], targets[index], copy_sem.at[index]).wait()


def unpack_images(parts, order, classes, band, chunks, rows, columns):
    bands = len(parts[0])
    count = bands * sum(chunks)
    made = pack_matrix(bands).transpose(0, 2, 1)
    half = made.shape[2] // 2
    tables = [jnp.asarray(t, BF16) for t in (made, made[..., :half], made[..., half:])]
    vmem = pl.BlockSpec(memory_space=pltpu.VMEM)
    flat = [piece for part in parts for piece in part]
    shape = (rows, count, columns)
    wide = (round_up(columns, LANE) // LANE, round_up(rows, 8) * (count + 1), LANE)
    return pl.pallas_call(
        functools.partial(unpack_kernel, chunks, bands),
        grid_spec=pltpu.PrefetchScalarGridSpec(
            num_scalar_prefetch=3,
            grid=(),
            in_specs=[vmem] * 3 + [pl.BlockSpec(memory_space=pl.ANY)] * len(flat),
            out_specs=[pl.BlockSpec(memory_space=pl.ANY)] * 2,
            scratch_shapes=[
                pltpu.VMEM(wide, F32),
                pltpu.VMEM(wide, F32),
                pltpu.VMEM(shape, BF16),
                pltpu.VMEM(shape, F32),
                *[pltpu.VMEM(piece.shape, BF16) for piece in flat],
                pltpu.SemaphoreType.DMA((2,)),
                pltpu.SemaphoreType.DMA((len(flat),)),
            ],
        ),
        out_shape=[jax.ShapeDtypeStruct(shape, BF16), jax.ShapeDtypeStruct(shape, F32)],
        compiler_params=pltpu.CompilerParams(vmem_limit_bytes=VMEM_LIMIT),
        cost_estimate=pl.CostEstimate(flops=10_000_000, bytes_accessed=16_000_000, transcendentals=0),
    )(order, classes, band, *tables, *flat)


def prep_kernel(head_ref, gate_ref, wqkv_in, wout_in, w1_in, w2t_in, *refs):
    wqkv, wback, wout, w1, w2t = refs[:5]
    places, moments = refs[5:8], refs[8:11]
    columns = wout_in.shape[0]
    width = wout.shape[0]
    heads = head_ref.shape[1]
    wback[...] = wqkv_in[...].astype(BF16)
    for part in range(3):
        low = part * width
        wqkv[:, low : low + columns] = wqkv_in[:, part * columns : (part + 1) * columns].astype(BF16)
        wqkv[:, low + columns : low + width] = jnp.zeros((columns, width - columns), BF16)
    wout[:columns, :] = wout_in[...].astype(BF16)
    wout[columns:, :] = jnp.zeros((width - columns, columns), BF16)
    for out, source in ((w1, w1_in), (w2t, w2t_in)):
        units = source.shape[1]
        out[:, :units] = source[...].astype(BF16)
        out[:, units:] = jnp.zeros((columns, out.shape[1] - units), BF16)

    for side, place, moment in zip(SIDES, places, moments):
        live, rows, lanes = side_sizes(side)

        def spots(axis, rows=rows, lanes=lanes, side=side):
            ids = lax.broadcasted_iota(jnp.int32, (rows, lanes), axis)
            spot = ids.astype(F32)
            row = jnp.floor((spot + 0.5) * (1.0 / side))
            return ids, spot - side * row, row

        key_ids, key_x, key_y = spots(0)
        query_ids, query_x, query_y = spots(1)
        delta_x, delta_y = key_x - query_x, key_y - query_y
        distance = delta_x * delta_x + delta_y * delta_y
        dead_key = key_ids >= live
        inside = (key_ids < live) & (query_ids < live)
        middle = 0.5 * (side - 1)
        from_x, from_y = key_x - middle, key_y - middle

        def one(head, carry, place=place, moment=moment, from_x=from_x, from_y=from_y):
            scores = head_ref[0, head] * delta_x + head_ref[1, head] * delta_y
            scores = jnp.where(dead_key, MASKED, scores + head_ref[2, head] * distance)
            top = jnp.max(scores, axis=0, keepdims=True)
            raised = jnp.exp(scores - top)
            total = jnp.sum(raised, axis=0, keepdims=True)
            made = jnp.where(inside, raised * (gate_ref[head] / total), 0.0)
            place[head] = made
            for row, factor in enumerate((from_x, from_y, from_x * from_x + from_y * from_y)):
                moment[head, row : row + 1, :] = jnp.sum(made * factor, axis=0, keepdims=True)
            return carry

        lax.fori_loop(0, heads, one, 0)


def prepare(w_qkv, w_out, w_fc1, w_fc2t, head_params, gate_value):
    columns, heads = w_out.shape[0], head_params.shape[1]
    width = round_up(columns, LANE)
    padded = round_up(w_fc1.shape[1], 256)
    vmem = pl.BlockSpec(memory_space=pltpu.VMEM)
    smem = pl.BlockSpec(memory_space=pltpu.SMEM)
    shapes = [
        (columns, 3 * width),
        (columns, 3 * columns),
        (width, columns),
        (columns, padded),
        (columns, padded),
    ]
    outs = [jax.ShapeDtypeStruct(shape, BF16) for shape in shapes]
    outs += [jax.ShapeDtypeStruct((heads,) + side_sizes(side)[1:], F32) for side in SIDES]
    outs += [jax.ShapeDtypeStruct((heads, 8, side_sizes(side)[2]), F32) for side in SIDES]
    made = pl.pallas_call(
        prep_kernel,
        out_shape=outs,
        in_specs=[smem, smem] + [vmem] * 4,
        out_specs=[vmem] * len(outs),
        compiler_params=pltpu.CompilerParams(vmem_limit_bytes=VMEM_LIMIT),
        cost_estimate=pl.CostEstimate(
            flops=50_000_000, bytes_accessed=22_000_000, transcendentals=2_000_000
        ),
    )(head_params, gate_value, w_qkv, w_out, w_fc1, w_fc2t)
    return made[:5], made[5:8], made[8:]


def reduce_plan(tile_total, devices):
    each = -(-tile_total // devices)
    weight = sum(wave[1] for wave in WAVES)
    waves = []
    base = before = taken = 0
    for order, part in WAVES:
        before += part
        share = -(-each * before // weight) - taken
        if share:
            waves.append((base, share, order))
            base += devices * share
            taken += share
    return waves, each * devices


def reduce_kernel(
    waves,
    rank_z,
    own_ref,
    small_ref,
    full_out,
    small_out,
    own,
    full,
    recv0,
    recv1,
    small_own,
    small_recv,
    send_sem,
    recv_sem,
    small_send,
    small_got,
    copy_sem,
):
    img = lax.axis_index("img")
    band = lax.axis_index("band")
    z, y = img // 2, img % 2
    x, c = band // 2, band % 2
    low_z, high_z = z % 2, z // 2
    high_count = rank_z // 2
    mesh_ids = pl.DeviceIdType.MESH
    axes = {
        "c": (c, 2, lambda k: (img, x * 2 + 1 - c)),
        "y": (y, 2, lambda k: (z * 2 + 1 - y, band)),
        "x": (x, 2, lambda k: (img, (1 - x) * 2 + c)),
        "l": (low_z, 2, lambda k: ((high_z * 2 + 1 - low_z) * 2 + y, band)),
        "h": (
            high_z,
            high_count,
            lambda k: ((lax.rem(high_z + k, high_count) * 2 + low_z) * 2 + y, band),
        ),
    }
    order = [name for name in "cyxlh" if axes[name][1] > 1]
    partners = [axes[name][2](k) for name in order for k in range(1, axes[name][1])]
    devices = 1
    for name in order:
        devices *= axes[name][1]

    loads = []
    for w, (base, share, _) in enumerate(waves):
        at = pl.ds(base, devices * share)
        loads.append(pltpu.make_async_copy(own_ref.at[at], own.at[at], copy_sem.at[w]))
        loads[-1].start()
    small_own[...] = small_ref[...]

    barrier = pltpu.get_barrier_semaphore()
    for partner in partners:
        pl.semaphore_signal(barrier, inc=1, device_id=partner, device_id_type=mesh_ids)
    pl.semaphore_wait(barrier, len(partners))

    counters = [0] * len(waves)

    def send(wave, src, dst, target):
        slot = counters[wave]
        counters[wave] += 1
        copy = pltpu.make_async_remote_copy(
            src_ref=src,
            dst_ref=dst,
            send_sem=send_sem.at[wave, slot],
            recv_sem=recv_sem.at[wave, slot],
            device_id=target,
            device_id_type=mesh_ids,
        )
        copy.start()
        return copy

    def add_tiles(dst, dst_at, parts, count, out, out_at):
        block = 8

        def one(offset, size):
            total = dst[pl.ds(dst_at + offset, size)].astype(F32)
            for ref, at in parts:
                total += ref[pl.ds(at + offset, size)].astype(F32)
            out[pl.ds(out_at + offset, size)] = total.astype(BF16)

        if count >= block:

            def step(index, carry):
                one(index * block, block)
                return carry

            lax.fori_loop(0, count // block, step, 0)
        rest = count % block
        if rest:
            one(count - rest, rest)

    stores = []

    def wave_stages(w):
        base, share, axis_order = waves[w]
        order = [name for name in axis_order if axes[name][1] > 1]
        state = {"at": base, "size": devices * share, "copies": [], "parts": []}
        taken = [base // 2]

        def finish():
            for copy in state["copies"]:
                copy.wait()

        def scatter(name):
            def run():
                if state["parts"]:
                    finish()
                    add_tiles(own, state["at"], state["parts"], state["size"], own, state["at"])
                else:
                    loads[w].wait()
                mine, count, target = axes[name]
                size = state["size"] // count
                state["copies"], state["parts"] = [], []
                for k in range(1, count):
                    other = lax.rem(mine + k, count)
                    if name == order[0]:
                        buffer, at = recv0, base // 2
                    else:
                        buffer, at = recv1, taken[0]
                        taken[0] += size
                    state["copies"].append(
                        send(
                            w,
                            own.at[pl.ds(state["at"] + other * size, size)],
                            buffer.at[pl.ds(at, size)],
                            target(k),
                        )
                    )
                    state["parts"].append((buffer, at))
                state["at"] = state["at"] + mine * size
                state["size"] = size

            return run

        def gather(name, first):
            def run():
                finish()
                if first:
                    at = state["at"]
                    add_tiles(own, at, state["parts"], state["size"], full, at)
                mine, count, target = axes[name]
                piece = full.at[pl.ds(state["at"], state["size"])]
                state["copies"] = [send(w, piece, piece, target(k)) for k in range(1, count)]
                state["at"] = state["at"] - mine * state["size"]
                state["size"] = state["size"] * count

            return run

        def close():
            finish()
            at = pl.ds(base, devices * share)
            stores.append(
                pltpu.make_async_copy(full.at[at], full_out.at[at], copy_sem.at[len(waves) + w])
            )
            stores[-1].start()

        steps = [scatter(name) for name in order]
        steps += [gather(name, name == order[-1]) for name in reversed(order)]
        return steps + [close]

    small_slots = [0]
    small_state = {}

    def small_start(name):
        mine, count, target = axes[name]
        first = small_slots[0]
        small_slots[0] += count - 1
        small_state["copies"] = []
        for k in range(1, count):
            slot = first + k - 1
            copy = pltpu.make_async_remote_copy(
                src_ref=small_own,
                dst_ref=small_recv.at[slot],
                send_sem=small_send.at[slot],
                recv_sem=small_got.at[slot],
                device_id=target(k),
                device_id_type=mesh_ids,
            )
            copy.start()
            small_state["copies"].append(copy)
        small_state["first"] = first

    def small_end(name):
        mine, count, _ = axes[name]
        first = small_state["first"]
        for copy in small_state["copies"]:
            copy.wait()
        if count == 2:
            small_own[...] = small_own[...] + small_recv[first]
        else:
            last = small_recv.shape[0] - 1
            small_recv[last] = small_own[...]

            def add_line(index, total):
                k = lax.rem(mine - index + count, count)
                slot = jnp.where(k == 0, last, first + k - 1)
                return total + small_recv[slot]

            small_own[...] = lax.fori_loop(0, count, add_line, jnp.zeros_like(small_own))

    programs = [wave_stages(w) for w in range(len(waves))]
    depth = len(programs[0])
    for program in programs:
        program[0]()
    for time in range(1, max(depth, len(order) + 2)):
        if time < depth:
            for program in programs:
                program[time]()
        if 1 <= time <= len(order) + 1:
            if time > 1:
                small_end(order[time - 2])
            if time <= len(order):
                small_start(order[time - 1])
    small_out[...] = small_own[...]
    for store in stores:
        store.wait()


def reduce_all(tiles, small, waves, img_count):
    total = tiles.shape[0]
    rank_z = img_count // 2
    copies = 2 * (4 + max(rank_z // 2 - 1, 0))
    hops = 4 + max(rank_z // 2 - 1, 0)
    return pl.pallas_call(
        functools.partial(reduce_kernel, waves, rank_z),
        out_shape=[
            jax.ShapeDtypeStruct(tiles.shape, BF16),
            jax.ShapeDtypeStruct(small.shape, F32),
        ],
        in_specs=[pl.BlockSpec(memory_space=pl.ANY), pl.BlockSpec(memory_space=pltpu.VMEM)],
        out_specs=[pl.BlockSpec(memory_space=pl.ANY), pl.BlockSpec(memory_space=pltpu.VMEM)],
        scratch_shapes=[
            pltpu.VMEM(tiles.shape, BF16),
            pltpu.VMEM(tiles.shape, BF16),
            pltpu.VMEM((total // 2, SUB, LANE), BF16),
            pltpu.VMEM((total // 2, SUB, LANE), BF16),
            pltpu.VMEM(small.shape, F32),
            pltpu.VMEM((hops + 1,) + small.shape, F32),
            pltpu.SemaphoreType.DMA((len(waves), copies)),
            pltpu.SemaphoreType.DMA((len(waves), copies)),
            pltpu.SemaphoreType.DMA((hops,)),
            pltpu.SemaphoreType.DMA((hops,)),
            pltpu.SemaphoreType.DMA((2 * len(waves),)),
        ],
        compiler_params=pltpu.CompilerParams(
            collective_id=1, has_side_effects=True, vmem_limit_bytes=VMEM_LIMIT
        ),
        cost_estimate=pl.CostEstimate(
            flops=10_000_000, bytes_accessed=200_000_000, transcendentals=0
        ),
    )(tiles, small)


def update_kernel(
    decay_rate,
    head_count,
    widths,
    tiles_ref,
    small_ref,
    weight_hbm,
    line_refs,
    vector_refs,
    moment_refs,
    norm_out,
    grad_hbm,
    new_hbm,
    vgrad_outs,
    vnew_outs,
    line_outs,
    moment_outs,
    weights,
    grads,
    news,
    row_s,
    col_s,
    copy_sem,
):
    columns = weights[0].shape[0]
    row_tiles = columns // SUB
    spans = [-(-wide // LANE) for wide in widths]
    total_span = tiles_stride(widths)
    starts = []
    at = 0
    for wide in widths:
        starts.append(at)
        at += tile_span(wide)
    loads = [
        pltpu.make_async_copy(weight_hbm[i], weights[i], copy_sem.at[i]) for i in range(4)
    ]
    for load in loads:
        load.start()

    def tile_rows(index, which):
        place = index * total_span + starts[which]
        pieces = [tiles_ref[place + col].astype(F32) for col in range(spans[which])]
        whole = jnp.concatenate(pieces, axis=1) if len(pieces) > 1 else pieces[0]
        return whole[:, : widths[which]]

    def all_sum(values):
        return jnp.sum(jnp.sum(values, axis=0, keepdims=True), axis=1, keepdims=True)

    def measure(index, carry):
        at = pl.ds(pl.multiple_of(index * SUB, SUB), SUB)
        made = []
        for which in range(4):
            grad = tile_rows(index, which)
            square = grad * grad
            row_s[which, at, :] = jnp.sum(square, axis=1, keepdims=True)
            made.append(carry[which] + fold_rows(square))
        return tuple(made)

    zeros = tuple(jnp.zeros((8, wide), F32) for wide in widths)
    folded = lax.fori_loop(0, row_tiles, measure, zeros)
    col_squares = [jnp.sum(fold, axis=0, keepdims=True) for fold in folded]
    total = jnp.zeros((1, 1), F32)
    for square in col_squares:
        total += jnp.sum(square, axis=1, keepdims=True)

    parts = vector_refs[2].shape[0]
    places = (
        (slice(0, 2), columns),
        (slice(2, 6), columns),
        (slice(6, 6 + parts), columns),
        (slice(6 + parts, 10 + parts), head_count),
    )
    vectors = [small_ref[rows, :wide] for rows, wide in places]
    for grad in vectors:
        total += all_sum(grad * grad)
    norm = jnp.sqrt(total)
    norm_out[...] = norm
    factor = 1.0 / jnp.maximum(norm, 1.0)

    for index in range(4):
        grad = vectors[index] * factor
        weight = vector_refs[index][...]
        moment = decay_rate * moment_refs[index][...] + (1.0 - decay_rate) * (
            grad * grad + FLOOR_ONE
        )
        update = grad * lax.rsqrt(moment)
        size = weight.shape[0] * weight.shape[1]
        mean_square = all_sum(update * update) / size
        update = update / jnp.maximum(1.0, jnp.sqrt(mean_square) / CLIP_RMS)
        scale = STEP_RATE * jnp.maximum(FLOOR_TWO, jnp.sqrt(all_sum(weight * weight) / size))
        vgrad_outs[index][...] = grad
        vnew_outs[index][...] = weight - scale * update
        moment_outs[index][...] = moment

    row_factors, col_factors = [], []
    for which in range(4):
        wide = widths[which]
        down_old, along_old = line_refs[which]
        down_out, along_out = line_outs[which]
        down = jnp.broadcast_to(down_old[...].reshape(1, columns), (LANE, columns)).T
        down = decay_rate * down + (1.0 - decay_rate) * (
            row_s[which] * (factor * factor) / wide + FLOOR_ONE
        )
        along = decay_rate * along_old[...].reshape(1, wide) + (1.0 - decay_rate) * (
            col_squares[which] * (factor * factor) / columns + FLOOR_ONE
        )
        down_out[...] = down.T[:1, :].reshape(columns)
        along_out[...] = along.reshape(wide)
        down = down[:, :1]
        if which == 3:
            along = along / (jnp.sum(along, axis=1, keepdims=True) / wide)
        else:
            down = down / (jnp.sum(down, axis=0, keepdims=True) / columns)
        row_s[which] = lax.rsqrt(down) * factor
        col_s[which, :, :wide] = lax.rsqrt(along)

    for load in loads:
        load.wait()

    def scan(index, carry):
        at = pl.ds(pl.multiple_of(index * SUB, SUB), SUB)
        made = []
        for which in range(4):
            wide = widths[which]
            update = tile_rows(index, which) * col_s[which, :, :wide] * row_s[which, at, :]
            weight = weights[which][at, :]
            made.append(carry[2 * which] + fold_rows(update * update))
            made.append(carry[2 * which + 1] + fold_rows(weight * weight))
        return tuple(made)

    sums = lax.fori_loop(0, row_tiles, scan, tuple(z for z in zeros for _ in range(2)))
    stores = []
    for which in (2, 3, 0, 1):
        wide = widths[which]
        size = columns * wide
        scale = STEP_RATE * jnp.maximum(FLOOR_TWO, jnp.sqrt(all_sum(sums[2 * which + 1]) / size))
        scale = scale / jnp.maximum(1.0, jnp.sqrt(all_sum(sums[2 * which]) / size) / CLIP_RMS)
        col_factor = col_s[which, :, :wide] * scale

        def write(index, carry, which=which, col_factor=col_factor):
            at = pl.ds(pl.multiple_of(index * SUB, SUB), SUB)
            grad = tile_rows(index, which)
            grads[which][at, :] = grad * factor
            news[which][at, :] = weights[which][at, :] - grad * col_factor * row_s[which, at, :]
            return carry

        lax.fori_loop(0, row_tiles, write, 0)
        for source, target, slot in (
            (grads[which], grad_hbm[which], 4 + which),
            (news[which], new_hbm[which], 8 + which),
        ):
            stores.append(pltpu.make_async_copy(source, target, copy_sem.at[slot]))
            stores[-1].start()
    for store in stores:
        store.wait()


def tile_span(wide):
    return round_up(wide, 256 if wide > 1500 else LANE) // LANE


def tiles_stride(widths):
    return sum(tile_span(wide) for wide in widths)


def update_all(tiles, small, weights, rows, cols, vectors, moments, decay_rate):
    columns = weights[1].shape[0]
    head_count = vectors[3].shape[1]
    units = weights[2].shape[1]
    parts = units // columns
    lines = [[r, c] for r, c in zip(rows, cols)]
    lines[3] = lines[3][::-1]
    vectors = [v.reshape(parts, columns) if v.ndim == 1 else v for v in vectors]
    moments = [v.reshape(parts, columns) if v.ndim == 1 else v for v in moments]
    widths = [weight.shape[1] for weight in weights]
    like = lambda group: [jax.ShapeDtypeStruct(v.shape, F32) for v in group]
    outs = [
        jax.ShapeDtypeStruct((1, 1), F32),
        like(weights),
        like(weights),
        like(vectors),
        like(vectors),
        [like(pair) for pair in lines],
        like(vectors),
    ]
    vmem = pl.BlockSpec(memory_space=pltpu.VMEM)
    hbm = pl.BlockSpec(memory_space=pl.ANY)
    args = (tiles, small, list(weights), lines, vectors, moments)
    in_specs = list(jax.tree.map(lambda _: vmem, args))
    in_specs[2] = [hbm] * 4
    out_specs = jax.tree.map(lambda _: vmem, outs)
    out_specs[1] = [hbm] * 4
    out_specs[2] = [hbm] * 4
    full = lambda: [pltpu.VMEM(weight.shape, F32) for weight in weights]
    scratch = [
        full(),
        full(),
        full(),
        pltpu.VMEM((4, columns, 1), F32),
        pltpu.VMEM((4, 1, round_up(max(widths), LANE)), F32),
        pltpu.SemaphoreType.DMA((12,)),
    ]
    made = pl.pallas_call(
        functools.partial(update_kernel, decay_rate, head_count, widths),
        out_shape=outs,
        in_specs=in_specs,
        out_specs=out_specs,
        scratch_shapes=scratch,
        compiler_params=pltpu.CompilerParams(vmem_limit_bytes=VMEM_LIMIT),
    )(*args)
    norm, grads, news, vgrads, vnews, line_new, moment_new = made
    spread = lambda group: [v.reshape(-1) if i == 2 else v for i, v in enumerate(group)]
    line_new[3] = line_new[3][::-1]
    moved = [line for pair in line_new for line in pair]
    grads[3], news[3] = grads[3].T, news[3].T
    return (
        norm.reshape(1),
        *grads,
        *spread(vgrads),
        *news,
        *spread(vnews),
        *moved,
        *spread(moment_new),
    )


def deal_images(grid_sizes, devices):
    count = grid_sizes.shape[0]
    ids = jnp.arange(count, dtype=jnp.int32)
    ahead = (grid_sizes[None, :] > grid_sizes[:, None]) | (
        (grid_sizes[None, :] == grid_sizes[:, None]) & (ids[None, :] < ids[:, None])
    )
    rank = jnp.sum(ahead.astype(jnp.int32), axis=1)
    turn = rank // devices
    seat = rank % devices
    seat = jnp.where(turn % 2 == 0, seat, devices - 1 - seat)
    place = seat * (count // devices) + turn
    hit = place[None, :] == ids[:, None]
    order = jnp.sum(jnp.where(hit, ids[None, :], 0), axis=1)
    sizes = jnp.sum(jnp.where(hit, grid_sizes[None, :], 0), axis=1)
    return order, sizes


def per_device(
    inputs,
    cotangent,
    grid_sizes,
    w_qkv,
    w_out,
    w_fc1,
    w_fc2,
    norm_gains,
    biases,
    fc1_bias,
    head_params,
    rows_qkv,
    cols_qkv,
    rows_out,
    cols_out,
    rows_fc1,
    cols_fc1,
    rows_fc2,
    cols_fc2,
    gain_moment,
    bias_moment,
    fc1_bias_moment,
    head_moment,
):
    band_count = lax.axis_size("band")
    img_count = lax.axis_size("img")
    band_index = lax.axis_index("band")
    columns = inputs.shape[2]
    units = w_fc1.shape[1]
    per_band = inputs.shape[0] // band_count
    order, sizes_ordered = deal_images(grid_sizes, band_count)
    classes = sum(
        (jnp.where(sizes_ordered == side, index, 0) for index, side in enumerate(SIDES)),
        jnp.zeros_like(order),
    )
    sizes_used = lax.dynamic_slice_in_dim(sizes_ordered, band_index * per_band, per_band)
    early = max(1, per_band // 2)
    chunks = (early, per_band - early)
    band = band_index.astype(jnp.int32).reshape(1)
    x_stored, ct_stored = jnp.swapaxes(inputs, 0, 1), jnp.swapaxes(cotangent, 0, 1)
    pack = lambda first, size: pack_images(
        x_stored, ct_stored, order, classes, band, band_count, first, size
    )

    def exchange(parts):
        swaps = [[(i, i ^ step) for i in range(band_count)] for step in range(band_count)]
        return [parts[0]] + [
            lax.ppermute(parts[step], "band", swaps[step]) for step in range(1, band_count)
        ]

    waves, tile_count = reduce_plan(
        (columns // SUB) * tiles_stride((3 * columns, columns, units, units)),
        band_count * img_count,
    )
    w_fc2t = w_fc2.T
    gate_value = jax.nn.sigmoid(head_params[3])
    matrices, places, spots = prepare(w_qkv, w_out, w_fc1, w_fc2t, head_params, gate_value)
    first_part = pack(0, early)
    first_moved = exchange(first_part)
    later_part = pack(early, per_band - early)
    later_part, matrices, first_moved = lax.optimization_barrier(
        (later_part, matrices, first_moved)
    )
    moved = [first_moved, exchange(later_part)]
    fc1b = jnp.pad(fc1_bias[None, :], ((0, 0), (0, matrices[3].shape[1] - units)))
    shared = (places, spots, 1.0 - gate_value, matrices, norm_gains, biases, fc1b)
    previous = None
    start = 0
    results = []
    for part, size in zip(moved, chunks):
        result, *previous = run_images(
            part, sizes_used, start, band, shared, previous, units, tile_count
        )
        results.append(result)
        start += size
    tiles, small = previous
    results[0], tiles = lax.optimization_barrier((exchange(results[0]), tiles))
    full, small = reduce_all(tiles, small, waves, img_count)
    results[1], full = lax.optimization_barrier((results[1], full))
    results[1] = exchange(results[1])
    updated = update_all(
        full,
        small,
        (w_qkv, w_out, w_fc1, w_fc2t),
        (rows_qkv, rows_out, rows_fc1, rows_fc2),
        (cols_qkv, cols_out, cols_fc1, cols_fc2),
        (norm_gains, biases, fc1_bias, head_params),
        (gain_moment, bias_moment, fc1_bias_moment, head_moment),
        1.0 - STEP ** (-0.8),
    )
    output, input_grad = unpack_images(
        results, order, classes, band, chunks, inputs.shape[1], columns
    )
    return (jnp.swapaxes(output, 0, 1), jnp.swapaxes(input_grad, 0, 1), *updated)


def solution(mesh):
    split = P("img", "band", None)
    return jax.shard_map(
        per_device,
        mesh=mesh,
        in_specs=(split, split, P("img")) + (P(),) * 20,
        out_specs=(split, split) + (P(),) * 29,
        check_vma=False,
    )
```
